32 devices in a mesh: img: 8 (over y, x, core), head: 4 (over z).
Axes of the slice: x: 2, y: 2, z: 4, core: 2. Of those that a mesh axis runs over, the one named last changes fastest.
Arguments:
- tokens: bfloat16 [50176, 256], P(('img', 'head')), may hold values from -6 to 6
- image_sides: int32 [8, 32], P('img'), may hold values from 0 to 4, as said below
- qkv_weight: bfloat16 [3, 256, 256], P(None, None, 'head'), may hold values from -0.375 to 0.375
- proj_weight: bfloat16 [256, 256], P('head'), may hold values from -1.5 to 1.5
- proj_bias: float32 [256], replicated, may hold values from -3 to 3
- fc_in: bfloat16 [1024, 256], P(('img', 'head')), may hold values from -0.375 to 0.375
- fc_in_bias: float32 [1024], replicated, may hold values from -3 to 3
- fc_out: bfloat16 [1024, 256], P(('img', 'head')), may hold values from -0.375 to 0.375
- fc_out_bias: float32 [256], replicated, may hold values from -3 to 3
- norm_gains: float32 [2, 256], replicated, may hold values from 0.5 to 1.5
- norm_shifts: float32 [2, 256], replicated, may hold values from -2 to 2
- peg_weight: float32 [9, 256], replicated, may hold values from -2 to 2
- peg_bias: float32 [256], replicated, may hold values from -3 to 3
- out_grad: bfloat16 [50176, 256], P(('img', 'head')), may hold values from -6 to 6
Outputs:
- output: bfloat16 [50176, 256], P(('img', 'head'))
- d_tokens: float32 [50176, 256], P(('img', 'head'))
- d_qkv_weight: float32 [3, 256, 256], P(None, None, 'head')
- d_proj_weight: float32 [256, 256], P('head')
- d_proj_bias: float32 [256], replicated
- d_fc_in: float32 [1024, 256], P(('img', 'head'))
- d_fc_in_bias: float32 [1024], replicated
- d_fc_out: float32 [1024, 256], P(('img', 'head'))
- d_fc_out_bias: float32 [256], replicated
- d_norm_gains: float32 [2, 256], replicated
- d_norm_shifts: float32 [2, 256], replicated
- d_peg_weight: float32 [9, 256], replicated
- d_peg_bias: float32 [256], replicated
The draws below stay inside these ranges and needn't reach their ends.
Inputs may be any that keep to these rules, and one draw needn't show every extreme that they name: `image_sides`: each row lists one group's images in slot order, each of side 2, 3 or 4 windows; a 0 marks an unused slot and only follows used ones. The squared sides of a row add up to at most 128, and in some row to exactly 128.
All inputs are finite; a program needn't handle non-finite values.
Results may differ from the reference program's by a relative error of at most 0.017.
Values may be sent and summed in bfloat16 or wider, within the bound.
A program may use at most 192 MiB of HBM per device.

```python
import jax
import jax.numpy as jnp
from jax import lax

D = 256
HEADS = 8
HDIM = 32
FF = 1024
WS = 7
WIN_GRP = 128
SLOTS = 32
GROUPS = 8
TOKENS = 50176


def draw_image_sides(key, part):
    key = jax.random.fold_in(key, 7)
    pick_key = jax.random.fold_in(key, 1)
    budget_key = jax.random.fold_in(key, 2)
    full_key = jax.random.fold_in(key, 3)
    picked = jax.random.randint(pick_key, (GROUPS, SLOTS), 2, 5, dtype=jnp.int32)
    filled = jnp.cumsum(picked * picked, axis=1)
    budget = jax.random.randint(budget_key, (GROUPS, 1), 3 * WIN_GRP // 8, WIN_GRP + 1, dtype=jnp.int32)
    chosen = jnp.where(filled <= budget, picked, 0)
    full_row = jax.random.randint(full_key, (), 0, GROUPS, dtype=jnp.int32)
    slot_ids = jnp.arange(SLOTS, dtype=jnp.int32)
    whole_row = jnp.where(slot_ids < WIN_GRP // 16, 4, 0)
    rows_ids = jnp.arange(GROUPS, dtype=jnp.int32)
    return jnp.where((rows_ids == full_row)[:, None], whole_row[None, :], chosen).astype(jnp.int32)


def steps_of(key, dims, cuts, smallest, top_value):
    factor_of, own = 1.0, jax.random.fold_in(key, 6)
    for position, parts in cuts:
        heights = jnp.exp(jax.random.uniform(jax.random.fold_in(own, position), (parts,), jnp.float32, smallest / len(cuts), top_value / len(cuts)))
        factor_of = factor_of * jnp.repeat(heights, dims[position] // parts).reshape([-1 if axis == position else 1 for axis in range(len(dims))])
    return factor_of


def scatter_about(rng, dims, deviation, reach, split=(), held_as=jnp.bfloat16):
    values = jax.random.normal(rng, dims, jnp.float32) * deviation
    if len(split) > 0:
        values = steps_of(rng, dims, split, -0.22, 0.18) * values
    return jnp.clip(values, min=-reach, max=reach).astype(held_as)


def setup_inputs(seed: int = 0) -> dict:
    key_list = jax.random.split(jax.random.key(seed), 15)
    return {
        "tokens": scatter_about(key_list[0], (TOKENS, D), 1.0, 6.0, ((0, 32),)),
        "image_sides": draw_image_sides(jax.random.fold_in(key_list[14], 71), 0),
        "qkv_weight": scatter_about(key_list[2], (3, D, D), D ** -0.5, 0.375, ((2, 4),)),
        "proj_weight": scatter_about(key_list[3], (D, D), (D // 16) ** -0.5, 1.5, ((0, 4),)),
        "proj_bias": scatter_about(key_list[4], (D,), 0.5, 3.0, (), jnp.float32),
        "fc_in": scatter_about(key_list[5], (FF, D), D ** -0.5, 0.375, ((0, 32),)),
        "fc_in_bias": scatter_about(key_list[6], (FF,), 0.5, 3.0, (), jnp.float32),
        "fc_out": scatter_about(key_list[7], (FF, D), (FF // 4) ** -0.5, 0.375, ((0, 32),)),
        "fc_out_bias": scatter_about(key_list[8], (D,), 0.5, 3.0, (), jnp.float32),
        "norm_gains": jnp.clip(1.0 + 0.1 * jax.random.normal(key_list[9], (2, D), jnp.float32), 0.5, 1.5),
        "norm_shifts": scatter_about(key_list[10], (2, D), 0.3, 2.0, (), jnp.float32),
        "peg_weight": scatter_about(key_list[11], (9, D), 9 ** -0.5, 2.0, (), jnp.float32),
        "peg_bias": scatter_about(key_list[12], (D,), 0.5, 3.0, (), jnp.float32),
        "out_grad": scatter_about(key_list[13], (TOKENS, D), 1.0, 6.0, ((0, 32),)),
    }


@jax.custom_vjp
def low(v):
    return lax.optimization_barrier(v.astype(jnp.bfloat16)).astype(jnp.float32)

@jax.custom_vjp
def low_back(v):
    return v

def low_keep(v):
    return (low(v), None)

def low_pass(kept, grad):
    return (grad,)

def back_keep(v):
    return (v, None)

def back_low(kept, grad):
    return (low(grad),)
low.defvjp(low_keep, low_pass)
low_back.defvjp(back_keep, back_low)

def layout(side_table, windows):
    side_sizes = side_table.astype(jnp.int32)
    window_areas = side_sizes * side_sizes
    finish = jnp.cumsum(window_areas).astype(jnp.int32)
    starts = finish - window_areas
    window_ids = jnp.arange(windows, dtype=jnp.int32)
    holding = ((window_ids[:, None] >= starts[None, :]) & (window_ids[:, None] < finish[None, :])).astype(jnp.int32)
    image_side = lax.optimization_barrier(jnp.sum(holding * side_sizes[None, :], axis=1)).astype(jnp.int32)
    image_start = lax.optimization_barrier(jnp.sum(holding * starts[None, :], axis=1)).astype(jnp.int32)
    grid_size = jnp.where(image_side == 2, 14, jnp.where(image_side == 3, 18, jnp.where(image_side == 4, 24, 0))).astype(jnp.int32)
    place_id = window_ids - image_start
    across = jnp.maximum(image_side, 1)
    window_row = place_id // across
    window_col = place_id % across
    cell_ids = jnp.arange(WS * WS, dtype=jnp.int32)
    patch_row = window_row[:, None] * WS + cell_ids[None, :] // WS
    patch_col = window_col[:, None] * WS + cell_ids[None, :] % WS
    grid_limit = grid_size[:, None]
    valid_mask = (patch_row < grid_limit) & (patch_col < grid_limit)
    index_list = []
    inside_list = []
    for shift_row in (-1, 0, 1):
        for shift_col in (-1, 0, 1):
            near_row = patch_row + shift_row
            near_col = patch_col + shift_col
            in_grid = valid_mask & (near_row >= 0) & (near_row < grid_limit) & (near_col >= 0) & (near_col < grid_limit)
            target = (image_start[:, None] + near_row // WS * across[:, None] + near_col // WS) * (WS * WS) + near_row % WS * WS + near_col % WS
            index_list.append(jnp.where(in_grid, target, 0).reshape(-1).astype(jnp.int32))
            inside_list.append(in_grid.reshape(-1).astype(jnp.float32))
    return (valid_mask.reshape(-1).astype(jnp.float32), jnp.stack(index_list), jnp.stack(inside_list))

def normalize(values, gain_vec, shift_vec):
    centre = values - lax.optimization_barrier(jnp.mean(values, axis=-1, keepdims=True))
    scaled = centre * lax.rsqrt(lax.optimization_barrier(jnp.mean(centre * centre, axis=-1, keepdims=True)) + 1e-06)
    return scaled * gain_vec + shift_vec

def group_forward(inputs, side_table, qkv_weight, proj_weight, proj_bias, fc_in, fc_in_bias, fc_out, fc_out_bias, norm_gains, norm_shifts, peg_weight, peg_bias):
    row_count = inputs.shape[0]
    windows = row_count // (WS * WS)
    valid_mask, indices, inside = layout(side_table, windows)
    mixed_sum = inputs + peg_bias
    for tap_id in range(9):
        mixed_sum = mixed_sum + inside[tap_id][:, None] * peg_weight[tap_id] * inputs[indices[tap_id]]
    field = valid_mask[:, None] * mixed_sum
    normed = low(normalize(field, norm_gains[0], norm_shifts[0]))
    projected = jnp.einsum('rd,tdc->trc', normed, qkv_weight, precision=lax.Precision.HIGHEST)
    qkv_parts = low(low_back(projected)).reshape(3, windows, WS * WS, HEADS, HDIM)
    scores = jnp.einsum('wqhe,wkhe->whqk', qkv_parts[0], qkv_parts[1], precision=lax.Precision.HIGHEST) * HDIM ** (-0.5)
    key_bias = ((valid_mask - 1.0) * 1000000000.0).reshape(windows, 1, 1, WS * WS)
    scores = low_back(scores + key_bias)
    top_score = lax.optimization_barrier(jnp.max(scores, axis=-1, keepdims=True))
    exponent = jnp.exp(scores - top_score)
    prob_low = low(exponent / lax.optimization_barrier(jnp.sum(exponent, axis=-1, keepdims=True)))
    context = jnp.einsum('whqk,wkhe->wqhe', prob_low, qkv_parts[2], precision=lax.Precision.HIGHEST).reshape(row_count, HEADS * HDIM)
    context = low(low_back(context))
    branch = low_back(jnp.dot(context, proj_weight, precision=lax.Precision.HIGHEST) + proj_bias)
    hidden_in = field + branch
    normed_two = low(normalize(hidden_in, norm_gains[1], norm_shifts[1]))
    pre_act = low_back(jnp.einsum('rd,fd->rf', normed_two, fc_in, precision=lax.Precision.HIGHEST) + fc_in_bias)
    active = low(jax.nn.gelu(pre_act, approximate=False))
    result = jnp.dot(active, fc_out, precision=lax.Precision.HIGHEST) + fc_out_bias
    return valid_mask[:, None] * (hidden_in + result)

def reference(tokens, image_sides, qkv_weight, proj_weight, proj_bias, fc_in, fc_in_bias, fc_out, fc_out_bias, norm_gains, norm_shifts, peg_weight, peg_bias, out_grad):
    weights = (qkv_weight.astype(jnp.float32), proj_weight.astype(jnp.float32), proj_bias, fc_in.astype(jnp.float32), fc_in_bias, fc_out.astype(jnp.float32), fc_out_bias, norm_gains, norm_shifts, peg_weight, peg_bias)
    grouped = tokens.astype(jnp.float32).reshape(GROUPS, -1, D)
    cotangent = out_grad.astype(jnp.float32).reshape(GROUPS, -1, D)

    def forward(inputs, *params):

        def single(member):
            return group_forward(member[0], member[1], *params)
        return lax.map(jax.checkpoint(single), (inputs, image_sides))
    result, pullback = jax.vjp(forward, grouped, *weights)
    gradients = pullback(cotangent)
    return (result.reshape(-1, D).astype(jnp.bfloat16), gradients[0].reshape(-1, D), gradients[1], gradients[2], gradients[3], gradients[4], gradients[5], gradients[6], gradients[7], gradients[8], gradients[9], gradients[10], gradients[11])
```

```python
import functools

import jax
import jax.numpy as jnp
from jax import lax
from jax.experimental import pallas as pl
from jax.experimental.pallas import tpu as pltpu
from jax.sharding import PartitionSpec as P

F32 = jnp.float32
BF16 = jnp.bfloat16
MESH = pl.DeviceIdType.MESH

HDIM = 32
WS = 7
CELLS = WS * WS
SLOT = WS * 8
TALL = 64
MARGIN = 5
HALO = 256
EDGE = 6
OFFSET = 8
BLOCK = 4
SMALL = 32
VMEM_LIMIT = 56 * 1024 * 1024


def nn(left, right):
    return lax.dot_general(left, right, (((1,), (0,)), ((), ())), preferred_element_type=F32)


def nt(left, right):
    return lax.dot_general(left, right, (((1,), (1,)), ((), ())), preferred_element_type=F32)


def tn(left, right):
    return lax.dot_general(left, right, (((0,), (0,)), ((), ())), preferred_element_type=F32)


def iota(shape, axis):
    return lax.broadcasted_iota(jnp.int32, shape, axis)


def identity(size):
    return jnp.where(iota((size, size), 0) == iota((size, size), 1), 1.0, 0.0).astype(BF16)


def scan_windows(sides_ref, info_ref, windows):
    slots = sides_ref.shape[-1]

    def clear(index, carry):
        for kind in range(3):
            info_ref[kind, index] = 0
            info_ref[kind, OFFSET + windows + index] = 0
        return carry

    lax.fori_loop(0, OFFSET, clear, 0)

    def body(window, carry):
        slot, row, col = carry
        side = jnp.where(slot < slots, sides_ref[0, jnp.minimum(slot, slots - 1)], 0)
        info_ref[0, OFFSET + window] = side
        info_ref[1, OFFSET + window] = row
        info_ref[2, OFFSET + window] = col
        end_col = col + 1 >= side
        end_row = row + 1 >= side
        next_slot = jnp.where(end_col & end_row, slot + 1, slot)
        next_row = jnp.where(end_col, jnp.where(end_row, 0, row + 1), row)
        next_col = jnp.where(end_col, 0, col + 1)
        return (next_slot, next_row, next_col)

    zero = jnp.int32(0)
    lax.fori_loop(0, windows, body, (zero, zero, zero))


def window_of(info_ref, window):
    side = info_ref[0, OFFSET + window]
    row = info_ref[1, OFFSET + window]
    col = info_ref[2, OFFSET + window]
    limit = jnp.where(side == 2, 14, jnp.where(side == 3, 18, jnp.where(side == 4, 24, 0)))
    high = jnp.minimum(limit - WS * row, WS)
    wide = jnp.minimum(limit - WS * col, WS)
    return side, row, col, high, wide


def expand(rows_ref, start, high, wide):
    base = pl.multiple_of((start // 16) * 16, 16)
    shift = start - base
    place = iota((SLOT, TALL), 0)
    patch_row, patch_col = place >> 3, place & 7
    hit = (
        (iota((SLOT, TALL), 1) == WS * patch_row + patch_col + shift)
        & (patch_col < wide)
        & (patch_row < high)
    )
    return nn(jnp.where(hit, 1.0, 0.0).astype(BF16), rows_ref[pl.ds(base, TALL), :])


def contract_mask(step, rows):
    first = rows * step
    window = first // CELLS
    shift = first - CELLS * window
    source = iota((rows, BLOCK * SLOT), 1)
    hit = (iota((rows, BLOCK * SLOT), 0) + shift == WS * (source >> 3) + (source & 7)) & (
        (source & 7) < WS
    )
    return window, jnp.where(hit, 1.0, 0.0).astype(BF16)


def near(ext_ref, place, side, row, col):
    lane_col = iota((1, 8, ext_ref.shape[-1]), 1)
    first = jnp.where(col > 0, 0, 8)
    last = jnp.where(col < side - 1, WS - 1, 8)

    def triple(window, rows):
        own = ext_ref[window, rows]
        left = pltpu.roll(ext_ref[window - 1, rows], 2, 1)
        right = pltpu.roll(ext_ref[window + 1, rows], 6, 1)
        return (
            jnp.where(lane_col == first, left, pltpu.roll(own, 1, 1)),
            own,
            jnp.where(lane_col == last, right, pltpu.roll(own, 7, 1)),
        )

    above_on = jnp.where(row > 0, 1.0, 0.0)
    below_on = jnp.where(row < side - 1, 1.0, 0.0)
    above = triple(place - side, slice(WS - 1, WS))
    middle = triple(place, slice(0, WS))
    below = triple(place + side, slice(0, 1))
    return [
        jnp.concatenate([up * above_on, mid, down * below_on], axis=0)
        for up, mid, down in zip(above, middle, below)
    ]


def valid_cells(high, wide, width):
    shape = (WS, 8, width)
    return (iota(shape, 0) < high) & (iota(shape, 1) < wide)


def fold(values):
    rows, width = values.shape
    return jnp.sum(values.reshape(rows // 8, 8, width), axis=0)


def normalize(values):
    centre = values - jnp.mean(values, axis=-1, keepdims=True)
    inverse = lax.rsqrt(jnp.mean(centre * centre, axis=-1, keepdims=True) + 1e-06)
    return centre * inverse, inverse


def normalize_back(gradient, scaled, inverse, gain):
    d_scaled = gradient * gain
    mean_one = jnp.mean(d_scaled, axis=-1, keepdims=True)
    mean_two = jnp.mean(d_scaled * scaled, axis=-1, keepdims=True)
    return inverse * (d_scaled - mean_one - scaled * mean_two)


def stack_heads(values):
    head = iota(values.shape, 1) // HDIM
    zero = jnp.zeros_like(values)
    return jnp.concatenate([jnp.where(head == g, values, zero) for g in range(128 // HDIM)], axis=0)


def pick_heads(stacked):
    head = iota((TALL, 128), 1) // HDIM
    taken = stacked[0:TALL]
    for g in range(1, 128 // HDIM):
        taken = jnp.where(head == g, stacked[TALL * g : TALL * (g + 1)], taken)
    return taken


def to_tall(rows):
    return jnp.concatenate([rows, jnp.zeros((TALL - SLOT, rows.shape[1]), F32)], axis=0).astype(
        BF16
    )


def gelu_parts(values):
    cdf = 0.5 + 0.5 * lax.erf(values * (0.5**0.5))
    density = jnp.exp(-0.5 * values * values) * 0.3989422804014327
    return values * cdf, cdf + values * density


def rows_at(index, size):
    return pl.ds(pl.multiple_of(index * size, size), size)


def front(first, tokens_ref, og_ref, info_ref, ext_ref, dout_ref, windows):
    def source(place, carry):
        _, _, _, high, wide = window_of(info_ref, first + place - MARGIN)
        start = HALO - MARGIN * CELLS + CELLS * place
        ext_ref[place] = expand(tokens_ref, start, high, wide).reshape(WS, 8, -1)
        return carry

    lax.fori_loop(0, windows + 2 * MARGIN, source, 0, unroll=2)

    def cotangent(window, carry):
        _, _, _, high, wide = window_of(info_ref, first + window)
        dout_ref[rows_at(window, SLOT), :] = expand(og_ref, CELLS * window, high, wide)
        return carry

    lax.fori_loop(0, windows, cotangent, 0, unroll=2)


def field_pass(first, info_ref, ext_ref, peg_ref, peg_bias_ref, gain_ref, shift_ref, field_ref, scaled_ref, inverse_ref, normed_ref, windows):
    def pair(step, carry):
        normed = []
        for sub in range(2):
            window = 2 * step + sub
            side, row, col, high, wide = window_of(info_ref, first + window)
            bands = near(ext_ref, window + MARGIN, side, row, col)
            total = bands[1][1 : 1 + WS] + peg_bias_ref[...]
            for a in range(3):
                for b in range(3):
                    tap = 3 * a + b
                    total = total + bands[b][a : a + WS] * peg_ref[tap : tap + 1, :]
            total = jnp.where(valid_cells(high, wide, total.shape[-1]), total, 0.0)
            field = total.reshape(SLOT, -1)
            scaled, inverse = normalize(field)
            place = rows_at(window, SLOT)
            field_ref[place, :] = field
            scaled_ref[place, :] = scaled
            inverse_ref[place, :] = inverse
            normed.append(scaled * gain_ref[0:1, :] + shift_ref[0:1, :])
        normed_ref[rows_at(step, 2 * SLOT), :] = jnp.concatenate(normed, axis=0).astype(BF16)
        return carry

    lax.fori_loop(0, windows // 2, pair, 0)


def attend(qkv, high, wide, probs_ref, window):
    width = qkv.shape[1] // 3
    key = iota((TALL, 256), 0)
    usable = ((key >> 3) < high) & ((key & 7) < wide)
    halves = []
    for half in range(width // 128):
        query, keys, value = (
            qkv[:, width * t + 128 * half : width * t + 128 * (half + 1)] for t in range(3)
        )
        scores = jnp.where(usable, nt(keys, stack_heads(query)), -1e30)
        top = jnp.max(scores, axis=0, keepdims=True)
        exponent = jnp.exp((scores - top) * HDIM**-0.5)
        probs = exponent * (1.0 / jnp.sum(exponent, axis=0, keepdims=True))
        probs_ref[window, :, 256 * half : 256 * (half + 1)] = probs
        halves.append(pick_heads(tn(probs.astype(BF16), value)))
    return jnp.concatenate(halves, axis=1)


def attend_back(qkv, d_context, probs_ref, window):
    width = qkv.shape[1] // 3
    d_query, d_key, d_value = [], [], []
    for half in range(width // 128):
        query, keys, value = (
            qkv[:, width * t + 128 * half : width * t + 128 * (half + 1)] for t in range(3)
        )
        d_stack = stack_heads(d_context[:, 128 * half : 128 * (half + 1)])
        probs = probs_ref[window, :, 256 * half : 256 * (half + 1)]
        d_value.append(nn(probs.astype(BF16), d_stack))
        d_probs = nt(value, d_stack)
        inner = jnp.sum(d_probs * probs, axis=0, keepdims=True)
        d_score = (probs * (d_probs - inner)).astype(BF16)
        d_key.append(nn(d_score, stack_heads(query)) * HDIM**-0.5)
        d_query.append(pick_heads(tn(d_score, keys)) * HDIM**-0.5)
    return jnp.concatenate(d_query + d_key + d_value, axis=1)


def forward_block(first, refs, step):
    (info_ref, dout_ref, field_ref, normed_ref, wt_ref, proj_ref, proj_bias_ref, fc_ref, fc_in_bias_ref, fc_out_bias_ref,
     gain_ref, shift_ref, qkv_ref, probs_ref, context_ref, hidden_ref, result_ref, g_fc_ref, g_proj_ref, sums_ref, bias_ref) = refs
    rows = BLOCK * SLOT
    place = rows_at(step, rows)
    projected = nt(normed_ref[place, :], wt_ref[...])
    context = []
    for sub in range(BLOCK):
        window = BLOCK * step + sub
        _, _, _, high, wide = window_of(info_ref, first + window)
        qkv = to_tall(projected[SLOT * sub : SLOT * (sub + 1)])
        qkv_ref[window] = qkv
        context.append(attend(qkv, high, wide, probs_ref, window)[0:SLOT])
    context = jnp.concatenate(context, axis=0).astype(BF16)
    context_ref[place, :] = context
    hidden = field_ref[place, :] + nn(context, proj_ref[...]) + proj_bias_ref[...]
    scaled, inverse = normalize(hidden)
    normed = (scaled * gain_ref[1:2, :] + shift_ref[1:2, :]).astype(BF16)
    d_output = dout_ref[place, :]
    d_low = d_output.astype(BF16)
    normed_t = normed.T
    d_low_t = d_low.T
    ones = jnp.ones((8, rows), BF16)
    result = hidden + fc_out_bias_ref[...]
    d_normed = jnp.zeros_like(hidden)
    width = 256
    for chunk in range(fc_ref.shape[1] // width):
        cols = slice(width * chunk, width * (chunk + 1))
        w_in, w_out = fc_ref[0, cols, :], fc_ref[1, cols, :]
        pre = nt(normed, w_in) + fc_in_bias_ref[:, cols]
        active, slope = gelu_parts(pre)
        active = active.astype(BF16)
        d_pre = (nt(d_low, w_out) * slope).astype(BF16)
        result = result + nn(active, w_out)
        d_normed = d_normed + nn(d_pre, w_in)
        g_fc_ref[0, :, cols] += nn(normed_t, d_pre)
        g_fc_ref[1, :, cols] += nn(d_low_t, active)
        bias_ref[:, cols] += nn(ones, d_pre)
    result_ref[place, :] = result
    d_hidden = d_output + normalize_back(d_normed, scaled, inverse, gain_ref[1:2, :])
    hidden_ref[place, :] = d_hidden
    d_branch = d_hidden.astype(BF16)
    g_proj_ref[...] += nn(context.T, d_branch)
    sums_ref[0] += fold(d_branch.astype(F32))
    sums_ref[1] += fold(d_output)
    sums_ref[3] += fold(d_normed * scaled)
    sums_ref[5] += fold(d_normed)


def backward_block(first, refs, step):
    (info_ref, hidden_ref, proj_ref, qkv_ref, probs_ref, wt_ref, normed_ref, scaled_ref, inverse_ref, gain_ref,
     g_qkv_ref, sums_ref, mixed_ref) = refs
    rows = BLOCK * SLOT
    place = rows_at(step, rows)
    d_hidden = hidden_ref[place, :]
    d_context = nt(d_hidden.astype(BF16), proj_ref[...])
    d_qkv = []
    for sub in range(BLOCK):
        window = BLOCK * step + sub
        d_qkv.append(
            attend_back(
                qkv_ref[window],
                to_tall(d_context[SLOT * sub : SLOT * (sub + 1)]),
                probs_ref,
                window,
            )[0:SLOT]
        )
    d_qkv = jnp.concatenate(d_qkv, axis=0).astype(BF16)
    d_normed = nn(d_qkv, wt_ref[...])
    g_qkv_ref[...] += nn(normed_ref[place, :].T, d_qkv)
    scaled = scaled_ref[place, :]
    sums_ref[2] += fold(d_normed * scaled)
    sums_ref[4] += fold(d_normed)
    d_field = d_hidden + normalize_back(d_normed, scaled, inverse_ref[place, :], gain_ref[0:1, :])
    for sub in range(BLOCK):
        window = BLOCK * step + sub
        _, _, _, high, wide = window_of(info_ref, first + window)
        cells = d_field[SLOT * sub : SLOT * (sub + 1)].reshape(WS, 8, -1)
        mixed_ref[window] = jnp.where(valid_cells(high, wide, cells.shape[-1]), cells, 0.0)


def shrink(first, info_ref, padded_ref, dense_ref, exact):
    rows = 112

    def body(step, carry):
        window, hit = contract_mask(step, rows)
        values = padded_ref[pl.ds(pl.multiple_of(SLOT * window, 8), BLOCK * SLOT), :]
        high = values.astype(BF16)
        dense = nn(hit, high)
        if exact:
            dense = dense + nn(hit, (values - high.astype(F32)).astype(BF16))
        dense_ref[rows_at(step, rows), :] = dense.astype(dense_ref.dtype)
        return carry

    lax.fori_loop(0, dense_ref.shape[0] // rows, body, 0)


def compute_kernel(heads, sides_ref, tokens_ref, og_ref, wt_ref, proj_ref, fc_ref, proj_bias_ref, fc_in_bias_ref, fc_out_bias_ref,
                   gain_ref, shift_ref, peg_ref, peg_bias_ref,
                   output_ref, mixed_ref, ext_ref, g_fc_out_ref, g_at_ref, small_ref,
                   info_ref, dout_ref, field_ref, scaled_ref, inverse_ref, normed_ref, qkv_ref, probs_ref, context_ref, hidden_ref,
                   result_ref, g_fc_ref, g_proj_ref, g_qkv_ref, sums_ref, bias_ref):
    windows = mixed_ref.shape[0]
    first = lax.axis_index("head") * windows
    scan_windows(sides_ref, info_ref, heads * windows)
    front(first, tokens_ref, og_ref, info_ref, ext_ref, dout_ref, windows)
    for ref in (g_fc_ref, g_proj_ref, g_qkv_ref, sums_ref, bias_ref):
        ref[...] = jnp.zeros_like(ref)
    result_ref[windows * SLOT :, :] = jnp.zeros((result_ref.shape[0] - windows * SLOT, result_ref.shape[1]), F32)
    field_pass(first, info_ref, ext_ref, peg_ref, peg_bias_ref, gain_ref, shift_ref, field_ref, scaled_ref, inverse_ref, normed_ref, windows)
    forward_refs = (info_ref, dout_ref, field_ref, normed_ref, wt_ref, proj_ref, proj_bias_ref, fc_ref, fc_in_bias_ref, fc_out_bias_ref,
                    gain_ref, shift_ref, qkv_ref, probs_ref, context_ref, hidden_ref, result_ref, g_fc_ref, g_proj_ref, sums_ref, bias_ref)
    backward_refs = (info_ref, hidden_ref, proj_ref, qkv_ref, probs_ref, wt_ref, normed_ref, scaled_ref, inverse_ref, gain_ref,
                     g_qkv_ref, sums_ref, mixed_ref)

    def forward(step, carry):
        forward_block(first, forward_refs, step)
        return carry

    lax.fori_loop(0, windows // BLOCK, forward, 0)

    def mask_result(window, carry):
        _, _, _, high, wide = window_of(info_ref, first + window)
        place = rows_at(window, SLOT)
        cells = result_ref[place, :].reshape(WS, 8, -1)
        result_ref[place, :] = jnp.where(valid_cells(high, wide, cells.shape[-1]), cells, 0.0).reshape(SLOT, -1)
        return carry

    lax.fori_loop(0, windows, mask_result, 0)
    shrink(first, info_ref, result_ref, output_ref, False)

    def backward(step, carry):
        backward_block(first, backward_refs, step)
        return carry

    lax.fori_loop(0, windows // BLOCK, backward, 0)

    eye = identity(256)
    for kind in range(2):
        for chunk in range(g_fc_out_ref.shape[1] // 256):
            cols = slice(256 * chunk, 256 * (chunk + 1))
            g_fc_out_ref[kind, cols, :] = nt(eye, g_fc_ref[kind, :, cols].astype(BF16)).astype(BF16)
    for kind in range(3):
        cols = slice(256 * kind, 256 * (kind + 1))
        g_at_ref[kind] = nt(eye, g_qkv_ref[:, cols].astype(BF16)).astype(BF16)
    g_at_ref[3] = g_proj_ref[...].astype(BF16)
    small_ref[...] = jnp.zeros_like(small_ref)
    total = jnp.sum(sums_ref[...], axis=1)
    small_ref[0:1, :] = total[0:1]
    for chunk in range(4):
        small_ref[1 + chunk : 2 + chunk, :] = bias_ref[0:1, 256 * chunk : 256 * (chunk + 1)]
    small_ref[5:6, :] = total[1:2]
    small_ref[6:10, :] = total[2:6]


def peg_back(first, info_ref, ext_ref, mixed_ref, peg_ref, taps_ref, source_ref, windows):
    def body(window, carry):
        side, row, col, high, wide = window_of(info_ref, first + window)
        bands = near(ext_ref, window + MARGIN, side, row, col)
        grads = near(mixed_ref, window + MARGIN, side, row, col)
        own = grads[1][1 : 1 + WS]
        total = own
        for a in range(3):
            for b in range(3):
                tap = 3 * a + b
                taps_ref[tap] += jnp.sum(own * bands[b][a : a + WS], axis=0)
                total = total + grads[2 - b][2 - a : 2 - a + WS] * peg_ref[tap : tap + 1, :]
        taps_ref[9] += jnp.sum(own, axis=0)
        total = jnp.where(valid_cells(high, wide, total.shape[-1]), total, 0.0)
        source_ref[rows_at(window, SLOT), :] = total.reshape(SLOT, -1)
        return carry

    lax.fori_loop(0, windows, body, 0)


def peg_kernel(heads, sides_ref, ext_ref, mixed_ref, peg_ref, d_tokens_ref, taps_out_ref, info_ref, taps_ref, source_ref):
    windows = ext_ref.shape[0] - 2 * MARGIN
    first = lax.axis_index("head") * windows
    scan_windows(sides_ref, info_ref, heads * windows)
    taps_ref[...] = jnp.zeros_like(taps_ref)
    source_ref[windows * SLOT :, :] = jnp.zeros((source_ref.shape[0] - windows * SLOT, source_ref.shape[1]), F32)
    peg_back(first, info_ref, ext_ref, mixed_ref, peg_ref, taps_ref, source_ref, windows)
    taps_out_ref[...] = jnp.sum(taps_ref[...], axis=1)
    shrink(first, info_ref, source_ref, d_tokens_ref, True)


def vmem():
    return pl.BlockSpec(memory_space=pltpu.VMEM)


def smem():
    return pl.BlockSpec(memory_space=pltpu.SMEM)


def on_device(tokens, image_sides, qkv_weight, proj_weight, proj_bias, fc_in, fc_in_bias, fc_out, fc_out_bias,
              norm_gains, norm_shifts, peg_weight, peg_bias, out_grad):
    own_rows, width = tokens.shape
    windows = own_rows // CELLS
    heads = lax.axis_size("head")
    hidden = fc_in_bias.shape[0]
    padded = windows * SLOT
    extra = (windows + BLOCK) * SLOT
    me = lax.axis_index("head")

    gathered = lax.all_gather(tokens, "head", axis=0, tiled=True)
    gathered = jnp.pad(gathered, ((HALO, HALO), (0, 0)))
    tokens_ext = lax.dynamic_slice_in_dim(gathered, me * own_rows, own_rows + 2 * HALO, 0)
    qkv_t = jnp.swapaxes(qkv_weight, 1, 2)
    wt = lax.all_gather(qkv_t, "head", axis=1, tiled=True).reshape(-1, width)
    proj = lax.all_gather(proj_weight, "head", axis=0, tiled=True)
    fc = jnp.stack([
        lax.all_gather(fc_in, ("img", "head"), axis=0, tiled=True),
        lax.all_gather(fc_out, ("img", "head"), axis=0, tiled=True),
    ])

    shape = jax.ShapeDtypeStruct
    output, mixed, ext, g_fc, g_at, small = pl.pallas_call(
        functools.partial(compute_kernel, heads),
        out_shape=(
            shape((own_rows, width), BF16),
            shape((windows, WS, 8, width), F32),
            shape((windows + 2 * MARGIN, WS, 8, width), F32),
            shape((2, hidden, width), BF16),
            shape((4, width, width), BF16),
            shape((SMALL, width), F32),
        ),
        in_specs=[smem()] + [vmem()] * 12,
        out_specs=(vmem(),) * 6,
        scratch_shapes=[
            pltpu.SMEM((3, heads * windows + 2 * OFFSET), jnp.int32),
            pltpu.VMEM((padded, width), F32),
            pltpu.VMEM((padded, width), F32),
            pltpu.VMEM((padded, width), F32),
            pltpu.VMEM((padded, 1), F32),
            pltpu.VMEM((padded, width), BF16),
            pltpu.VMEM((windows, TALL, 3 * width), BF16),
            pltpu.VMEM((windows, TALL, 2 * width), F32),
            pltpu.VMEM((padded, width), BF16),
            pltpu.VMEM((padded, width), F32),
            pltpu.VMEM((extra, width), F32),
            pltpu.VMEM((2, width, hidden), F32),
            pltpu.VMEM((width, width), F32),
            pltpu.VMEM((width, 3 * width), F32),
            pltpu.VMEM((6, 8, width), F32),
            pltpu.VMEM((8, hidden), F32),
        ],
        compiler_params=pltpu.CompilerParams(vmem_limit_bytes=VMEM_LIMIT),
        name="block",
    )(image_sides, tokens_ext, out_grad, wt, proj, fc, proj_bias[None], fc_in_bias[None], fc_out_bias[None],
      norm_gains, norm_shifts, peg_weight, peg_bias[None])

    before = [(i, i + 1) for i in range(heads - 1)]
    after = [(i + 1, i) for i in range(heads - 1)]
    left = lax.ppermute(mixed[windows - MARGIN :].astype(BF16), "head", before).astype(F32)
    right = lax.ppermute(mixed[:MARGIN].astype(BF16), "head", after).astype(F32)
    mixed_ext = jnp.concatenate([left, mixed, right], axis=0)

    d_tokens, taps = pl.pallas_call(
        functools.partial(peg_kernel, heads),
        out_shape=(shape((own_rows, width), F32), shape((10, width), F32)),
        in_specs=[smem()] + [vmem()] * 3,
        out_specs=(vmem(),) * 2,
        scratch_shapes=[
            pltpu.SMEM((3, heads * windows + 2 * OFFSET), jnp.int32),
            pltpu.VMEM((10, 8, width), F32),
            pltpu.VMEM((extra, width), F32),
        ],
        compiler_params=pltpu.CompilerParams(vmem_limit_bytes=VMEM_LIMIT),
        name="peg_back",
    )(image_sides, ext, mixed_ext, peg_weight)

    small = small.at[10:20].set(taps)
    small = lax.psum(small, ("img", "head"))
    d_fc_in = lax.psum_scatter(g_fc[0].astype(F32), ("img", "head"), scatter_dimension=0, tiled=True)
    d_fc_out = lax.psum_scatter(g_fc[1].astype(F32), ("img", "head"), scatter_dimension=0, tiled=True)
    g_at = lax.psum(lax.psum_scatter(g_at.astype(F32), "head", scatter_dimension=1, tiled=True), "img")
    return (
        output,
        d_tokens,
        jnp.swapaxes(g_at[:3], 1, 2),
        g_at[3],
        small[0],
        d_fc_in,
        small[1:5].reshape(-1),
        d_fc_out,
        small[5],
        small[6:8],
        small[8:10],
        small[10:19],
        small[19],
    )


def solution(mesh):
    rows = P(("img", "head"), None)
    placed = (rows, P("img", None), P(None, None, "head"), P("head", None), P(), rows, P(), rows, P(), P(), P(), P(), P(), rows)
    return jax.shard_map(
        on_device,
        mesh=mesh,
        in_specs=placed,
        out_specs=(rows, rows, P(None, None, "head"), P("head", None), P(), rows, P(), rows, P(), P(), P(), P(), P()),
        check_vma=False,
    )
```

```python
import functools
from types import SimpleNamespace

import jax
import jax.numpy as jnp
from jax import lax
from jax.experimental import pallas as pl
from jax.experimental.pallas import tpu as pltpu
from jax.sharding import PartitionSpec as P

F32 = jnp.float32
BF16 = jnp.bfloat16
MESH = pl.DeviceIdType.MESH

HDIM = 32
WS = 7
CELLS = WS * WS
SLOT = WS * 8
TALL = 64
MARGIN = 5
HALO = 256
EDGE = 6
OFFSET = 8
BLOCK = 4
SMALL = 32
VMEM_LIMIT = 56 * 1024 * 1024


def nn(left, right):
    return lax.dot_general(left, right, (((1,), (0,)), ((), ())), preferred_element_type=F32)


def nt(left, right):
    return lax.dot_general(left, right, (((1,), (1,)), ((), ())), preferred_element_type=F32)


def tn(left, right):
    return lax.dot_general(left, right, (((0,), (0,)), ((), ())), preferred_element_type=F32)


def iota(shape, axis):
    return lax.broadcasted_iota(jnp.int32, shape, axis)


def identity(size):
    return jnp.where(iota((size, size), 0) == iota((size, size), 1), 1.0, 0.0).astype(BF16)


def scan_windows(sides_ref, info_ref, windows):
    slots = sides_ref.shape[-1]

    def clear(index, carry):
        for kind in range(3):
            info_ref[kind, index] = 0
            info_ref[kind, OFFSET + windows + index] = 0
        return carry

    lax.fori_loop(0, OFFSET, clear, 0)

    def body(window, carry):
        slot, row, col = carry
        side = jnp.where(slot < slots, sides_ref[0, jnp.minimum(slot, slots - 1)], 0)
        info_ref[0, OFFSET + window] = side
        info_ref[1, OFFSET + window] = row
        info_ref[2, OFFSET + window] = col
        end_col = col + 1 >= side
        end_row = row + 1 >= side
        next_slot = jnp.where(end_col & end_row, slot + 1, slot)
        next_row = jnp.where(end_col, jnp.where(end_row, 0, row + 1), row)
        next_col = jnp.where(end_col, 0, col + 1)
        return (next_slot, next_row, next_col)

    zero = jnp.int32(0)
    lax.fori_loop(0, windows, body, (zero, zero, zero))


def window_of(info_ref, window):
    side = info_ref[0, OFFSET + window]
    row = info_ref[1, OFFSET + window]
    col = info_ref[2, OFFSET + window]
    limit = jnp.where(side == 2, 14, jnp.where(side == 3, 18, jnp.where(side == 4, 24, 0)))
    high = jnp.minimum(limit - WS * row, WS)
    wide = jnp.minimum(limit - WS * col, WS)
    return side, row, col, high, wide


def expand(rows_ref, start, high, wide):
    base = pl.multiple_of((start // 16) * 16, 16)
    shift = start - base
    place = iota((SLOT, TALL), 0)
    patch_row, patch_col = place >> 3, place & 7
    hit = (
        (iota((SLOT, TALL), 1) == WS * patch_row + patch_col + shift)
        & (patch_col < wide)
        & (patch_row < high)
    )
    return nn(jnp.where(hit, 1.0, 0.0).astype(BF16), rows_ref[pl.ds(base, TALL), :])


def contract_mask(step, rows):
    first = rows * step
    window = first // CELLS
    shift = first - CELLS * window
    source = iota((rows, BLOCK * SLOT), 1)
    hit = (iota((rows, BLOCK * SLOT), 0) + shift == WS * (source >> 3) + (source & 7)) & (
        (source & 7) < WS
    )
    return window, jnp.where(hit, 1.0, 0.0).astype(BF16)


def near(ext_ref, place, side, row, col):
    lane_col = iota((1, 8, ext_ref.shape[-1]), 1)
    first = jnp.where(col > 0, 0, 8)
    last = jnp.where(col < side - 1, WS - 1, 8)

    def triple(window, rows):
        own = ext_ref[window, rows]
        left = pltpu.roll(ext_ref[window - 1, rows], 2, 1)
        right = pltpu.roll(ext_ref[window + 1, rows], 6, 1)
        return (
            jnp.where(lane_col == first, left, pltpu.roll(own, 1, 1)),
            own,
            jnp.where(lane_col == last, right, pltpu.roll(own, 7, 1)),
        )

    above_on = jnp.where(row > 0, 1.0, 0.0)
    below_on = jnp.where(row < side - 1, 1.0, 0.0)
    above = triple(place - side, slice(WS - 1, WS))
    middle = triple(place, slice(0, WS))
    below = triple(place + side, slice(0, 1))
    return [
        jnp.concatenate([up * above_on, mid, down * below_on], axis=0)
        for up, mid, down in zip(above, middle, below)
    ]


def valid_cells(high, wide, width):
    shape = (WS, 8, width)
    return (iota(shape, 0) < high) & (iota(shape, 1) < wide)


def fold(values):
    rows, width = values.shape
    return jnp.sum(values.reshape(rows // 8, 8, width), axis=0)


def normalize(values):
    centre = values - jnp.mean(values, axis=-1, keepdims=True)
    inverse = lax.rsqrt(jnp.mean(centre * centre, axis=-1, keepdims=True) + 1e-06)
    return centre * inverse, inverse


def normalize_back(gradient, scaled, inverse, gain):
    d_scaled = gradient * gain
    mean_one = jnp.mean(d_scaled, axis=-1, keepdims=True)
    mean_two = jnp.mean(d_scaled * scaled, axis=-1, keepdims=True)
    return inverse * (d_scaled - mean_one - scaled * mean_two)


def stack_heads(values):
    head = iota(values.shape, 1) // HDIM
    zero = jnp.zeros_like(values)
    return jnp.concatenate([jnp.where(head == g, values, zero) for g in range(128 // HDIM)], axis=0)


def pick_heads(stacked):
    head = iota((TALL, 128), 1) // HDIM
    taken = stacked[0:TALL]
    for g in range(1, 128 // HDIM):
        taken = jnp.where(head == g, stacked[TALL * g : TALL * (g + 1)], taken)
    return taken


def to_tall(rows):
    return jnp.concatenate([rows, jnp.zeros((TALL - SLOT, rows.shape[1]), F32)], axis=0).astype(
        BF16
    )


def gelu_parts(values):
    cdf = 0.5 + 0.5 * lax.erf(values * (0.5**0.5))
    density = jnp.exp(-0.5 * values * values) * 0.3989422804014327
    return values * cdf, cdf + values * density


def rows_at(index, size):
    return pl.ds(pl.multiple_of(index * size, size), size)


def take_tokens(first, r, places):
    def source(place, carry):
        _, _, _, high, wide = window_of(r.info, first + place - MARGIN)
        start = HALO - MARGIN * CELLS + CELLS * place
        r.ext[place] = expand(r.rows, start, high, wide).reshape(WS, 8, -1)
        return carry

    lax.fori_loop(places[0], places[1], source, 0)


def take_cotangent(first, r):
    def cotangent(window, carry):
        _, _, _, high, wide = window_of(r.info, first + window)
        r.dout[rows_at(window, SLOT), :] = expand(r.og, CELLS * window, high, wide)
        return carry

    lax.fori_loop(0, r.windows, cotangent, 0, unroll=2)


def field_pass(first, r):
    def pair(step, carry):
        normed = []
        for sub in range(2):
            window = 2 * step + sub
            side, row, col, high, wide = window_of(r.info, first + window)
            bands = near(r.ext, window + MARGIN, side, row, col)
            total = bands[1][1 : 1 + WS] + r.peg_bias[...]
            for a in range(3):
                for b in range(3):
                    tap = 3 * a + b
                    total = total + bands[b][a : a + WS] * r.peg[tap : tap + 1, :]
            total = jnp.where(valid_cells(high, wide, total.shape[-1]), total, 0.0)
            field = total.reshape(SLOT, -1)
            scaled, inverse = normalize(field)
            place = rows_at(window, SLOT)
            r.field[place, :] = field
            r.scaled[place, :] = scaled
            r.inverse[place, :] = inverse
            normed.append(scaled * r.gain[0:1, :] + r.shift[0:1, :])
        r.normed[rows_at(step, 2 * SLOT), :] = jnp.concatenate(normed, axis=0).astype(BF16)
        return carry

    lax.fori_loop(0, r.windows // 2, pair, 0)


def attend(qkv, high, wide, probs_ref, window):
    width = qkv.shape[1] // 3
    key = iota((TALL, 256), 0)
    usable = ((key >> 3) < high) & ((key & 7) < wide)
    halves = []
    for half in range(width // 128):
        query, keys, value = (
            qkv[:, width * t + 128 * half : width * t + 128 * (half + 1)] for t in range(3)
        )
        scores = jnp.where(usable, nt(keys, stack_heads(query)), -1e30)
        top = jnp.max(scores, axis=0, keepdims=True)
        exponent = jnp.exp((scores - top) * HDIM**-0.5)
        probs = exponent * (1.0 / jnp.sum(exponent, axis=0, keepdims=True))
        probs_ref[window, :, 256 * half : 256 * (half + 1)] = probs
        halves.append(pick_heads(tn(probs.astype(BF16), value)))
    return jnp.concatenate(halves, axis=1)


def attend_back(qkv, d_context, probs_ref, window):
    width = qkv.shape[1] // 3
    d_query, d_key, d_value = [], [], []
    for half in range(width // 128):
        query, keys, value = (
            qkv[:, width * t + 128 * half : width * t + 128 * (half + 1)] for t in range(3)
        )
        d_stack = stack_heads(d_context[:, 128 * half : 128 * (half + 1)])
        probs = probs_ref[window, :, 256 * half : 256 * (half + 1)]
        d_value.append(nn(probs.astype(BF16), d_stack))
        d_probs = nt(value, d_stack)
        inner = jnp.sum(d_probs * probs, axis=0, keepdims=True)
        d_score = (probs * (d_probs - inner)).astype(BF16)
        d_key.append(nn(d_score, stack_heads(query)) * HDIM**-0.5)
        d_query.append(pick_heads(tn(d_score, keys)) * HDIM**-0.5)
    return jnp.concatenate(d_query + d_key + d_value, axis=1)


def qkv_weights(r):
    heads, halves = r.at_w.shape[:2]
    return jnp.concatenate(
        [r.at_w[z, half, kind] for kind in range(3) for z in range(heads) for half in range(halves)], axis=0
    )


def proj_weights(r):
    heads, halves = r.at_w.shape[:2]
    return jnp.concatenate([r.at_w[z, half, 3] for z in range(heads) for half in range(halves)], axis=0)


def feed_weights(r, chunk, kind):
    cores, _, heads = r.fc_w.shape[:3]
    return jnp.concatenate(
        [r.fc_w[core, chunk, z, kind] for core in range(cores) for z in range(heads)], axis=0
    )


def attention_block(first, r, step):
    rows = BLOCK * SLOT
    place = rows_at(step, rows)
    width = r.field.shape[1]
    projected = nt(r.normed[place, :], qkv_weights(r))
    context = []
    for sub in range(BLOCK):
        window = BLOCK * step + sub
        _, _, _, high, wide = window_of(r.info, first + window)
        qkv = to_tall(projected[SLOT * sub : SLOT * (sub + 1)])
        r.qkv[window] = qkv
        context.append(attend(qkv, high, wide, r.probs, window)[0:SLOT])
    context = jnp.concatenate(context, axis=0).astype(BF16)
    r.context[place, :] = context
    r.field[place, :] += nn(context, proj_weights(r)) + r.proj_bias[...]


def feed_block(first, r, step):
    rows = BLOCK * SLOT
    place = rows_at(step, rows)
    width = r.field.shape[1]
    hidden = r.field[place, :]
    scaled, inverse = normalize(hidden)
    normed = (scaled * r.gain[1:2, :] + r.shift[1:2, :]).astype(BF16)
    d_output = r.dout[place, :]
    d_low = d_output.astype(BF16)
    normed_t = normed.T
    d_low_t = d_low.T
    ones = jnp.ones((8, rows), BF16)
    result = hidden + r.fc_out_bias[...]
    d_normed = jnp.zeros_like(hidden)
    for chunk in range(r.fc_w.shape[1]):
        w_in, w_out = feed_weights(r, chunk, 0), feed_weights(r, chunk, 1)
        cols = slice(w_in.shape[0] * chunk, w_in.shape[0] * (chunk + 1))
        pre = nt(normed, w_in) + r.fc_in_bias[:, cols]
        active, slope = gelu_parts(pre)
        active = active.astype(BF16)
        d_pre = (nt(d_low, w_out) * slope).astype(BF16)
        result = result + nn(active, w_out)
        d_normed = d_normed + nn(d_pre, w_in)
        r.g_fc_t[0, :, cols] += nn(normed_t, d_pre)
        r.g_fc_t[1, :, cols] += nn(d_low_t, active)
        r.bias[:, cols] += nn(ones, d_pre)
    for sub in range(BLOCK):
        _, _, _, high, wide = window_of(r.info, first + BLOCK * step + sub)
        cells = result[SLOT * sub : SLOT * (sub + 1)].reshape(WS, 8, -1)
        cells = jnp.where(valid_cells(high, wide, width), cells, 0.0)
        r.result[rows_at(BLOCK * step + sub, SLOT), :] = cells.reshape(SLOT, -1)
    d_hidden = d_output + normalize_back(d_normed, scaled, inverse, r.gain[1:2, :])
    r.hidden[place, :] = d_hidden
    d_branch = d_hidden.astype(BF16)
    r.g_proj[...] += nn(r.context[place, :].T, d_branch)
    r.sums[0] += fold(d_branch.astype(F32))
    r.sums[1] += fold(d_output)
    r.sums[3] += fold(d_normed * scaled)
    r.sums[5] += fold(d_normed)


def backward_block(first, r, step):
    rows = BLOCK * SLOT
    place = rows_at(step, rows)
    width = r.field.shape[1]
    d_hidden = r.hidden[place, :]
    d_context = nt(d_hidden.astype(BF16), proj_weights(r))
    d_qkv = []
    for sub in range(BLOCK):
        window = BLOCK * step + sub
        d_window = to_tall(d_context[SLOT * sub : SLOT * (sub + 1)])
        d_qkv.append(attend_back(r.qkv[window], d_window, r.probs, window)[0:SLOT])
    d_qkv = jnp.concatenate(d_qkv, axis=0).astype(BF16)
    d_normed = nn(d_qkv, qkv_weights(r))
    r.g_qkv[...] += nn(r.normed[place, :].T, d_qkv)
    scaled = r.scaled[place, :]
    r.sums[2] += fold(d_normed * scaled)
    r.sums[4] += fold(d_normed)
    d_field = d_hidden + normalize_back(d_normed, scaled, r.inverse[place, :], r.gain[0:1, :])
    for sub in range(BLOCK):
        window = BLOCK * step + sub
        side, row, col, high, wide = window_of(r.info, first + window)
        own = d_field[SLOT * sub : SLOT * (sub + 1)].reshape(WS, 8, -1)
        own = jnp.where(valid_cells(high, wide, width), own, 0.0)
        r.mixed[window + MARGIN] = own
        bands = near(r.ext, window + MARGIN, side, row, col)
        for a in range(3):
            for b in range(3):
                r.sums[6 + 3 * a + b] += jnp.sum(own * bands[b][a : a + WS], axis=0)
        r.sums[15] += jnp.sum(own, axis=0)


def token_pass(first, r, start, stop):
    def body(window, carry):
        side, row, col, high, wide = window_of(r.info, first + window)
        grads = near(r.mixed, window + MARGIN, side, row, col)
        total = grads[1][1 : 1 + WS]
        for a in range(3):
            for b in range(3):
                tap = 3 * a + b
                total = total + grads[2 - b][2 - a : 2 - a + WS] * r.peg[tap : tap + 1, :]
        total = jnp.where(valid_cells(high, wide, total.shape[-1]), total, 0.0)
        r.source[rows_at(window, SLOT), :] = total.reshape(SLOT, -1)
        return carry

    lax.fori_loop(start, stop, body, 0)


def shrink(padded_ref, dense_ref, exact):
    rows = 112

    def body(step, carry):
        window, hit = contract_mask(step, rows)
        values = padded_ref[pl.ds(pl.multiple_of(SLOT * window, 8), BLOCK * SLOT), :]
        high = values.astype(BF16)
        dense = nn(hit, high)
        if exact:
            dense = dense + nn(hit, (values - high.astype(F32)).astype(BF16))
        dense_ref[rows_at(step, rows), :] = dense.astype(dense_ref.dtype)
        return carry

    lax.fori_loop(0, dense_ref.shape[0] // rows, body, 0)


def clear(r):
    for ref in (r.g_fc_t, r.g_proj, r.g_qkv, r.sums, r.bias):
        ref[...] = jnp.zeros_like(ref)
    tail = r.windows * SLOT
    for ref in (r.result, r.source):
        ref[tail:, :] = jnp.zeros((ref.shape[0] - tail, ref.shape[1]), F32)


def turn_feed_gradients(r):
    eye = identity(256)
    cores, quads, heads, _, own, _ = r.g_fc.shape
    for kind in range(2):
        for chunk in range(quads):
            piece = r.g_fc_t[kind, :, 256 * chunk : 256 * (chunk + 1)].astype(BF16)
            turned = nt(eye, piece).astype(BF16)
            for core in range(cores):
                for z in range(heads):
                    place = own * (heads * core + z)
                    r.g_fc[core, chunk, z, kind] = turned[place : place + own]


def turn_attention_gradients(r):
    eye = identity(256)
    halves, _, heads, piece, _ = r.g_at.shape
    for kind in range(4):
        if kind < 3:
            turned = nt(eye, r.g_qkv[:, 256 * kind : 256 * (kind + 1)].astype(BF16)).astype(BF16)
        else:
            turned = r.g_proj[...].astype(BF16)
        for half in range(halves):
            for z in range(heads):
                place = piece * (halves * z + half)
                r.g_at[half, kind, z] = turned[place : place + piece]


def collect_small(r):
    total = jnp.sum(r.sums[...], axis=1)
    r.small[...] = jnp.zeros_like(r.small)
    r.small[0:1, :] = total[0:1]
    for chunk in range(4):
        r.small[1 + chunk : 2 + chunk, :] = r.bias[0:1, 256 * chunk : 256 * (chunk + 1)]
    r.small[5:6, :] = total[1:2]
    r.small[6:10, :] = total[2:6]
    r.small[10:20, :] = total[6:16]


def loop(start, stop, body):
    def step(index, carry):
        body(index)
        return carry

    lax.fori_loop(start, stop, step, 0)


COPIES = 50


def fused_kernel(names, *refs):
    r = SimpleNamespace(**dict(zip(names, refs)))
    r.windows = r.mixed.shape[0] - 2 * MARGIN
    blocks = r.windows // BLOCK
    own_rows = r.tokens.shape[0]
    heads = r.at_w.shape[0]
    quads = r.fc_w.shape[1]
    z, img = lax.axis_index("head"), lax.axis_index("img")
    yx, core = img // 2, img % 2
    other = 1 - core
    first = z * r.windows

    def flip(value, mask):
        low, high = value % 2, value // 2
        low = 1 - low if mask & 1 else low
        high = 1 - high if mask & 2 else high
        return 2 * high + low

    z_peer = {m: (img, flip(z, m)) for m in range(1, heads)}
    yx_peer = {m: (2 * flip(yx, m) + core, z) for m in range(1, quads)}
    sibling = (2 * yx + other, z)
    cross = {m: (2 * flip(yx, m) + other, z) for m in range(1, quads)}
    plane = [yx_peer[m] for m in yx_peer] + [sibling] + [cross[m] for m in cross]

    def copy(index, source, target, device):
        return pltpu.make_async_remote_copy(
            src_ref=source,
            dst_ref=target,
            send_sem=r.send.at[index],
            recv_sem=r.recv.at[index],
            device_id=device,
            device_id_type=MESH,
        )

    forth = copy(0, r.tokens.at[own_rows - HALO : own_rows], r.rows.at[0:HALO], (img, z + 1))
    back = copy(1, r.tokens.at[0:HALO], r.rows.at[HALO + own_rows :], (img, z - 1))
    at_z = [copy(1 + m, r.at_w.at[z, core], r.at_w.at[z, core], z_peer[m]) for m in z_peer]
    at_core = [copy(4 + m, r.at_w.at[flip(z, m), core], r.at_w.at[flip(z, m), core], sibling) for m in z_peer]
    fc_z = [copy(7 + m, r.fc_w.at[core, yx, z], r.fc_w.at[core, yx, z], z_peer[m]) for m in z_peer]
    fc_yx = [copy(10 + m, r.fc_w.at[core, yx], r.fc_w.at[core, yx], yx_peer[m]) for m in yx_peer]
    fc_core = copy(14, r.fc_w.at[core], r.fc_w.at[core], sibling)
    gf_core = copy(15, r.g_fc.at[other], r.gf_one, sibling)
    gf_yx = [copy(15 + m, r.gf_two.at[flip(yx, m)], r.gf_three.at[m - 1], yx_peer[m]) for m in yx_peer]
    gf_z = [copy(18 + m, r.gf_four.at[flip(z, m)], r.gf_five.at[m - 1], z_peer[m]) for m in z_peer]
    ga_core = copy(22, r.g_at.at[other], r.ga_one, sibling)
    ga_yx = [copy(22 + m, r.ga_two.at[flip(yx, m)], r.ga_three.at[m - 1], yx_peer[m]) for m in yx_peer]
    ga_z = [copy(25 + m, r.ga_four.at[flip(z, m)], r.ga_five.at[m - 1], z_peer[m]) for m in z_peer]
    ga_plane = [copy(29 + i, r.ga_all.at[yx, core], r.ga_all.at[yx, core], peer) for i, peer in enumerate(plane)]
    sm_plane = [copy(36 + i, r.small, r.small_plane.at[yx, core], peer) for i, peer in enumerate(plane)]
    sm_z = [copy(42 + m, r.small_sum, r.small_z.at[z], z_peer[m]) for m in z_peer]
    mix_forth = copy(46, r.edge_out.at[0], r.edge_in.at[0], (img, z + 1))
    mix_back = copy(47, r.edge_out.at[1], r.edge_in.at[1], (img, z - 1))

    eye = identity(r.qkv_w.shape[2])
    for kind in range(4):
        turned = nt(eye, r.qkv_w[kind]).astype(BF16) if kind < 3 else r.proj_w[...]
        for half in range(2):
            r.at_w[z, half, kind] = turned[half * (turned.shape[0] // 2) : (half + 1) * (turned.shape[0] // 2)]
    r.fc_w[core, yx, z, 0] = r.fc_in[...]
    r.fc_w[core, yx, z, 1] = r.fc_out[...]
    barrier = pltpu.get_barrier_semaphore()
    greeted = [z_peer[m] for m in z_peer] + plane
    for peer in greeted:
        pl.semaphore_signal(barrier, inc=1, device_id=peer, device_id_type=MESH)

    pl.semaphore_wait(barrier, len(greeted))

    @pl.when(z < heads - 1)
    def _():
        forth.start()

    @pl.when(z > 0)
    def _():
        back.start()

    for one in at_z + fc_z:
        one.start()

    scan_windows(r.sides, r.info, heads * r.windows)
    clear(r)
    r.rows[HALO : HALO + own_rows, :] = r.tokens[...]

    @pl.when(z == 0)
    def _():
        r.rows[0:HALO, :] = jnp.zeros((HALO, r.rows.shape[1]), BF16)

    @pl.when(z == heads - 1)
    def _():
        r.rows[HALO + own_rows :, :] = jnp.zeros((HALO, r.rows.shape[1]), BF16)

    take_cotangent(first, r)

    @pl.when(z > 0)
    def _():
        forth.wait_recv()

    @pl.when(z < heads - 1)
    def _():
        back.wait_recv()

    take_tokens(first, r, (0, 2 * MARGIN + r.windows))
    for one, two in zip(at_z, at_core):
        one.wait_recv()
        two.start()
    for one in fc_z:
        one.wait_recv()
    for one in fc_yx:
        one.start()
    field_pass(first, r)
    for one in at_core:
        one.wait_recv()

    loop(0, 1, lambda step: attention_block(first, r, step))
    for one in fc_yx:
        one.wait_recv()
    fc_core.start()
    loop(1, blocks, lambda step: attention_block(first, r, step))
    fc_core.wait_recv()
    loop(0, blocks, lambda step: feed_block(first, r, step))
    turn_feed_gradients(r)
    gf_core.start()

    def backward(start, stop):
        loop(start, stop, lambda step: backward_block(first, r, (step + blocks - 2) % blocks))

    backward(0, 2)
    gf_core.wait_recv()
    r.gf_two[...] = (r.g_fc[core].astype(F32) + r.gf_one[...].astype(F32)).astype(BF16)
    for one in gf_yx:
        one.start()
    backward(2, 4)
    edge = EDGE * SLOT
    last = r.mixed[MARGIN + r.windows - EDGE : MARGIN + r.windows]
    r.edge_out[0] = last.reshape(edge, -1).astype(BF16)
    r.edge_out[1] = r.mixed[MARGIN : MARGIN + EDGE].reshape(edge, -1).astype(BF16)

    @pl.when(z < heads - 1)
    def _():
        mix_forth.start()

    @pl.when(z > 0)
    def _():
        mix_back.start()

    backward(4, 5)
    for one in gf_yx:
        one.wait_recv()
    total = r.gf_two[yx].astype(F32)
    for m in range(quads - 1):
        total = total + r.gf_three[m].astype(F32)
    r.gf_four[...] = total.astype(BF16)
    for one in gf_z:
        one.start()
    backward(5, blocks)

    turn_attention_gradients(r)
    ga_core.start()
    collect_small(r)
    for one in sm_plane:
        one.start()
    for one in gf_z:
        one.wait_recv()
    total = r.gf_four[z].astype(F32)
    for m in range(heads - 1):
        total = total + r.gf_five[m].astype(F32)
    r.d_fc_in[...] = total[0]
    r.d_fc_out[...] = total[1]

    shape = (MARGIN, WS, 8, r.mixed.shape[-1])
    skip = (EDGE - MARGIN) * SLOT

    @pl.when(z > 0)
    def _():
        mix_forth.wait_recv()
        r.mixed[0:MARGIN] = r.edge_in[0].astype(F32)[skip:].reshape(shape)

    @pl.when(z == 0)
    def _():
        r.mixed[0:MARGIN] = jnp.zeros(shape, F32)

    @pl.when(z < heads - 1)
    def _():
        mix_back.wait_recv()
        r.mixed[MARGIN + r.windows :] = r.edge_in[1].astype(F32)[0 : MARGIN * SLOT].reshape(shape)

    @pl.when(z == heads - 1)
    def _():
        r.mixed[MARGIN + r.windows :] = jnp.zeros(shape, F32)

    shrink(r.result, r.output, False)
    ga_core.wait_recv()
    r.ga_two[...] = (r.g_at[core].astype(F32) + r.ga_one[...].astype(F32)).astype(BF16)
    for one in ga_yx:
        one.start()
    for one in sm_plane:
        one.wait_recv()
    r.small_plane[yx, core] = r.small[...]
    total = jnp.zeros(r.small.shape, F32)
    for a in range(quads):
        for b in range(2):
            total = total + r.small_plane[a, b]
    r.small_sum[...] = total
    for one in sm_z:
        one.start()
    token_pass(first, r, 0, r.windows // 2)
    for one in ga_yx:
        one.wait_recv()
    total = r.ga_two[yx].astype(F32)
    for m in range(quads - 1):
        total = total + r.ga_three[m].astype(F32)
    r.ga_four[...] = total.astype(BF16)
    for one in ga_z:
        one.start()
    token_pass(first, r, r.windows // 2, r.windows)
    for one in ga_z:
        one.wait_recv()
    total = r.ga_four[z].astype(F32)
    for m in range(heads - 1):
        total = total + r.ga_five[m].astype(F32)
    r.ga_all[yx, core] = total.astype(BF16)
    for one in ga_plane:
        one.start()
    shrink(r.source, r.d_tokens, True)
    for one in sm_z:
        one.wait_recv()
    r.small_z[z] = r.small_sum[...]
    total = jnp.zeros(r.small.shape, F32)
    for a in range(heads):
        total = total + r.small_z[a]
    r.d_proj_bias[...] = total[0:1]
    for chunk in range(4):
        r.d_fc_in_bias[:, 256 * chunk : 256 * (chunk + 1)] = total[1 + chunk : 2 + chunk]
    r.d_fc_out_bias[...] = total[5:6]
    r.d_gains[...] = total[6:8]
    r.d_shifts[...] = total[8:10]
    r.d_peg[...] = total[10:19]
    r.d_peg_bias[...] = total[19:20]
    for one in ga_plane:
        one.wait_recv()
    eye = identity(256)
    for kind in range(3):
        r.d_qkv[kind] = nt(eye, r.ga_all[kind].reshape(-1, 256))
    r.d_proj[...] = r.ga_all[3].reshape(-1, 256).astype(F32)

    for one in at_z + at_core + fc_z + fc_yx + [fc_core, gf_core] + gf_yx + gf_z + [ga_core] + ga_yx + ga_z + ga_plane + sm_plane + sm_z:
        one.wait_send()

    @pl.when(z < heads - 1)
    def _():
        forth.wait_send()
        mix_forth.wait_send()

    @pl.when(z > 0)
    def _():
        back.wait_send()
        mix_back.wait_send()


def local_kernel(names, *refs):
    r = SimpleNamespace(**dict(zip(names, refs)))
    r.windows = r.mixed.shape[0] - 2 * MARGIN
    blocks = r.windows // BLOCK
    first = lax.axis_index("head") * r.windows
    scan_windows(r.sides, r.info, r.at_w.shape[0] * r.windows)
    clear(r)
    take_cotangent(first, r)
    take_tokens(first, r, (0, r.windows + 2 * MARGIN))
    field_pass(first, r)
    loop(0, blocks, lambda step: attention_block(first, r, step))
    loop(0, blocks, lambda step: feed_block(first, r, step))
    turn_feed_gradients(r)
    loop(0, blocks, lambda step: backward_block(first, r, step))
    turn_attention_gradients(r)
    collect_small(r)
    shrink(r.result, r.output, False)
    for edge in (slice(0, MARGIN), slice(MARGIN + r.windows, 2 * MARGIN + r.windows)):
        r.mixed[edge] = jnp.zeros((MARGIN,) + r.mixed.shape[1:], F32)


def token_kernel(names, *refs):
    r = SimpleNamespace(**dict(zip(names, refs)))
    r.windows = r.mixed.shape[0] - 2 * MARGIN
    heads = (r.info.shape[1] - 2 * OFFSET) // r.windows
    first = lax.axis_index("head") * r.windows
    scan_windows(r.sides, r.info, heads * r.windows)
    tail = r.windows * SLOT
    r.source[tail:, :] = jnp.zeros((r.source.shape[0] - tail, r.source.shape[1]), F32)
    token_pass(first, r, 0, r.windows)
    shrink(r.source, r.d_tokens, True)


def vmem():
    return pl.BlockSpec(memory_space=pltpu.VMEM)


def smem():
    return pl.BlockSpec(memory_space=pltpu.SMEM)


def work_buffers(windows, heads, width, hidden):
    padded = windows * SLOT
    extra = (windows + BLOCK) * SLOT
    return {
        "info": pltpu.SMEM((3, heads * windows + 2 * OFFSET), jnp.int32),
        "dout": pltpu.VMEM((padded, width), F32),
        "field": pltpu.VMEM((padded, width), F32),
        "scaled": pltpu.VMEM((padded, width), F32),
        "inverse": pltpu.VMEM((padded, 1), F32),
        "normed": pltpu.VMEM((padded, width), BF16),
        "qkv": pltpu.VMEM((windows, TALL, 3 * width), BF16),
        "probs": pltpu.VMEM((windows, TALL, 2 * width), F32),
        "context": pltpu.VMEM((padded, width), BF16),
        "hidden": pltpu.VMEM((padded, width), F32),
        "result": pltpu.VMEM((extra, width), F32),
        "source": pltpu.VMEM((extra, width), F32),
        "g_fc_t": pltpu.VMEM((2, width, hidden), F32),
        "g_proj": pltpu.VMEM((width, width), F32),
        "g_qkv": pltpu.VMEM((width, 3 * width), F32),
        "sums": pltpu.VMEM((16, 8, width), F32),
        "bias": pltpu.VMEM((8, hidden), F32),
    }


def call(kernel, name, inputs, outputs, scratch, **params):
    names = list(inputs) + list(outputs) + list(scratch)
    results = pl.pallas_call(
        functools.partial(kernel, names),
        out_shape=tuple(outputs.values()),
        in_specs=[smem()] + [vmem()] * (len(inputs) - 1),
        out_specs=(vmem(),) * len(outputs),
        scratch_shapes=list(scratch.values()),
        compiler_params=pltpu.CompilerParams(vmem_limit_bytes=VMEM_LIMIT, **params),
        name=name,
    )(*inputs.values())
    return dict(zip(outputs, results))


def on_any_device(tokens, image_sides, qkv_weight, proj_weight, proj_bias, fc_in, fc_in_bias, fc_out, fc_out_bias,
                  norm_gains, norm_shifts, peg_weight, peg_bias, out_grad):
    own_rows, width = tokens.shape
    windows = own_rows // CELLS
    heads = lax.axis_size("head")
    hidden = fc_in_bias.shape[0]
    piece = width // heads // 2
    own = 256 // heads // 2
    shape = jax.ShapeDtypeStruct
    place = lax.axis_index("head") * own_rows
    around = jnp.pad(lax.all_gather(tokens, "head", axis=0, tiled=True), ((HALO, HALO), (0, 0)))
    turned = jnp.concatenate([jnp.swapaxes(qkv_weight, 1, 2), proj_weight[None]], axis=0)
    at_w = lax.all_gather(turned, "head", axis=1, tiled=True)
    fc_w = jnp.stack(
        [lax.all_gather(fc, ("img", "head"), axis=0, tiled=True) for fc in (fc_in, fc_out)]
    )
    edges = (windows + 2 * MARGIN, WS, 8, width)
    out = call(
        local_kernel,
        "block",
        {
            "sides": image_sides,
            "rows": lax.dynamic_slice_in_dim(around, place, own_rows + 2 * HALO, 0),
            "og": out_grad,
            "at_w": at_w.reshape(4, heads, 2, piece, width).transpose(1, 2, 0, 3, 4),
            "fc_w": fc_w.reshape(2, hidden // 256, 2, heads, own, width).transpose(2, 1, 3, 0, 4, 5),
            "proj_bias": proj_bias[None],
            "fc_in_bias": fc_in_bias[None],
            "fc_out_bias": fc_out_bias[None],
            "gain": norm_gains,
            "shift": norm_shifts,
            "peg": peg_weight,
            "peg_bias": peg_bias[None],
        },
        {
            "output": shape((own_rows, width), BF16),
            "mixed": shape(edges, F32),
            "g_fc": shape((2, hidden // 256, heads, 2, own, width), BF16),
            "g_at": shape((2, 4, heads, piece, width), BF16),
            "small": shape((SMALL, width), F32),
        },
        dict(work_buffers(windows, heads, width, hidden), ext=pltpu.VMEM(edges, F32)),
    )
    mixed = out["mixed"]
    last, start = windows, MARGIN
    forth = lax.ppermute(mixed[last : last + MARGIN].astype(BF16), "head", [(i, i + 1) for i in range(heads - 1)])
    back = lax.ppermute(mixed[start : start + MARGIN].astype(BF16), "head", [(i + 1, i) for i in range(heads - 1)])
    own = mixed[MARGIN : MARGIN + windows]
    mixed = jnp.concatenate([forth.astype(F32), own, back.astype(F32)], axis=0)
    d_tokens = call(
        token_kernel,
        "tokens",
        {"sides": image_sides, "mixed": mixed, "peg": peg_weight},
        {"d_tokens": shape((own_rows, width), F32)},
        {name: work_buffers(windows, heads, width, hidden)[name] for name in ("info", "source")},
    )["d_tokens"]
    everywhere = ("img", "head")
    d_fc_in, d_fc_out = (
        lax.psum_scatter(g.reshape(hidden, width).astype(F32), everywhere, scatter_dimension=0, tiled=True)
        for g in out["g_fc"].transpose(3, 1, 0, 2, 4, 5)
    )
    g_at = out["g_at"].transpose(1, 2, 0, 3, 4).reshape(4, width, width).astype(F32)
    g_at = lax.psum(lax.psum_scatter(g_at, "head", scatter_dimension=1, tiled=True), "img")
    small = lax.psum(out["small"], everywhere)
    return (out["output"], d_tokens, jnp.swapaxes(g_at[:3], 1, 2), g_at[3], small[0], d_fc_in, small[1:5].reshape(-1),
            d_fc_out, small[5], small[6:8], small[8:10], small[10:19], small[19])


def on_device(tokens, image_sides, qkv_weight, proj_weight, proj_bias, fc_in, fc_in_bias, fc_out, fc_out_bias,
              norm_gains, norm_shifts, peg_weight, peg_bias, out_grad):
    own_rows, width = tokens.shape
    windows = own_rows // CELLS
    heads = lax.axis_size("head")
    hidden = fc_in_bias.shape[0]
    quads = lax.axis_size("img") // 2
    own = fc_in.shape[0]
    if quads != 4 or heads != 4 or own % 16 != 0:
        return on_any_device(tokens, image_sides, qkv_weight, proj_weight, proj_bias, fc_in, fc_in_bias, fc_out,
                             fc_out_bias, norm_gains, norm_shifts, peg_weight, peg_bias, out_grad)
    piece = width // heads // 2
    shape = jax.ShapeDtypeStruct
    inputs = {
        "sides": image_sides,
        "tokens": tokens,
        "og": out_grad,
        "qkv_w": qkv_weight,
        "proj_w": proj_weight,
        "fc_in": fc_in,
        "fc_out": fc_out,
        "proj_bias": proj_bias[None],
        "fc_in_bias": fc_in_bias[None],
        "fc_out_bias": fc_out_bias[None],
        "gain": norm_gains,
        "shift": norm_shifts,
        "peg": peg_weight,
        "peg_bias": peg_bias[None],
    }
    outputs = {
        "output": shape((own_rows, width), BF16),
        "d_tokens": shape((own_rows, width), F32),
        "d_qkv": shape(qkv_weight.shape, F32),
        "d_proj": shape(proj_weight.shape, F32),
        "d_proj_bias": shape((1, width), F32),
        "d_fc_in": shape(fc_in.shape, F32),
        "d_fc_in_bias": shape((1, hidden), F32),
        "d_fc_out": shape(fc_out.shape, F32),
        "d_fc_out_bias": shape((1, width), F32),
        "d_gains": shape(norm_gains.shape, F32),
        "d_shifts": shape(norm_shifts.shape, F32),
        "d_peg": shape(peg_weight.shape, F32),
        "d_peg_bias": shape((1, width), F32),
    }
    scratch = work_buffers(windows, heads, width, hidden)
    scratch.update({
        "rows": pltpu.VMEM((own_rows + 2 * HALO, width), BF16),
        "ext": pltpu.VMEM((windows + 2 * MARGIN, WS, 8, width), F32),
        "mixed": pltpu.VMEM((windows + 2 * MARGIN, WS, 8, width), F32),
        "edge_out": pltpu.VMEM((2, EDGE * SLOT, width), BF16),
        "edge_in": pltpu.VMEM((2, EDGE * SLOT, width), BF16),
        "at_w": pltpu.VMEM((heads, 2, 4, piece, width), BF16),
        "fc_w": pltpu.VMEM((2, quads, heads, 2, own, width), BF16),
        "g_fc": pltpu.VMEM((2, quads, heads, 2, own, width), BF16),
        "gf_one": pltpu.VMEM((quads, heads, 2, own, width), BF16),
        "gf_two": pltpu.VMEM((quads, heads, 2, own, width), BF16),
        "gf_three": pltpu.VMEM((quads - 1, heads, 2, own, width), BF16),
        "gf_four": pltpu.VMEM((heads, 2, own, width), BF16),
        "gf_five": pltpu.VMEM((heads - 1, 2, own, width), BF16),
        "g_at": pltpu.VMEM((2, 4, heads, piece, width), BF16),
        "ga_one": pltpu.VMEM((4, heads, piece, width), BF16),
        "ga_two": pltpu.VMEM((4, heads, piece, width), BF16),
        "ga_three": pltpu.VMEM((quads - 1, heads, piece, width), BF16),
        "ga_four": pltpu.VMEM((heads, piece, width), BF16),
        "ga_five": pltpu.VMEM((heads - 1, piece, width), BF16),
        "ga_all": pltpu.VMEM((4, 2, piece, width), BF16),
        "small": pltpu.VMEM((SMALL, width), F32),
        "small_plane": pltpu.VMEM((quads, 2, SMALL, width), F32),
        "small_sum": pltpu.VMEM((SMALL, width), F32),
        "small_z": pltpu.VMEM((heads, SMALL, width), F32),
        "send": pltpu.SemaphoreType.DMA((COPIES,)),
        "recv": pltpu.SemaphoreType.DMA((COPIES,)),
    })
    out = call(fused_kernel, "block", inputs, outputs, scratch, collective_id=0, has_side_effects=True)
    for name in ("d_proj_bias", "d_fc_in_bias", "d_fc_out_bias", "d_peg_bias"):
        out[name] = out[name].reshape(-1)
    return tuple(out.values())


def solution(mesh):
    rows = P(("img", "head"), None)
    placed = (rows, P("img", None), P(None, None, "head"), P("head", None), P(), rows, P(), rows, P(), P(), P(), P(), P(), rows)
    return jax.shard_map(
        on_device,
        mesh=mesh,
        in_specs=placed,
        out_specs=(rows, rows, P(None, None, "head"), P("head", None), P(), rows, P(), rows, P(), P(), P(), P(), P()),
        check_vma=False,
    )
```

```python
import functools
from types import SimpleNamespace

import jax
import jax.numpy as jnp
from jax import lax
from jax.experimental import pallas as pl
from jax.experimental.pallas import tpu as pltpu
from jax.sharding import PartitionSpec as P

F32 = jnp.float32
BF16 = jnp.bfloat16
MESH = pl.DeviceIdType.MESH

HDIM = 32
WS = 7
CELLS = WS * WS
SLOT = WS * 8
TALL = 64
MARGIN = 5
HALO = 256
EDGE = 6
OFFSET = 8
BLOCK = 8
FEED = 8
SPAN = 4
SMALL = 32
VMEM_LIMIT = 56 * 1024 * 1024


def nn(left, right):
    return lax.dot_general(left, right, (((1,), (0,)), ((), ())), preferred_element_type=F32)


def nt(left, right):
    return lax.dot_general(left, right, (((1,), (1,)), ((), ())), preferred_element_type=F32)


def tn(left, right):
    return lax.dot_general(left, right, (((0,), (0,)), ((), ())), preferred_element_type=F32)


def iota(shape, axis):
    return lax.broadcasted_iota(jnp.int32, shape, axis)


def identity(size):
    return jnp.where(iota((size, size), 0) == iota((size, size), 1), 1.0, 0.0).astype(BF16)


def scan_windows(sides_ref, info_ref, windows):
    slots = sides_ref.shape[-1]

    def clear(index, carry):
        for kind in range(3):
            info_ref[kind, index] = 0
            info_ref[kind, OFFSET + windows + index] = 0
        return carry

    lax.fori_loop(0, OFFSET, clear, 0)

    def body(window, carry):
        slot, row, col = carry
        side = jnp.where(slot < slots, sides_ref[0, jnp.minimum(slot, slots - 1)], 0)
        info_ref[0, OFFSET + window] = side
        info_ref[1, OFFSET + window] = row
        info_ref[2, OFFSET + window] = col
        end_col = col + 1 >= side
        end_row = row + 1 >= side
        next_slot = jnp.where(end_col & end_row, slot + 1, slot)
        next_row = jnp.where(end_col, jnp.where(end_row, 0, row + 1), row)
        next_col = jnp.where(end_col, 0, col + 1)
        return (next_slot, next_row, next_col)

    zero = jnp.int32(0)
    lax.fori_loop(0, windows, body, (zero, zero, zero))


def window_of(info_ref, window):
    side = info_ref[0, OFFSET + window]
    row = info_ref[1, OFFSET + window]
    col = info_ref[2, OFFSET + window]
    limit = jnp.where(side == 2, 14, jnp.where(side == 3, 18, jnp.where(side == 4, 24, 0)))
    high = jnp.minimum(limit - WS * row, WS)
    wide = jnp.minimum(limit - WS * col, WS)
    return side, row, col, high, wide


def expand(rows_ref, starts, limits):
    place = iota((SLOT, TALL), 0)
    patch_row, patch_col = place >> 3, place & 7
    wanted = WS * patch_row + patch_col - iota((SLOT, TALL), 1)
    hits, bases = [], []
    for start, (high, wide) in zip(starts, limits):
        base = (start // 16) * 16
        base = base if isinstance(base, int) else pl.multiple_of(base, 16)
        hit = (wanted == base - start) & (patch_col < wide) & (patch_row < high)
        hits.append(jnp.where(hit, 1.0, 0.0).astype(BF16))
        bases.append(base)
    return [nn(hit, rows_ref[pl.ds(base, TALL), :]) for hit, base in zip(hits, bases)]


def contract_mask(step, rows):
    first = rows * step
    window = first // CELLS
    shift = first - CELLS * window
    source = iota((rows, SPAN * SLOT), 1)
    hit = (iota((rows, SPAN * SLOT), 0) + shift == WS * (source >> 3) + (source & 7)) & (
        (source & 7) < WS
    )
    return window, jnp.where(hit, 1.0, 0.0).astype(BF16)


def near(ext_ref, place, side, row, col):
    lane_col = iota((1, 8, ext_ref.shape[-1]), 1)
    first = jnp.where(col > 0, 0, 8)
    last = jnp.where(col < side - 1, WS - 1, 8)

    def triple(window, rows):
        own = ext_ref[window, rows]
        left = pltpu.roll(ext_ref[window - 1, rows], 2, 1)
        right = pltpu.roll(ext_ref[window + 1, rows], 6, 1)
        return (
            jnp.where(lane_col == first, left, pltpu.roll(own, 1, 1)),
            own,
            jnp.where(lane_col == last, right, pltpu.roll(own, 7, 1)),
        )

    above_on = jnp.where(row > 0, 1.0, 0.0)
    below_on = jnp.where(row < side - 1, 1.0, 0.0)
    above = triple(place - side, slice(WS - 1, WS))
    middle = triple(place, slice(0, WS))
    below = triple(place + side, slice(0, 1))
    return [
        jnp.concatenate([up * above_on, mid, down * below_on], axis=0)
        for up, mid, down in zip(above, middle, below)
    ]


def valid_cells(high, wide, width):
    shape = (WS, 8, width)
    return (iota(shape, 0) < high) & (iota(shape, 1) < wide)


def fold(values):
    rows, width = values.shape
    return jnp.sum(values.reshape(rows // 8, 8, width), axis=0)


def normalize(values):
    centre = values - jnp.mean(values, axis=-1, keepdims=True)
    inverse = lax.rsqrt(jnp.mean(centre * centre, axis=-1, keepdims=True) + 1e-06)
    return centre * inverse, inverse


def normalize_back(gradient, scaled, inverse, gain):
    d_scaled = gradient * gain
    mean_one = jnp.mean(d_scaled, axis=-1, keepdims=True)
    mean_two = jnp.mean(d_scaled * scaled, axis=-1, keepdims=True)
    return inverse * (d_scaled - mean_one - scaled * mean_two)


def stack_heads(values):
    head = iota(values.shape, 1) // HDIM
    zero = jnp.zeros_like(values)
    return jnp.concatenate([jnp.where(head == g, values, zero) for g in range(128 // HDIM)], axis=0)


def pick_heads(stacked):
    head = iota((TALL, 128), 1) // HDIM
    taken = stacked[0:TALL]
    for g in range(1, 128 // HDIM):
        taken = jnp.where(head == g, stacked[TALL * g : TALL * (g + 1)], taken)
    return taken


def to_tall(rows):
    return jnp.concatenate([rows, jnp.zeros((TALL - SLOT, rows.shape[1]), F32)], axis=0).astype(
        BF16
    )


def gelu_parts(values):
    cdf = 0.5 + 0.5 * lax.erf(values * (0.5**0.5))
    density = jnp.exp(-0.5 * values * values) * 0.3989422804014327
    return values * cdf, cdf + values * density


def rows_at(index, size):
    return pl.ds(pl.multiple_of(index * size, size), size)


def take_tokens(first, r):
    def source(step, carry):
        windows = [BLOCK * step + i for i in range(BLOCK)]
        limits = [window_of(r.info, first + window)[3:] for window in windows]
        starts = [CELLS * window for window in windows]
        for window, rows in zip(windows, expand(r.tokens, starts, limits)):
            r.ext[MARGIN + window] = rows.reshape(WS, 8, -1)
        return carry

    lax.fori_loop(0, r.windows // BLOCK, source, 0)


def take_margin(first, r, rows_ref, skip, place):
    windows = list(range(MARGIN))
    limits = [window_of(r.info, first + place - MARGIN + window)[3:] for window in windows]
    starts = [skip + CELLS * window for window in windows]
    for window, rows in zip(windows, expand(rows_ref, starts, limits)):
        r.ext[place + window] = rows.reshape(WS, 8, -1)


def take_cotangent(first, r):
    def cotangent(step, carry):
        windows = [BLOCK * step + i for i in range(BLOCK)]
        limits = [window_of(r.info, first + window)[3:] for window in windows]
        starts = [CELLS * window for window in windows]
        for window, rows in zip(windows, expand(r.og, starts, limits)):
            r.dout[rows_at(window, SLOT), :] = rows
        return carry

    lax.fori_loop(0, r.windows // BLOCK, cotangent, 0)


def field_pass(first, r, start, stop):
    count = 4

    def body(step, carry):
        totals = []
        for sub in range(count):
            window = count * step + sub
            side, row, col, high, wide = window_of(r.info, first + window)
            bands = near(r.ext, window + MARGIN, side, row, col)
            total = bands[1][1 : 1 + WS] + r.peg_bias[...]
            for a in range(3):
                for b in range(3):
                    tap = 3 * a + b
                    total = total + bands[b][a : a + WS] * r.peg[tap : tap + 1, :]
            total = jnp.where(valid_cells(high, wide, total.shape[-1]), total, 0.0)
            totals.append(total.reshape(SLOT, -1))
        field = jnp.concatenate(totals, axis=0)
        scaled, inverse = normalize(field)
        place = rows_at(step, count * SLOT)
        r.field[place, :] = field
        r.scaled[place, :] = scaled
        r.inverse[place, :] = inverse
        r.normed[place, :] = (scaled * r.gain[0:1, :] + r.shift[0:1, :]).astype(BF16)
        return carry

    lax.fori_loop(start // count, stop // count, body, 0)


def parts_of(qkv, half):
    width = qkv.shape[1] // 3
    return [qkv[:, width * t + 128 * half : width * t + 128 * (half + 1)] for t in range(3)]


def attend(qkvs, limits, probs_ref, windows):
    key = iota((TALL, 256), 0)
    key_row, key_col = key >> 3, key & 7
    usable = [(key_row < high) & (key_col < wide) for high, wide in limits]
    halves = range(qkvs[0].shape[1] // 3 // 128)
    pairs = [(i, half) for i in range(len(windows)) for half in halves]
    parts = [parts_of(qkvs[i], half) for i, half in pairs]
    scores = [nt(keys, stack_heads(query)) for query, keys, _ in parts]
    scores = [jnp.where(usable[i], score, -1e30) for (i, _), score in zip(pairs, scores)]
    tops = [jnp.max(score, axis=0, keepdims=True) for score in scores]
    exponents = [jnp.exp((score - top) * HDIM**-0.5) for score, top in zip(scores, tops)]
    shares = [1.0 / jnp.sum(exponent, axis=0, keepdims=True) for exponent in exponents]
    probs = [exponent * share for exponent, share in zip(exponents, shares)]
    for (i, half), prob in zip(pairs, probs):
        probs_ref[windows[i], :, 256 * half : 256 * (half + 1)] = prob
    context = [tn(prob.astype(BF16), value) for prob, (_, _, value) in zip(probs, parts)]
    context = [pick_heads(one) for one in context]
    return [
        jnp.concatenate([one for (j, _), one in zip(pairs, context) if j == i], axis=1)
        for i in range(len(windows))
    ]


def attend_back(qkvs, d_contexts, probs_ref, windows):
    halves = range(qkvs[0].shape[1] // 3 // 128)
    pairs = [(i, half) for i in range(len(windows)) for half in halves]
    parts = [parts_of(qkvs[i], half) for i, half in pairs]
    stacks = [stack_heads(d_contexts[i][:, 128 * half : 128 * (half + 1)]) for i, half in pairs]
    probs = [probs_ref[windows[i], :, 256 * half : 256 * (half + 1)] for i, half in pairs]
    d_probs = [nt(value, stack) for (_, _, value), stack in zip(parts, stacks)]
    d_value = [nn(prob.astype(BF16), stack) for prob, stack in zip(probs, stacks)]
    inner = [jnp.sum(d * prob, axis=0, keepdims=True) for d, prob in zip(d_probs, probs)]
    d_score = [(prob * (d - one)).astype(BF16) for prob, d, one in zip(probs, d_probs, inner)]
    d_key = [nn(d, stack_heads(query)) * HDIM**-0.5 for d, (query, _, _) in zip(d_score, parts)]
    d_query = [tn(d, keys) for d, (_, keys, _) in zip(d_score, parts)]
    d_query = [pick_heads(one) * HDIM**-0.5 for one in d_query]
    return [
        jnp.concatenate(
            [one for kind in (d_query, d_key, d_value) for (j, _), one in zip(pairs, kind) if j == i],
            axis=1,
        )
        for i in range(len(windows))
    ]


def qkv_weights(r):
    halves, _, heads = r.at_w.shape[:3]
    return jnp.concatenate(
        [r.at_w[half, kind, z] for kind in range(3) for z in range(heads) for half in range(halves)], axis=0
    )


def proj_weights(r):
    halves, _, heads = r.at_w.shape[:3]
    return jnp.concatenate([r.at_w[half, 3, z] for z in range(heads) for half in range(halves)], axis=0)


def feed_weights(r, slot, kind):
    cores, _, heads = r.fc_w.shape[:3]
    return jnp.concatenate(
        [r.fc_w[core, slot, z, kind] for core in range(cores) for z in range(heads)], axis=0
    )


def attention_block(first, r, step):
    rows = BLOCK * SLOT
    place = rows_at(step, rows)
    windows = [BLOCK * step + sub for sub in range(BLOCK)]
    limits = [window_of(r.info, first + window)[3:] for window in windows]
    projected = nt(r.normed[place, :], qkv_weights(r))
    qkvs = [to_tall(projected[SLOT * sub : SLOT * (sub + 1)]) for sub in range(BLOCK)]
    for window, qkv in zip(windows, qkvs):
        r.qkv[window] = qkv
    context = attend(qkvs, limits, r.probs, windows)
    context = jnp.concatenate([one[0:SLOT] for one in context], axis=0).astype(BF16)
    r.context[place, :] = context
    hidden = r.field[place, :] + nn(context, proj_weights(r)) + r.proj_bias[...]
    scaled, inverse = normalize(hidden)
    r.scaled_two[place, :] = scaled
    r.inverse_two[place, :] = inverse
    r.normed_two[place, :] = (scaled * r.gain[1:2, :] + r.shift[1:2, :]).astype(BF16)
    r.result[place, :] = hidden + r.fc_out_bias[...]


def feed_chunk(r, slot, chunk):
    rows = FEED * SLOT
    blocks = r.windows // FEED
    w_in, w_out = feed_weights(r, slot, 0), feed_weights(r, slot, 1)
    bias = r.fc_in_bias[chunk]
    places = [slice(rows * block, rows * (block + 1)) for block in range(blocks)]

    def ahead(block):
        place = places[block]
        return nt(r.normed_two[place, :], w_in), nt(r.dout[place, :].astype(BF16), w_out)

    waiting = ahead(0)
    d_bias = jnp.zeros((8, w_in.shape[0]), F32)
    for block in range(blocks):
        pre, d_active = waiting
        place = places[block]
        if block + 1 < blocks:
            waiting = ahead(block + 1)
        active, slope = gelu_parts(pre + bias)
        active = active.astype(BF16)
        d_pre = d_active * slope
        d_bias = d_bias + fold(d_pre)
        d_pre = d_pre.astype(BF16)
        r.active[place, :] = active
        r.d_pre[place, :] = d_pre
        r.result[place, :] += nn(active, w_out)
        d_normed = nn(d_pre, w_in)
        r.d_two[place, :] = d_normed if slot == 0 else r.d_two[place, :] + d_normed
    r.bias[chunk] = d_bias
    cores, _, heads, _, own, _ = r.g_fc.shape
    d_in = tn(r.d_pre[...], r.normed_two[...]).astype(BF16)
    d_out = tn(r.active[...], r.dout[...].astype(BF16)).astype(BF16)
    for core in range(cores):
        for z in range(heads):
            place = own * (heads * core + z)
            r.g_fc[core, slot, z, 0] = d_in[place : place + own]
            r.g_fc[core, slot, z, 1] = d_out[place : place + own]


def attention_back(first, r, step):
    rows = BLOCK * SLOT
    place = rows_at(step, rows)
    windows = [BLOCK * step + sub for sub in range(BLOCK)]
    d_output = r.dout[place, :]
    scaled = r.scaled_two[place, :]
    d_normed = r.d_two[place, :]
    d_hidden = d_output + normalize_back(d_normed, scaled, r.inverse_two[place, :], r.gain[1:2, :])
    r.hidden[place, :] = d_hidden
    d_branch = d_hidden.astype(BF16)
    d_context = nt(d_branch, proj_weights(r))
    d_context = [to_tall(d_context[SLOT * sub : SLOT * (sub + 1)]) for sub in range(BLOCK)]
    r.g_proj[...] += tn(r.context[place, :], d_branch)
    r.sums[0] += fold(d_branch.astype(F32))
    r.sums[1] += fold(d_output)
    r.sums[3] += fold(d_normed * scaled)
    r.sums[5] += fold(d_normed)
    d_qkv = attend_back([r.qkv[window] for window in windows], d_context, r.probs, windows)
    d_qkv = jnp.concatenate([one[0:SLOT] for one in d_qkv], axis=0).astype(BF16)
    r.d_parts[place, :] = d_qkv
    r.g_qkv[...] += tn(d_qkv, r.normed[place, :])


def field_back(first, r, step):
    rows = BLOCK * SLOT
    place = rows_at(step, rows)
    width = r.field.shape[1]
    d_normed = nn(r.d_parts[place, :], qkv_weights(r))
    scaled = r.scaled[place, :]
    r.sums[2] += fold(d_normed * scaled)
    r.sums[4] += fold(d_normed)
    d_norm = normalize_back(d_normed, scaled, r.inverse[place, :], r.gain[0:1, :])
    d_field = r.hidden[place, :] + d_norm
    taps = [jnp.zeros((8, width), F32) for _ in range(10)]
    for sub in range(BLOCK):
        window = BLOCK * step + sub
        side, row, col, high, wide = window_of(r.info, first + window)
        own = d_field[SLOT * sub : SLOT * (sub + 1)].reshape(WS, 8, -1)
        own = jnp.where(valid_cells(high, wide, width), own, 0.0)
        r.mixed[window + MARGIN] = own
        bands = near(r.ext, window + MARGIN, side, row, col)
        for a in range(3):
            for b in range(3):
                taps[3 * a + b] = taps[3 * a + b] + jnp.sum(own * bands[b][a : a + WS], axis=0)
        taps[9] = taps[9] + jnp.sum(own, axis=0)
    for tap in range(10):
        r.sums[6 + tap] += taps[tap]


def token_pass(first, r, start, stop):
    count = 4

    def body(step, carry):
        for sub in range(count):
            window = start + count * step + sub
            side, row, col, high, wide = window_of(r.info, first + window)
            grads = near(r.mixed, window + MARGIN, side, row, col)
            total = grads[1][1 : 1 + WS]
            for a in range(3):
                for b in range(3):
                    tap = 3 * a + b
                    total = total + grads[2 - b][2 - a : 2 - a + WS] * r.peg[tap : tap + 1, :]
            total = jnp.where(valid_cells(high, wide, total.shape[-1]), total, 0.0)
            r.source[rows_at(window, SLOT), :] = total.reshape(SLOT, -1)
        return carry

    lax.fori_loop(0, (stop - start) // count, body, 0)


def shrink(padded_ref, dense_ref, exact):
    rows, count = 112, 7

    def body(step, carry):
        steps = [count * step + i for i in range(count)]
        masks = [contract_mask(one, rows) for one in steps]
        values = [
            padded_ref[pl.ds(pl.multiple_of(SLOT * window, 8), SPAN * SLOT), :] for window, _ in masks
        ]
        highs = [value.astype(BF16) for value in values]
        dense = [nn(hit, high) for (_, hit), high in zip(masks, highs)]
        if exact:
            lows = [(value - high.astype(F32)).astype(BF16) for value, high in zip(values, highs)]
            dense = [one + nn(hit, low) for one, (_, hit), low in zip(dense, masks, lows)]
        for one, result in zip(steps, dense):
            dense_ref[rows_at(one, rows), :] = result.astype(dense_ref.dtype)
        return carry

    lax.fori_loop(0, dense_ref.shape[0] // rows // count, body, 0)


def clear(r):
    for ref in (r.g_proj, r.g_qkv, r.sums):
        ref[...] = jnp.zeros_like(ref)
    tail = r.windows * SLOT
    for ref in (r.result, r.source):
        ref[tail:, :] = jnp.zeros((ref.shape[0] - tail, ref.shape[1]), F32)


def mask_result(first, r):
    def body(step, carry):
        for sub in range(BLOCK):
            window = BLOCK * step + sub
            _, _, _, high, wide = window_of(r.info, first + window)
            place = rows_at(window, SLOT)
            cells = r.result[place, :].reshape(WS, 8, -1)
            cells = jnp.where(valid_cells(high, wide, cells.shape[-1]), cells, 0.0)
            r.result[place, :] = cells.reshape(SLOT, -1)
        return carry

    lax.fori_loop(0, r.windows // BLOCK, body, 0)


def turn_attention_gradients(r):
    halves, _, heads, piece, width = r.g_at.shape
    for kind in range(4):
        rows = r.g_qkv[width * kind : width * (kind + 1), :] if kind < 3 else r.g_proj[...]
        rows = rows.astype(BF16)
        for half in range(halves):
            for z in range(heads):
                place = piece * (halves * z + half)
                r.g_at[half, kind, z] = rows[place : place + piece]


def collect_small(r):
    total = jnp.sum(r.sums[...], axis=1)
    r.small[...] = jnp.zeros_like(r.small)
    r.small[0:1, :] = total[0:1]
    r.small[1:5, :] = jnp.sum(r.bias[...], axis=1)
    r.small[5:6, :] = total[1:2]
    r.small[6:10, :] = total[2:6]
    r.small[10:20, :] = total[6:16]


def loop(start, stop, body):
    def step(index, carry):
        body(index)
        return carry

    lax.fori_loop(start, stop, step, 0)


COPIES = 55


def fused_kernel(names, *refs):
    r = SimpleNamespace(**dict(zip(names, refs)))
    r.windows = r.mixed.shape[0] - 2 * MARGIN
    blocks = r.windows // BLOCK
    own_rows = r.tokens.shape[0]
    heads = r.at_w.shape[2]
    quads = r.fc_w.shape[1]
    piece = r.at_w.shape[3]
    z, img = lax.axis_index("head"), lax.axis_index("img")
    yx, core = img // 2, img % 2
    other = 1 - core
    first = z * r.windows

    def flip(value, mask):
        low, high = value % 2, value // 2
        low = 1 - low if mask & 1 else low
        high = 1 - high if mask & 2 else high
        return 2 * high + low

    z_peer = {m: (img, flip(z, m)) for m in range(1, heads)}
    yx_peer = {m: (2 * flip(yx, m) + core, z) for m in range(1, quads)}
    sibling = (2 * yx + other, z)
    cross = {m: (2 * flip(yx, m) + other, z) for m in range(1, quads)}
    plane = [yx_peer[m] for m in yx_peer] + [sibling] + [cross[m] for m in cross]
    numbers = iter(range(COPIES))

    def copy(source, target, device):
        index = next(numbers)
        return pltpu.make_async_remote_copy(
            src_ref=source,
            dst_ref=target,
            send_sem=r.send.at[index],
            recv_sem=r.recv.at[index],
            device_id=device,
            device_id_type=MESH,
        )

    forth = copy(r.tokens.at[own_rows - HALO : own_rows], r.halo_low, (img, z + 1))
    back = copy(r.tokens.at[0:HALO], r.halo_high, (img, z - 1))
    at_own = r.at_w.at[core, yx]
    at_z = [copy(at_own.at[z], at_own.at[z], z_peer[m]) for m in z_peer]
    at_yx = [copy(at_own, at_own, yx_peer[m]) for m in yx_peer]
    at_core = copy(r.at_w.at[core], r.at_w.at[core], sibling)
    fc_own = r.fc_w.at[core, 0]
    fc_z = [copy(fc_own.at[z], fc_own.at[z], z_peer[m]) for m in z_peer]
    fc_yx = [copy(fc_own, r.fc_w.at[core, m], yx_peer[m]) for m in yx_peer]
    fc_core = [copy(r.fc_w.at[core, m], r.fc_w.at[core, m], sibling) for m in range(quads)]
    gf_core = [copy(r.g_fc.at[other, m], r.gf_one.at[m], sibling) for m in range(quads)]
    gf_yx = [copy(r.gf_two.at[m], r.gf_three.at[m - 1], yx_peer[m]) for m in yx_peer]
    gf_z = [copy(r.gf_four.at[flip(z, m)], r.gf_five.at[m - 1], z_peer[m]) for m in z_peer]
    ga_core = copy(r.g_at.at[other], r.ga_one, sibling)
    ga_yx = [copy(r.ga_two.at[flip(yx, m)], r.ga_three.at[m - 1], yx_peer[m]) for m in yx_peer]
    ga_z = [copy(r.ga_four.at[flip(z, m)], r.ga_five.at[m - 1], z_peer[m]) for m in z_peer]
    ga_plane = [copy(r.ga_all.at[yx, core], r.ga_all.at[yx, core], peer) for peer in plane]
    sm_plane = [copy(r.small, r.small_plane.at[yx, core], peer) for peer in plane]
    sm_z = [copy(r.small_sum, r.small_z.at[z], z_peer[m]) for m in z_peer]
    mix_forth = copy(r.edge_out.at[0], r.edge_in.at[0], (img, z + 1))
    mix_back = copy(r.edge_out.at[1], r.edge_in.at[1], (img, z - 1))
    has_next, has_last = z < heads - 1, z > 0

    def start(copies):
        for one in copies:
            one.start()

    def arrive(copies):
        for one in copies:
            one.wait_recv()

    def total_of(own, others):
        total = own.astype(F32)
        for index in range(others.shape[0]):
            total = total + others[index].astype(F32)
        return total

    for kind in range(4):
        rows = r.qkv_w[kind] if kind < 3 else r.proj_w[...]
        for half in range(2):
            r.at_own[kind, half] = rows[piece * half : piece * (half + 1)]
    r.at_w[core, yx, z] = r.at_own[yx, core]
    r.fc_w[core, 0, z, 0] = r.fc_in[...]
    r.fc_w[core, 0, z, 1] = r.fc_out[...]
    barrier = pltpu.get_barrier_semaphore()
    greeted = [z_peer[m] for m in z_peer] + plane
    for peer in greeted:
        pl.semaphore_signal(barrier, inc=1, device_id=peer, device_id_type=MESH)
    scan_windows(r.sides, r.info, heads * r.windows)
    pl.semaphore_wait(barrier, len(greeted))
    start(at_z)

    @pl.when(has_next)
    def _():
        forth.start()

    @pl.when(has_last)
    def _():
        back.start()

    take_cotangent(first, r)
    start(fc_z)
    clear(r)
    take_tokens(first, r)
    arrive(at_z)
    start(at_yx)
    field_pass(first, r, BLOCK, r.windows - BLOCK)
    margin = (MARGIN,) + r.ext.shape[1:]

    @pl.when(has_last)
    def _():
        forth.wait_recv()
        take_margin(first, r, r.halo_low, HALO - MARGIN * CELLS, 0)

    @pl.when(z == 0)
    def _():
        r.ext[0:MARGIN] = jnp.zeros(margin, F32)

    @pl.when(has_next)
    def _():
        back.wait_recv()
        take_margin(first, r, r.halo_high, 0, MARGIN + r.windows)

    @pl.when(z == heads - 1)
    def _():
        r.ext[MARGIN + r.windows :] = jnp.zeros(margin, F32)

    arrive(fc_z)
    start(fc_yx)
    fc_core[0].start()
    field_pass(first, r, 0, BLOCK)
    field_pass(first, r, r.windows - BLOCK, r.windows)
    arrive(at_yx)
    at_core.start()
    at_core.wait_recv()
    loop(0, 2, lambda step: attention_block(first, r, step))
    for one, two in zip(fc_yx, fc_core[1:]):
        one.wait_recv()
        two.start()
    loop(2, blocks, lambda step: attention_block(first, r, step))

    def add_cores(m):
        gf_core[m].wait_recv()
        r.gf_two[m] = (r.g_fc[core, m].astype(F32) + r.gf_one[m].astype(F32)).astype(BF16)
        if m > 0:
            gf_yx[m - 1].start()

    for m in range(quads):
        fc_core[m].wait_recv()
        feed_chunk(r, m, flip(yx, m))
        gf_core[m].start()
        if m > 0:
            add_cores(m - 1)

    def attention(start, stop):
        loop(start, stop, lambda step: attention_back(first, r, step))

    attention(0, 1)
    add_cores(quads - 1)
    attention(1, 3)
    arrive(gf_yx)
    r.gf_four[...] = total_of(r.gf_two[0], r.gf_three).astype(BF16)
    start(gf_z)
    attention(3, blocks)
    turn_attention_gradients(r)
    ga_core.start()

    def field(start, stop):
        loop(start, stop, lambda step: field_back(first, r, (step + blocks - 1) % blocks))

    field(0, 2)
    edge = EDGE * SLOT
    last = r.mixed[MARGIN + r.windows - EDGE : MARGIN + r.windows]
    r.edge_out[0] = last.reshape(edge, -1).astype(BF16)
    r.edge_out[1] = r.mixed[MARGIN : MARGIN + EDGE].reshape(edge, -1).astype(BF16)

    @pl.when(has_next)
    def _():
        mix_forth.start()

    @pl.when(has_last)
    def _():
        mix_back.start()

    ga_core.wait_recv()
    r.ga_two[...] = (r.g_at[core].astype(F32) + r.ga_one[...].astype(F32)).astype(BF16)
    start(ga_yx)
    field(2, blocks)
    collect_small(r)
    start(sm_plane)
    mask_result(first, r)
    shrink(r.result, r.output, False)
    arrive(gf_z)
    total = total_of(r.gf_four[z], r.gf_five)
    r.d_fc_in[...] = total[0]
    r.d_fc_out[...] = total[1]
    token_pass(first, r, BLOCK, r.windows - BLOCK)
    arrive(ga_yx)
    r.ga_four[...] = total_of(r.ga_two[yx], r.ga_three).astype(BF16)
    start(ga_z)
    arrive(sm_plane)
    r.small_plane[yx, core] = r.small[...]
    total = jnp.zeros(r.small.shape, F32)
    for a in range(quads):
        for b in range(2):
            total = total + r.small_plane[a, b]
    r.small_sum[...] = total
    start(sm_z)
    skip = (EDGE - MARGIN) * SLOT

    @pl.when(has_last)
    def _():
        mix_forth.wait_recv()
        r.mixed[0:MARGIN] = r.edge_in[0].astype(F32)[skip:].reshape(margin)

    @pl.when(z == 0)
    def _():
        r.mixed[0:MARGIN] = jnp.zeros(margin, F32)

    @pl.when(has_next)
    def _():
        mix_back.wait_recv()
        r.mixed[MARGIN + r.windows :] = r.edge_in[1].astype(F32)[0 : MARGIN * SLOT].reshape(margin)

    @pl.when(z == heads - 1)
    def _():
        r.mixed[MARGIN + r.windows :] = jnp.zeros(margin, F32)

    token_pass(first, r, 0, BLOCK)
    token_pass(first, r, r.windows - BLOCK, r.windows)
    arrive(ga_z)
    r.ga_all[yx, core] = total_of(r.ga_four[z], r.ga_five).astype(BF16)
    start(ga_plane)
    shrink(r.source, r.d_tokens, True)
    arrive(sm_z)
    r.small_z[z] = r.small_sum[...]
    total = jnp.zeros(r.small.shape, F32)
    for a in range(heads):
        total = total + r.small_z[a]
    r.small_out[...] = total
    arrive(ga_plane)
    for kind in range(4):
        for half in range(2):
            rows = r.ga_all[kind, half].astype(F32)
            place = slice(piece * half, piece * (half + 1))
            if kind < 3:
                r.d_qkv[kind, place, :] = rows
            else:
                r.d_proj[place, :] = rows

    sent = at_z + at_yx + [at_core] + fc_z + fc_yx + fc_core + gf_core + gf_yx + gf_z + [ga_core] + ga_yx + ga_z
    for one in sent + ga_plane + sm_plane + sm_z:
        one.wait_send()

    @pl.when(has_next)
    def _():
        forth.wait_send()
        mix_forth.wait_send()

    @pl.when(has_last)
    def _():
        back.wait_send()
        mix_back.wait_send()


def local_kernel(names, *refs):
    r = SimpleNamespace(**dict(zip(names, refs)))
    r.windows = r.mixed.shape[0] - 2 * MARGIN
    blocks = r.windows // BLOCK
    first = lax.axis_index("head") * r.windows
    scan_windows(r.sides, r.info, r.at_w.shape[2] * r.windows)
    clear(r)
    take_cotangent(first, r)
    take_tokens(first, r)
    take_margin(first, r, r.halo_low, HALO - MARGIN * CELLS, 0)
    take_margin(first, r, r.halo_high, 0, MARGIN + r.windows)
    field_pass(first, r, 0, r.windows)
    loop(0, blocks, lambda step: attention_block(first, r, step))
    for chunk in range(r.fc_w.shape[1]):
        feed_chunk(r, chunk, chunk)
    loop(0, blocks, lambda step: attention_back(first, r, step))
    loop(0, blocks, lambda step: field_back(first, r, step))
    turn_attention_gradients(r)
    collect_small(r)
    mask_result(first, r)
    shrink(r.result, r.output, False)
    for edge in (slice(0, MARGIN), slice(MARGIN + r.windows, 2 * MARGIN + r.windows)):
        r.mixed[edge] = jnp.zeros((MARGIN,) + r.mixed.shape[1:], F32)


def token_kernel(names, *refs):
    r = SimpleNamespace(**dict(zip(names, refs)))
    r.windows = r.mixed.shape[0] - 2 * MARGIN
    heads = (r.info.shape[1] - 2 * OFFSET) // r.windows
    first = lax.axis_index("head") * r.windows
    scan_windows(r.sides, r.info, heads * r.windows)
    tail = r.windows * SLOT
    r.source[tail:, :] = jnp.zeros((r.source.shape[0] - tail, r.source.shape[1]), F32)
    token_pass(first, r, 0, r.windows)
    shrink(r.source, r.d_tokens, True)


def vmem():
    return pl.BlockSpec(memory_space=pltpu.VMEM)


def smem():
    return pl.BlockSpec(memory_space=pltpu.SMEM)


def work_buffers(windows, heads, width, hidden):
    padded = windows * SLOT
    extra = (windows + SPAN) * SLOT
    return {
        "info": pltpu.SMEM((3, heads * windows + 2 * OFFSET), jnp.int32),
        "dout": pltpu.VMEM((padded, width), F32),
        "field": pltpu.VMEM((padded, width), F32),
        "scaled": pltpu.VMEM((padded, width), F32),
        "inverse": pltpu.VMEM((padded, 1), F32),
        "normed": pltpu.VMEM((padded, width), BF16),
        "qkv": pltpu.VMEM((windows, TALL, 3 * width), BF16),
        "probs": pltpu.VMEM((windows, TALL, 2 * width), F32),
        "context": pltpu.VMEM((padded, width), BF16),
        "hidden": pltpu.VMEM((padded, width), F32),
        "result": pltpu.VMEM((extra, width), F32),
        "source": pltpu.VMEM((extra, width), F32),
        "scaled_two": pltpu.VMEM((padded, width), F32),
        "inverse_two": pltpu.VMEM((padded, 1), F32),
        "normed_two": pltpu.VMEM((padded, width), BF16),
        "d_two": pltpu.VMEM((padded, width), F32),
        "active": pltpu.VMEM((padded, 256), BF16),
        "d_pre": pltpu.VMEM((padded, 256), BF16),
        "d_parts": pltpu.VMEM((padded, 3 * width), BF16),
        "g_proj": pltpu.VMEM((width, width), F32),
        "g_qkv": pltpu.VMEM((3 * width, width), F32),
        "sums": pltpu.VMEM((16, 8, width), F32),
        "bias": pltpu.VMEM((hidden // 256, 8, 256), F32),
    }


def call(kernel, name, inputs, outputs, scratch, **params):
    names = list(inputs) + list(outputs) + list(scratch)
    results = pl.pallas_call(
        functools.partial(kernel, names),
        out_shape=tuple(outputs.values()),
        in_specs=[smem()] + [vmem()] * (len(inputs) - 1),
        out_specs=(vmem(),) * len(outputs),
        scratch_shapes=list(scratch.values()),
        compiler_params=pltpu.CompilerParams(vmem_limit_bytes=VMEM_LIMIT, **params),
        name=name,
    )(*inputs.values())
    return dict(zip(outputs, results))


def on_any_device(tokens, image_sides, qkv_weight, proj_weight, proj_bias, fc_in, fc_in_bias, fc_out, fc_out_bias,
                  norm_gains, norm_shifts, peg_weight, peg_bias, out_grad):
    own_rows, width = tokens.shape
    windows = own_rows // CELLS
    heads = lax.axis_size("head")
    hidden = fc_in_bias.shape[0]
    piece = width // heads // 2
    own = 256 // heads // 2
    shape = jax.ShapeDtypeStruct
    place = lax.axis_index("head") * own_rows
    around = jnp.pad(lax.all_gather(tokens, "head", axis=0, tiled=True), ((HALO, HALO), (0, 0)))
    halo = jnp.stack(
        [lax.dynamic_slice_in_dim(around, place + shift, HALO, 0) for shift in (0, own_rows + HALO)]
    )
    turned = jnp.concatenate([jnp.swapaxes(qkv_weight, 1, 2), proj_weight[None]], axis=0)
    at_w = lax.all_gather(turned, "head", axis=1, tiled=True)
    fc_w = jnp.stack(
        [lax.all_gather(fc, ("img", "head"), axis=0, tiled=True) for fc in (fc_in, fc_out)]
    )
    edges = (windows + 2 * MARGIN, WS, 8, width)
    out = call(
        local_kernel,
        "block",
        {
            "sides": image_sides,
            "tokens": tokens,
            "halo_low": halo[0],
            "halo_high": halo[1],
            "og": out_grad,
            "at_w": at_w.reshape(4, heads, 2, piece, width).transpose(2, 0, 1, 3, 4),
            "fc_w": fc_w.reshape(2, hidden // 256, 2, heads, own, width).transpose(2, 1, 3, 0, 4, 5),
            "proj_bias": proj_bias[None],
            "fc_in_bias": fc_in_bias.reshape(-1, 1, 256),
            "fc_out_bias": fc_out_bias[None],
            "gain": norm_gains,
            "shift": norm_shifts,
            "peg": peg_weight,
            "peg_bias": peg_bias[None],
        },
        {
            "output": shape((own_rows, width), BF16),
            "mixed": shape(edges, F32),
            "g_fc": shape((2, hidden // 256, heads, 2, own, width), BF16),
            "g_at": shape((2, 4, heads, piece, width), BF16),
            "small": shape((SMALL, width), F32),
        },
        dict(work_buffers(windows, heads, width, hidden), ext=pltpu.VMEM(edges, F32)),
    )
    mixed = out["mixed"]
    last, start = windows, MARGIN
    forth = lax.ppermute(mixed[last : last + MARGIN].astype(BF16), "head", [(i, i + 1) for i in range(heads - 1)])
    back = lax.ppermute(mixed[start : start + MARGIN].astype(BF16), "head", [(i + 1, i) for i in range(heads - 1)])
    own = mixed[MARGIN : MARGIN + windows]
    mixed = jnp.concatenate([forth.astype(F32), own, back.astype(F32)], axis=0)
    d_tokens = call(
        token_kernel,
        "tokens",
        {"sides": image_sides, "mixed": mixed, "peg": peg_weight},
        {"d_tokens": shape((own_rows, width), F32)},
        {name: work_buffers(windows, heads, width, hidden)[name] for name in ("info", "source")},
    )["d_tokens"]
    everywhere = ("img", "head")
    d_fc_in, d_fc_out = (
        lax.psum_scatter(g.reshape(hidden, width).astype(F32), everywhere, scatter_dimension=0, tiled=True)
        for g in out["g_fc"].transpose(3, 1, 0, 2, 4, 5)
    )
    g_at = out["g_at"].transpose(1, 2, 0, 3, 4).reshape(4, width, width).astype(F32)
    g_at = lax.psum(lax.psum_scatter(g_at, "head", scatter_dimension=1, tiled=True), "img")
    small = lax.psum(out["small"], everywhere)
    return (out["output"], d_tokens, jnp.swapaxes(g_at[:3], 1, 2), g_at[3], small[0], d_fc_in, small[1:5].reshape(-1),
            d_fc_out, small[5], small[6:8], small[8:10], small[10:19], small[19])


def on_device(tokens, image_sides, qkv_weight, proj_weight, proj_bias, fc_in, fc_in_bias, fc_out, fc_out_bias,
              norm_gains, norm_shifts, peg_weight, peg_bias, out_grad):
    own_rows, width = tokens.shape
    windows = own_rows // CELLS
    heads = lax.axis_size("head")
    hidden = fc_in_bias.shape[0]
    quads = lax.axis_size("img") // 2
    own = fc_in.shape[0]
    if quads != 4 or heads != 4 or own % 16 != 0:
        return on_any_device(tokens, image_sides, qkv_weight, proj_weight, proj_bias, fc_in, fc_in_bias, fc_out,
                             fc_out_bias, norm_gains, norm_shifts, peg_weight, peg_bias, out_grad)
    piece = width // heads // 2
    shape = jax.ShapeDtypeStruct
    inputs = {
        "sides": image_sides,
        "tokens": tokens,
        "og": out_grad,
        "qkv_w": jnp.swapaxes(qkv_weight, 1, 2),
        "proj_w": proj_weight,
        "fc_in": fc_in,
        "fc_out": fc_out,
        "proj_bias": proj_bias[None],
        "fc_in_bias": fc_in_bias.reshape(-1, 1, 256),
        "fc_out_bias": fc_out_bias[None],
        "gain": norm_gains,
        "shift": norm_shifts,
        "peg": peg_weight,
        "peg_bias": peg_bias[None],
    }
    large = {
        "output": shape((own_rows, width), BF16),
        "d_tokens": shape((own_rows, width), F32),
        "d_qkv": shape((3, width // heads, width), F32),
        "d_proj": shape(proj_weight.shape, F32),
        "d_fc_in": shape(fc_in.shape, F32),
        "d_fc_out": shape(fc_out.shape, F32),
    }
    scratch = work_buffers(windows, heads, width, hidden)
    scratch.update({
        "halo_low": pltpu.VMEM((HALO, width), BF16),
        "halo_high": pltpu.VMEM((HALO, width), BF16),
        "ext": pltpu.VMEM((windows + 2 * MARGIN, WS, 8, width), F32),
        "mixed": pltpu.VMEM((windows + 2 * MARGIN, WS, 8, width), F32),
        "edge_out": pltpu.VMEM((2, EDGE * SLOT, width), BF16),
        "edge_in": pltpu.VMEM((2, EDGE * SLOT, width), BF16),
        "at_w": pltpu.VMEM((2, 4, heads, piece, width), BF16),
        "at_own": pltpu.VMEM((4, 2, piece, width), BF16),
        "fc_w": pltpu.VMEM((2, quads, heads, 2, own, width), BF16),
        "g_fc": pltpu.VMEM((2, quads, heads, 2, own, width), BF16),
        "gf_one": pltpu.VMEM((quads, heads, 2, own, width), BF16),
        "gf_two": pltpu.VMEM((quads, heads, 2, own, width), BF16),
        "gf_three": pltpu.VMEM((quads - 1, heads, 2, own, width), BF16),
        "gf_four": pltpu.VMEM((heads, 2, own, width), BF16),
        "gf_five": pltpu.VMEM((heads - 1, 2, own, width), BF16),
        "g_at": pltpu.VMEM((2, 4, heads, piece, width), BF16),
        "ga_one": pltpu.VMEM((4, heads, piece, width), BF16),
        "ga_two": pltpu.VMEM((4, heads, piece, width), BF16),
        "ga_three": pltpu.VMEM((quads - 1, heads, piece, width), BF16),
        "ga_four": pltpu.VMEM((heads, piece, width), BF16),
        "ga_five": pltpu.VMEM((heads - 1, piece, width), BF16),
        "ga_all": pltpu.VMEM((4, 2, piece, width), BF16),
        "small_plane": pltpu.VMEM((quads, 2, SMALL, width), F32),
        "small_sum": pltpu.VMEM((SMALL, width), F32),
        "small_z": pltpu.VMEM((heads, SMALL, width), F32),
        "small": pltpu.VMEM((SMALL, width), F32),
        "send": pltpu.SemaphoreType.DMA((COPIES,)),
        "recv": pltpu.SemaphoreType.DMA((COPIES,)),
    })
    made = call(
        fused_kernel,
        "block",
        inputs,
        dict(large, small_out=shape((SMALL, width), F32)),
        scratch,
        collective_id=0,
        has_side_effects=True,
    )
    small = {
        "d_proj_bias": shape((1, width), F32),
        "d_fc_in_bias": shape((1, hidden), F32),
        "d_fc_out_bias": shape((1, width), F32),
        "d_gains": shape(norm_gains.shape, F32),
        "d_shifts": shape(norm_shifts.shape, F32),
        "d_peg": shape(peg_weight.shape, F32),
        "d_peg_bias": shape((1, width), F32),
    }
    count = len(large)

    def hand_out(*refs):
        sources, targets = refs[: count + 1], refs[count + 1 :]
        for source, target in zip(sources[:count], targets[:count]):
            target[...] = source[...]
        row = 0
        for target in targets[count:]:
            for part in range(target.shape[1] // width):
                rows = target.shape[0]
                target[:, width * part : width * (part + 1)] = sources[count][row : row + rows, :]
                row += rows

    results = pl.pallas_call(
        hand_out,
        out_shape=tuple(large.values()) + tuple(small.values()),
        in_specs=[vmem()] * (count + 1),
        out_specs=(vmem(),) * (count + len(small)),
        compiler_params=pltpu.CompilerParams(vmem_limit_bytes=VMEM_LIMIT),
        name="hand_out",
    )(*made.values())
    out = dict(zip(list(large) + list(small), results))
    out["d_qkv"] = jnp.swapaxes(out["d_qkv"], 1, 2)
    for name in ("d_proj_bias", "d_fc_in_bias", "d_fc_out_bias", "d_peg_bias"):
        out[name] = out[name].reshape(-1)
    order = ("output", "d_tokens", "d_qkv", "d_proj", "d_proj_bias", "d_fc_in", "d_fc_in_bias", "d_fc_out", "d_fc_out_bias",
             "d_gains", "d_shifts", "d_peg", "d_peg_bias")
    return tuple(out[name] for name in order)


def solution(mesh):
    rows = P(("img", "head"), None)
    placed = (rows, P("img", None), P(None, None, "head"), P("head", None), P(), rows, P(), rows, P(), P(), P(), P(), P(), rows)
    return jax.shard_map(
        on_device,
        mesh=mesh,
        in_specs=placed,
        out_specs=(rows, rows, P(None, None, "head"), P("head", None), P(), rows, P(), rows, P(), P(), P(), P(), P()),
        check_vma=False,
    )
```

```python
import functools
from types import SimpleNamespace

import jax
import jax.numpy as jnp
from jax import lax
from jax.experimental import pallas as pl
from jax.experimental.pallas import tpu as pltpu
from jax.sharding import PartitionSpec as P

F32 = jnp.float32
BF16 = jnp.bfloat16
MESH = pl.DeviceIdType.MESH

HDIM = 32
WS = 7
CELLS = WS * WS
SLOT = WS * 8
TALL = 64
MARGIN = 5
HALO = 256
EDGE = 96
OFFSET = 8
BLOCK = 8
FEED = 8
SPAN = 4
SMALL = 24
VMEM_LIMIT = 56 * 1024 * 1024


def nn(left, right):
    return lax.dot_general(left, right, (((1,), (0,)), ((), ())), preferred_element_type=F32)


def nt(left, right):
    return lax.dot_general(left, right, (((1,), (1,)), ((), ())), preferred_element_type=F32)


def tn(left, right):
    return lax.dot_general(left, right, (((0,), (0,)), ((), ())), preferred_element_type=F32)


def iota(shape, axis):
    return lax.broadcasted_iota(jnp.int32, shape, axis)


def identity(size):
    return jnp.where(iota((size, size), 0) == iota((size, size), 1), 1.0, 0.0).astype(BF16)


def scan_windows(sides_ref, info_ref, windows):
    slots = sides_ref.shape[-1]

    def clear(index, carry):
        for kind in range(3):
            info_ref[kind, index] = 0
            info_ref[kind, OFFSET + windows + index] = 0
        return carry

    lax.fori_loop(0, OFFSET, clear, 0)

    def body(window, carry):
        slot, row, col = carry
        side = jnp.where(slot < slots, sides_ref[0, jnp.minimum(slot, slots - 1)], 0)
        info_ref[0, OFFSET + window] = side
        info_ref[1, OFFSET + window] = row
        info_ref[2, OFFSET + window] = col
        end_col = col + 1 >= side
        end_row = row + 1 >= side
        next_slot = jnp.where(end_col & end_row, slot + 1, slot)
        next_row = jnp.where(end_col, jnp.where(end_row, 0, row + 1), row)
        next_col = jnp.where(end_col, 0, col + 1)
        return (next_slot, next_row, next_col)

    zero = jnp.int32(0)
    lax.fori_loop(0, windows, body, (zero, zero, zero))


def window_of(info_ref, window):
    side = info_ref[0, OFFSET + window]
    row = info_ref[1, OFFSET + window]
    col = info_ref[2, OFFSET + window]
    limit = jnp.where(side == 2, 14, jnp.where(side == 3, 18, jnp.where(side == 4, 24, 0)))
    high = jnp.minimum(limit - WS * row, WS)
    wide = jnp.minimum(limit - WS * col, WS)
    return side, row, col, high, wide


def expand(rows_ref, starts, limits):
    place = iota((SLOT, TALL), 0)
    patch_row, patch_col = place >> 3, place & 7
    wanted = WS * patch_row + patch_col - iota((SLOT, TALL), 1)
    hits, bases = [], []
    for start, (high, wide) in zip(starts, limits):
        base = (start // 16) * 16
        base = base if isinstance(base, int) else pl.multiple_of(base, 16)
        hit = (wanted == base - start) & (patch_col < wide) & (patch_row < high)
        hits.append(jnp.where(hit, 1.0, 0.0).astype(BF16))
        bases.append(base)
    return [nn(hit, rows_ref[pl.ds(base, TALL), :]) for hit, base in zip(hits, bases)]


def contract_mask(step, rows):
    first = rows * step
    window = first // CELLS
    shift = first - CELLS * window
    source = iota((rows, SPAN * SLOT), 1)
    hit = (iota((rows, SPAN * SLOT), 0) + shift == WS * (source >> 3) + (source & 7)) & (
        (source & 7) < WS
    )
    return window, jnp.where(hit, 1.0, 0.0).astype(BF16)


def near(ext_ref, place, side, row, col):
    lane_col = iota((1, 8, ext_ref.shape[-1]), 1)
    first = jnp.where(col > 0, 0, 8)
    last = jnp.where(col < side - 1, WS - 1, 8)

    def triple(window, rows):
        own = ext_ref[window, rows]
        left = pltpu.roll(ext_ref[window - 1, rows], 2, 1)
        right = pltpu.roll(ext_ref[window + 1, rows], 6, 1)
        return (
            jnp.where(lane_col == first, left, pltpu.roll(own, 1, 1)),
            own,
            jnp.where(lane_col == last, right, pltpu.roll(own, 7, 1)),
        )

    above_on = jnp.where(row > 0, 1.0, 0.0)
    below_on = jnp.where(row < side - 1, 1.0, 0.0)
    above = triple(place - side, slice(WS - 1, WS))
    middle = triple(place, slice(0, WS))
    below = triple(place + side, slice(0, 1))
    return [
        jnp.concatenate([up * above_on, mid, down * below_on], axis=0)
        for up, mid, down in zip(above, middle, below)
    ]


def edge_of(ext_ref, full, rest, patch_row):
    width = ext_ref.shape[-1]
    tiles = [ext_ref[full].reshape(SLOT, width)] + [ext_ref[window, patch_row] for window in rest]
    rows = SLOT + 8 * len(rest)
    return jnp.concatenate(tiles + [jnp.zeros((EDGE - rows, width), F32)], axis=0).astype(BF16)


def edge_to(ext_ref, full, rest, patch_row, edge):
    edge = edge.astype(F32)
    ext_ref[full] = edge[0:SLOT].reshape(WS, 8, -1)
    for index, window in enumerate(rest):
        ext_ref[window, patch_row] = edge[SLOT + 8 * index : SLOT + 8 * (index + 1)]


def valid_cells(high, wide, width):
    shape = (WS, 8, width)
    return (iota(shape, 0) < high) & (iota(shape, 1) < wide)


def fold(values):
    rows, width = values.shape
    return jnp.sum(values.reshape(rows // 8, 8, width), axis=0)


def normalize(values):
    centre = values - jnp.mean(values, axis=-1, keepdims=True)
    inverse = lax.rsqrt(jnp.mean(centre * centre, axis=-1, keepdims=True) + 1e-06)
    return centre * inverse, inverse


def normalize_back(gradient, scaled, inverse, gain):
    d_scaled = gradient * gain
    mean_one = jnp.mean(d_scaled, axis=-1, keepdims=True)
    mean_two = jnp.mean(d_scaled * scaled, axis=-1, keepdims=True)
    return inverse * (d_scaled - mean_one - scaled * mean_two)


def stack_heads(values):
    head = iota(values.shape, 1) // HDIM
    zero = jnp.zeros_like(values)
    return jnp.concatenate([jnp.where(head == g, values, zero) for g in range(128 // HDIM)], axis=0)


def pick_heads(stacked):
    head = iota((TALL, 128), 1) // HDIM
    taken = stacked[0:TALL]
    for g in range(1, 128 // HDIM):
        taken = jnp.where(head == g, stacked[TALL * g : TALL * (g + 1)], taken)
    return taken


def to_tall(rows):
    return jnp.concatenate([rows, jnp.zeros((TALL - SLOT, rows.shape[1]), F32)], axis=0).astype(
        BF16
    )


def gelu_parts(values):
    cdf = 0.5 + 0.5 * lax.erf(values * (0.5**0.5))
    density = jnp.exp(-0.5 * values * values) * 0.3989422804014327
    return values * cdf, cdf + values * density


def rows_at(index, size):
    return pl.ds(pl.multiple_of(index * size, size), size)


def take_tokens(first, r):
    def source(step, carry):
        windows = [BLOCK * step + i for i in range(BLOCK)]
        limits = [window_of(r.info, first + window)[3:] for window in windows]
        starts = [CELLS * window for window in windows]
        for window, rows in zip(windows, expand(r.tokens, starts, limits)):
            r.ext[MARGIN + window] = rows.reshape(WS, 8, -1)
        return carry

    lax.fori_loop(0, r.windows // BLOCK, source, 0)


def take_margin(first, r, rows_ref, skip, place):
    windows = list(range(MARGIN))
    limits = [window_of(r.info, first + place - MARGIN + window)[3:] for window in windows]
    starts = [skip + CELLS * window for window in windows]
    for window, rows in zip(windows, expand(rows_ref, starts, limits)):
        r.ext[place + window] = rows.reshape(WS, 8, -1)


def take_cotangent(first, r):
    def cotangent(step, carry):
        windows = [BLOCK * step + i for i in range(BLOCK)]
        limits = [window_of(r.info, first + window)[3:] for window in windows]
        starts = [CELLS * window for window in windows]
        for window, rows in zip(windows, expand(r.og, starts, limits)):
            r.dout[rows_at(window, SLOT), :] = rows
        return carry

    lax.fori_loop(0, r.windows // BLOCK, cotangent, 0)


def field_pass(first, r, start, stop):
    count = 4

    def body(step, carry):
        totals = []
        for sub in range(count):
            window = count * step + sub
            side, row, col, high, wide = window_of(r.info, first + window)
            bands = near(r.ext, window + MARGIN, side, row, col)
            total = bands[1][1 : 1 + WS] + r.peg_bias[...]
            for a in range(3):
                for b in range(3):
                    tap = 3 * a + b
                    total = total + bands[b][a : a + WS] * r.peg[tap : tap + 1, :]
            total = jnp.where(valid_cells(high, wide, total.shape[-1]), total, 0.0)
            totals.append(total.reshape(SLOT, -1))
        field = jnp.concatenate(totals, axis=0)
        scaled, inverse = normalize(field)
        place = rows_at(step, count * SLOT)
        r.field[place, :] = field
        r.scaled[place, :] = scaled
        r.inverse[place, :] = inverse
        r.normed[place, :] = (scaled * r.gain[0:1, :] + r.shift[0:1, :]).astype(BF16)
        return carry

    lax.fori_loop(start // count, stop // count, body, 0)


def parts_of(qkv, half):
    width = qkv.shape[1] // 3
    return [qkv[:, width * t + 128 * half : width * t + 128 * (half + 1)] for t in range(3)]


def attend(qkvs, limits, probs_ref, windows):
    key = iota((TALL, 256), 0)
    key_row, key_col = key >> 3, key & 7
    usable = [(key_row < high) & (key_col < wide) for high, wide in limits]
    halves = range(qkvs[0].shape[1] // 3 // 128)
    pairs = [(i, half) for i in range(len(windows)) for half in halves]
    parts = [parts_of(qkvs[i], half) for i, half in pairs]
    scores = [nt(keys, stack_heads(query)) for query, keys, _ in parts]
    scores = [jnp.where(usable[i], score, -1e30) for (i, _), score in zip(pairs, scores)]
    tops = [jnp.max(score, axis=0, keepdims=True) for score in scores]
    exponents = [jnp.exp((score - top) * HDIM**-0.5) for score, top in zip(scores, tops)]
    shares = [1.0 / jnp.sum(exponent, axis=0, keepdims=True) for exponent in exponents]
    probs = [exponent * share for exponent, share in zip(exponents, shares)]
    for (i, half), prob in zip(pairs, probs):
        probs_ref[windows[i], :, 256 * half : 256 * (half + 1)] = prob
    context = [tn(prob.astype(BF16), value) for prob, (_, _, value) in zip(probs, parts)]
    context = [pick_heads(one) for one in context]
    return [
        jnp.concatenate([one for (j, _), one in zip(pairs, context) if j == i], axis=1)
        for i in range(len(windows))
    ]


def attend_back(qkvs, d_contexts, probs_ref, windows):
    halves = range(qkvs[0].shape[1] // 3 // 128)
    pairs = [(i, half) for i in range(len(windows)) for half in halves]
    parts = [parts_of(qkvs[i], half) for i, half in pairs]
    stacks = [stack_heads(d_contexts[i][:, 128 * half : 128 * (half + 1)]) for i, half in pairs]
    probs = [probs_ref[windows[i], :, 256 * half : 256 * (half + 1)] for i, half in pairs]
    d_probs = [nt(value, stack) for (_, _, value), stack in zip(parts, stacks)]
    d_value = [nn(prob.astype(BF16), stack) for prob, stack in zip(probs, stacks)]
    inner = [jnp.sum(d * prob, axis=0, keepdims=True) for d, prob in zip(d_probs, probs)]
    d_score = [(prob * (d - one)).astype(BF16) for prob, d, one in zip(probs, d_probs, inner)]
    d_key = [nn(d, stack_heads(query)) * HDIM**-0.5 for d, (query, _, _) in zip(d_score, parts)]
    d_query = [tn(d, keys) for d, (_, keys, _) in zip(d_score, parts)]
    d_query = [pick_heads(one) * HDIM**-0.5 for one in d_query]
    return [
        jnp.concatenate(
            [one for kind in (d_query, d_key, d_value) for (j, _), one in zip(pairs, kind) if j == i],
            axis=1,
        )
        for i in range(len(windows))
    ]


def qkv_weights(r):
    halves, heads = r.at_w.shape[:2]
    return jnp.concatenate(
        [r.at_w[half, z, kind] for kind in range(3) for z in range(heads) for half in range(halves)], axis=0
    )


def proj_weights(r):
    halves, heads = r.at_w.shape[:2]
    return jnp.concatenate([r.at_w[half, z, 3] for z in range(heads) for half in range(halves)], axis=0)


def feed_weights(r, slot, kind):
    cores, _, heads = r.fc_w.shape[:3]
    return jnp.concatenate(
        [r.fc_w[core, slot, z, kind] for core in range(cores) for z in range(heads)], axis=0
    )


def attention_block(first, r, step):
    rows = BLOCK * SLOT
    place = rows_at(step, rows)
    windows = [BLOCK * step + sub for sub in range(BLOCK)]
    limits = [window_of(r.info, first + window)[3:] for window in windows]
    projected = nt(r.normed[place, :], qkv_weights(r))
    qkvs = [to_tall(projected[SLOT * sub : SLOT * (sub + 1)]) for sub in range(BLOCK)]
    for window, qkv in zip(windows, qkvs):
        r.qkv[window] = qkv
    context = attend(qkvs, limits, r.probs, windows)
    context = jnp.concatenate([one[0:SLOT] for one in context], axis=0).astype(BF16)
    r.context[place, :] = context
    hidden = r.field[place, :] + nn(context, proj_weights(r)) + r.proj_bias[...]
    scaled, inverse = normalize(hidden)
    r.scaled_two[place, :] = scaled
    r.inverse_two[place, :] = inverse
    r.normed_two[place, :] = (scaled * r.gain[1:2, :] + r.shift[1:2, :]).astype(BF16)
    r.result[place, :] = hidden + r.fc_out_bias[...]


def feed_chunk(r, slot, chunk, keep):
    rows = FEED * SLOT
    blocks = r.windows // FEED
    w_in, w_out = feed_weights(r, slot, 0), feed_weights(r, slot, 1)
    bias = r.fc_in_bias[chunk]
    places = [slice(rows * block, rows * (block + 1)) for block in range(blocks)]

    def ahead(block):
        place = places[block]
        return nt(r.normed_two[place, :], w_in), nt(r.dout[place, :].astype(BF16), w_out)

    waiting = ahead(0)
    d_bias = jnp.zeros((8, w_in.shape[0]), F32)
    for block in range(blocks):
        pre, d_active = waiting
        place = places[block]
        if block + 1 < blocks:
            waiting = ahead(block + 1)
        active, slope = gelu_parts(pre + bias)
        active = active.astype(BF16)
        d_pre = d_active * slope
        d_bias = d_bias + fold(d_pre)
        d_pre = d_pre.astype(BF16)
        r.active[keep, place, :] = active
        r.d_pre[keep, place, :] = d_pre
        r.result[place, :] += nn(active, w_out)
        d_normed = nn(d_pre, w_in)
        r.d_two[place, :] = d_normed if slot == 0 else r.d_two[place, :] + d_normed
    r.bias[chunk] = d_bias


def feed_gradients(r, slot, keep):
    cores, _, heads, _, own, _ = r.g_fc.shape
    d_in = tn(r.d_pre[keep], r.normed_two[...]).astype(BF16)
    d_out = tn(r.active[keep], r.dout[...].astype(BF16)).astype(BF16)
    for core in range(cores):
        for z in range(heads):
            place = own * (heads * core + z)
            r.g_fc[core, slot, z, 0] = d_in[place : place + own]
            r.g_fc[core, slot, z, 1] = d_out[place : place + own]


def attention_back(first, r, step):
    rows = BLOCK * SLOT
    place = rows_at(step, rows)
    windows = [BLOCK * step + sub for sub in range(BLOCK)]
    d_output = r.dout[place, :]
    scaled = r.scaled_two[place, :]
    d_normed = r.d_two[place, :]
    d_hidden = d_output + normalize_back(d_normed, scaled, r.inverse_two[place, :], r.gain[1:2, :])
    r.hidden[place, :] = d_hidden
    d_branch = d_hidden.astype(BF16)
    d_context = nt(d_branch, proj_weights(r))
    d_context = [to_tall(d_context[SLOT * sub : SLOT * (sub + 1)]) for sub in range(BLOCK)]
    r.g_proj[...] += tn(r.context[place, :], d_branch)
    r.sums[0] += fold(d_branch.astype(F32))
    r.sums[1] += fold(d_output)
    r.sums[3] += fold(d_normed * scaled)
    r.sums[5] += fold(d_normed)
    d_qkv = attend_back([r.qkv[window] for window in windows], d_context, r.probs, windows)
    d_qkv = jnp.concatenate([one[0:SLOT] for one in d_qkv], axis=0).astype(BF16)
    r.d_parts[place, :] = d_qkv
    r.g_qkv[...] += tn(d_qkv, r.normed[place, :])


def field_back(first, r, step):
    rows = BLOCK * SLOT
    place = rows_at(step, rows)
    width = r.field.shape[1]
    d_normed = nn(r.d_parts[place, :], qkv_weights(r))
    scaled = r.scaled[place, :]
    r.sums[2] += fold(d_normed * scaled)
    r.sums[4] += fold(d_normed)
    d_norm = normalize_back(d_normed, scaled, r.inverse[place, :], r.gain[0:1, :])
    d_field = r.hidden[place, :] + d_norm
    taps = [jnp.zeros((8, width), F32) for _ in range(10)]
    for sub in range(BLOCK):
        window = BLOCK * step + sub
        side, row, col, high, wide = window_of(r.info, first + window)
        own = d_field[SLOT * sub : SLOT * (sub + 1)].reshape(WS, 8, -1)
        own = jnp.where(valid_cells(high, wide, width), own, 0.0)
        r.mixed[window + MARGIN] = own
        bands = near(r.ext, window + MARGIN, side, row, col)
        for a in range(3):
            for b in range(3):
                taps[3 * a + b] = taps[3 * a + b] + jnp.sum(own * bands[b][a : a + WS], axis=0)
        taps[9] = taps[9] + jnp.sum(own, axis=0)
    for tap in range(10):
        r.sums[6 + tap] += taps[tap]


def token_pass(first, r, start, stop):
    count = 4

    def body(step, carry):
        for sub in range(count):
            window = start + count * step + sub
            side, row, col, high, wide = window_of(r.info, first + window)
            grads = near(r.mixed, window + MARGIN, side, row, col)
            total = grads[1][1 : 1 + WS]
            for a in range(3):
                for b in range(3):
                    tap = 3 * a + b
                    total = total + grads[2 - b][2 - a : 2 - a + WS] * r.peg[tap : tap + 1, :]
            total = jnp.where(valid_cells(high, wide, total.shape[-1]), total, 0.0)
            r.source[rows_at(window, SLOT), :] = total.reshape(SLOT, -1)
        return carry

    lax.fori_loop(0, (stop - start) // count, body, 0)


def shrink(padded_ref, dense_ref, exact):
    rows, count = 112, 7

    def body(step, carry):
        steps = [count * step + i for i in range(count)]
        masks = [contract_mask(one, rows) for one in steps]
        values = [
            padded_ref[pl.ds(pl.multiple_of(SLOT * window, 8), SPAN * SLOT), :] for window, _ in masks
        ]
        highs = [value.astype(BF16) for value in values]
        dense = [nn(hit, high) for (_, hit), high in zip(masks, highs)]
        if exact:
            lows = [(value - high.astype(F32)).astype(BF16) for value, high in zip(values, highs)]
            dense = [one + nn(hit, low) for one, (_, hit), low in zip(dense, masks, lows)]
        for one, result in zip(steps, dense):
            dense_ref[rows_at(one, rows), :] = result.astype(dense_ref.dtype)
        return carry

    lax.fori_loop(0, dense_ref.shape[0] // rows // count, body, 0)


def share_buffers(r):
    r.d_two = r.field
    r.hidden = r.field
    r.source = r.result


def clear(r):
    for ref in (r.g_proj, r.g_qkv, r.sums):
        ref[...] = jnp.zeros_like(ref)
    tail = r.windows * SLOT
    r.result[tail:, :] = jnp.zeros((r.result.shape[0] - tail, r.result.shape[1]), F32)


def mask_result(first, r):
    def body(step, carry):
        for sub in range(BLOCK):
            window = BLOCK * step + sub
            _, _, _, high, wide = window_of(r.info, first + window)
            place = rows_at(window, SLOT)
            cells = r.result[place, :].reshape(WS, 8, -1)
            cells = jnp.where(valid_cells(high, wide, cells.shape[-1]), cells, 0.0)
            r.result[place, :] = cells.reshape(SLOT, -1)
        return carry

    lax.fori_loop(0, r.windows // BLOCK, body, 0)


def turn_attention_gradients(r):
    halves, _, heads, piece, width = r.g_at.shape
    for kind in range(4):
        rows = r.g_qkv[width * kind : width * (kind + 1), :] if kind < 3 else r.g_proj[...]
        rows = rows.astype(BF16)
        for half in range(halves):
            for z in range(heads):
                place = piece * (halves * z + half)
                r.g_at[half, kind, z] = rows[place : place + piece]


def collect_small(r):
    total = jnp.sum(r.sums[...], axis=1)
    r.small[...] = jnp.zeros_like(r.small)
    r.small[0:1, :] = total[0:1]
    r.small[1:5, :] = jnp.sum(r.bias[...], axis=1)
    r.small[5:6, :] = total[1:2]
    r.small[6:10, :] = total[2:6]
    r.small[10:20, :] = total[6:16]


def loop(start, stop, body):
    def step(index, carry):
        body(index)
        return carry

    lax.fori_loop(start, stop, step, 0)


COPIES = 65
FEED_ORDER = (0, 3, 1, 2)
FETCHED = ("sides", "qkv_w", "proj_w", "og", "tokens", "fc_in", "fc_out", "proj_bias", "fc_in_bias", "fc_out_bias", "gain", "shift",
           "peg", "peg_bias")


def fused_kernel(names, *refs):
    r = SimpleNamespace(**dict(zip(names, refs)))
    r.windows = r.mixed.shape[0] - 2 * MARGIN
    share_buffers(r)
    blocks = r.windows // BLOCK
    own_rows = r.tokens.shape[0]
    heads = r.at_w.shape[1]
    quads = r.fc_w.shape[1]
    piece = r.at_w.shape[3]
    z, img = lax.axis_index("head"), lax.axis_index("img")
    yx, core = img // 2, img % 2
    other = 1 - core
    first = z * r.windows

    def flip(value, mask):
        low, high = value % 2, value // 2
        low = 1 - low if mask & 1 else low
        high = 1 - high if mask & 2 else high
        return 2 * high + low

    z_peer = {m: (img, flip(z, m)) for m in range(1, heads)}
    yx_peer = {m: (2 * flip(yx, m) + core, z) for m in range(1, quads)}
    sibling = (2 * yx + other, z)
    cross = {m: (2 * flip(yx, m) + other, z) for m in range(1, quads)}
    plane = [yx_peer[m] for m in yx_peer] + [sibling] + [cross[m] for m in cross]
    numbers = iter(range(COPIES))

    def copy(source, target, device):
        index = next(numbers)
        return pltpu.make_async_remote_copy(
            src_ref=source,
            dst_ref=target,
            send_sem=r.send.at[index],
            recv_sem=r.recv.at[index],
            device_id=device,
            device_id_type=MESH,
        )

    forth = copy(r.tok_last, r.tok_above, (img, z + 1))
    back = copy(r.tok_first, r.tok_below, (img, z - 1))
    at_z = [copy(r.at_w.at[core, z, yx], r.at_w.at[core, z, yx], z_peer[m]) for m in z_peer]
    at_yx = [
        [copy(r.at_w.at[core, flip(z, m), yx], r.at_w.at[core, flip(z, m), yx], yx_peer[n]) for n in yx_peer]
        for m in z_peer
    ]
    at_core = [copy(r.at_w.at[core, flip(z, m)], r.at_w.at[core, flip(z, m)], sibling) for m in z_peer]
    fc_own = r.fc_w.at[core, 0]
    fc_z = [copy(fc_own.at[z], fc_own.at[z], z_peer[m]) for m in z_peer]
    fc_yx = [copy(fc_own, r.fc_w.at[core, m], yx_peer[m]) for m in yx_peer]
    fc_core = [copy(r.fc_w.at[core, m], r.fc_w.at[core, m], sibling) for m in range(quads)]
    gf_core = [copy(r.g_fc.at[other, m], r.gf_one.at[m], sibling) for m in range(quads)]
    gf_yx = [copy(r.gf_two.at[m], r.gf_three.at[m - 1], yx_peer[m]) for m in yx_peer]
    gf_z = [copy(r.gf_four.at[flip(z, m)], r.gf_five.at[m - 1], z_peer[m]) for m in z_peer]
    ga_core = copy(r.g_at.at[other], r.ga_one, sibling)
    ga_yx = [copy(r.ga_two.at[flip(yx, m)], r.ga_three.at[m - 1], yx_peer[m]) for m in yx_peer]
    ga_z = [copy(r.ga_four.at[flip(z, m)], r.ga_five.at[m - 1], z_peer[m]) for m in z_peer]
    ga_plane = [copy(r.ga_all.at[yx, core], r.ga_all.at[yx, core], peer) for peer in plane]
    sm_plane = [copy(r.small, r.small_plane.at[yx, core], peer) for peer in plane]
    sm_z = [copy(r.small_sum, r.small_z.at[z], z_peer[m]) for m in z_peer]
    mix_forth = copy(r.mix_last, r.mix_above, (img, z + 1))
    mix_back = copy(r.mix_first, r.mix_below, (img, z - 1))
    has_next, has_last = z < heads - 1, z > 0

    def start(copies):
        for one in copies:
            one.start()

    def arrive(copies):
        for one in copies:
            one.wait_recv()

    def total_of(own, others):
        total = own.astype(F32)
        for index in range(others.shape[0]):
            total = total + others[index].astype(F32)
        return total

    barrier = pltpu.get_barrier_semaphore()
    greeted = [z_peer[m] for m in z_peer] + plane
    for peer in greeted:
        pl.semaphore_signal(barrier, inc=1, device_id=peer, device_id_type=MESH)
    fetched = {}
    targets = {"qkv_w": r.at_own.at[0:3], "proj_w": r.at_own.at[3], "fc_in": r.fc_w.at[core, 0, z, 0], "fc_out": r.fc_w.at[core, 0, z, 1]}
    for index, name in enumerate(FETCHED):
        source = getattr(r, "far_" + name)
        target = targets[name] if name in targets else getattr(r, name)
        fetched[name] = pltpu.make_async_copy(source, target, r.local.at[index])
        fetched[name].start()
    fetched["sides"].wait()
    scan_windows(r.sides, r.info, heads * r.windows)
    fetched["qkv_w"].wait()
    fetched["proj_w"].wait()
    for kind in range(4):
        for half in range(2):
            r.at_w[half, z, kind] = r.at_own[kind, half]
    pl.semaphore_wait(barrier, len(greeted))
    start(at_z)
    fetched["tokens"].wait()
    take_tokens(first, r)
    margin = (MARGIN,) + r.ext.shape[1:]
    end = MARGIN + r.windows
    above, below = (MARGIN - 1, range(MARGIN - 1), WS - 1), (end, range(end + 1, end + MARGIN), 0)
    last, foremost = (end - 1, range(end - MARGIN, end - 1), WS - 1), (MARGIN, range(MARGIN + 1, 2 * MARGIN), 0)
    r.tok_last[...] = edge_of(r.ext, *last)
    r.tok_first[...] = edge_of(r.ext, *foremost)

    @pl.when(has_next)
    def _():
        forth.start()

    @pl.when(has_last)
    def _():
        back.start()

    fetched["og"].wait()
    take_cotangent(first, r)
    for name in FETCHED:
        if name not in ("sides", "tokens", "og", "qkv_w", "proj_w"):
            fetched[name].wait()
    for one, many in zip(at_z, at_yx):
        one.wait_recv()
        start(many)
    start(fc_z)
    clear(r)
    field_pass(first, r, BLOCK, r.windows - BLOCK)
    for many, one in zip(at_yx, at_core):
        arrive(many)
        one.start()

    def margins(ext_ref, forth, back, from_above, from_below):
        @pl.when(has_last)
        def _():
            forth.wait_recv()
            edge_to(ext_ref, *above, from_above[...])

        @pl.when(z == 0)
        def _():
            ext_ref[0:MARGIN] = jnp.zeros(margin, F32)

        @pl.when(has_next)
        def _():
            back.wait_recv()
            edge_to(ext_ref, *below, from_below[...])

        @pl.when(z == heads - 1)
        def _():
            ext_ref[end:] = jnp.zeros(margin, F32)

    margins(r.ext, forth, back, r.tok_above, r.tok_below)
    arrive(fc_z)
    start([fc_yx[m - 1] for m in FEED_ORDER[1:]])
    fc_core[0].start()
    field_pass(first, r, 0, BLOCK)
    field_pass(first, r, r.windows - BLOCK, r.windows)
    arrive(at_core)
    loop(0, 2, lambda step: attention_block(first, r, step))
    for one, two in zip(fc_yx, fc_core[1:]):
        one.wait_recv()
        two.start()
    loop(2, blocks, lambda step: attention_block(first, r, step))

    def add_cores(m):
        gf_core[m].wait_recv()
        r.gf_two[m] = (r.g_fc[core, m].astype(F32) + r.gf_one[m].astype(F32)).astype(BF16)
        if m > 0:
            gf_yx[m - 1].start()

    sent_slot = None
    for m in FEED_ORDER:
        fc_core[m].wait_recv()
        feed_chunk(r, m, flip(yx, m), min(m, 1))
        if m > 0:
            feed_gradients(r, m, 1)
            gf_core[m].start()
            if sent_slot is not None:
                add_cores(sent_slot)
            sent_slot = m

    def attention(start, stop):
        loop(start, stop, lambda step: attention_back(first, r, step))

    attention(0, 1)
    add_cores(sent_slot)
    attention(1, blocks)
    turn_attention_gradients(r)
    ga_core.start()

    def field(start, stop):
        loop(start, stop, lambda step: field_back(first, r, (step + blocks - 1) % blocks))

    feed_gradients(r, 0, 0)
    gf_core[0].start()
    ga_core.wait_recv()
    r.ga_two[...] = (r.g_at[core].astype(F32) + r.ga_one[...].astype(F32)).astype(BF16)
    start(ga_yx)
    field(0, 2)
    r.mix_last[...] = edge_of(r.mixed, *last)
    r.mix_first[...] = edge_of(r.mixed, *foremost)

    @pl.when(has_next)
    def _():
        mix_forth.start()

    @pl.when(has_last)
    def _():
        mix_back.start()

    add_cores(0)
    arrive(gf_yx)
    r.gf_four[...] = total_of(r.gf_two[0], r.gf_three).astype(BF16)
    start(gf_z)
    field(2, blocks)
    collect_small(r)
    arrive(ga_yx)
    r.ga_four[...] = total_of(r.ga_two[yx], r.ga_three).astype(BF16)
    start(ga_z)
    start(sm_plane)
    mask_result(first, r)
    shrink(r.result, r.output, False)
    token_pass(first, r, BLOCK, r.windows - BLOCK)
    arrive(ga_z)
    r.ga_all[yx, core] = total_of(r.ga_four[z], r.ga_five).astype(BF16)
    start(ga_plane)
    arrive(sm_plane)
    r.small_plane[yx, core] = r.small[...]
    total = jnp.zeros(r.small.shape, F32)
    for a in range(quads):
        for b in range(2):
            total = total + r.small_plane[a, b]
    r.small_sum[...] = total
    start(sm_z)
    margins(r.mixed, mix_forth, mix_back, r.mix_above, r.mix_below)
    token_pass(first, r, 0, BLOCK)
    token_pass(first, r, r.windows - BLOCK, r.windows)
    shrink(r.source, r.d_tokens, True)
    arrive(gf_z)
    total = total_of(r.gf_four[z], r.gf_five)
    r.d_fc_in[...] = total[0]
    r.d_fc_out[...] = total[1]
    arrive(sm_z)
    r.small_z[z] = r.small_sum[...]
    total = jnp.zeros(r.small.shape, F32)
    for a in range(heads):
        total = total + r.small_z[a]
    r.small_out[...] = total
    arrive(ga_plane)
    for kind in range(4):
        for half in range(2):
            rows = r.ga_all[kind, half].astype(F32)
            place = slice(piece * half, piece * (half + 1))
            if kind < 3:
                r.d_qkv[kind, place, :] = rows
            else:
                r.d_proj[place, :] = rows

    sent = at_z + sum(at_yx, []) + at_core + fc_z + fc_yx + fc_core + gf_core + gf_yx + gf_z + [ga_core] + ga_yx + ga_z
    for one in sent + ga_plane + sm_plane + sm_z:
        one.wait_send()

    @pl.when(has_next)
    def _():
        forth.wait_send()
        mix_forth.wait_send()

    @pl.when(has_last)
    def _():
        back.wait_send()
        mix_back.wait_send()


def local_kernel(names, *refs):
    r = SimpleNamespace(**dict(zip(names, refs)))
    r.windows = r.mixed.shape[0] - 2 * MARGIN
    share_buffers(r)
    blocks = r.windows // BLOCK
    first = lax.axis_index("head") * r.windows
    scan_windows(r.sides, r.info, r.at_w.shape[1] * r.windows)
    clear(r)
    take_cotangent(first, r)
    take_tokens(first, r)
    take_margin(first, r, r.halo_low, HALO - MARGIN * CELLS, 0)
    take_margin(first, r, r.halo_high, 0, MARGIN + r.windows)
    field_pass(first, r, 0, r.windows)
    loop(0, blocks, lambda step: attention_block(first, r, step))
    for chunk in range(r.fc_w.shape[1]):
        feed_chunk(r, chunk, chunk, 0)
        feed_gradients(r, chunk, 0)
    loop(0, blocks, lambda step: attention_back(first, r, step))
    loop(0, blocks, lambda step: field_back(first, r, step))
    turn_attention_gradients(r)
    collect_small(r)
    mask_result(first, r)
    shrink(r.result, r.output, False)
    for edge in (slice(0, MARGIN), slice(MARGIN + r.windows, 2 * MARGIN + r.windows)):
        r.mixed[edge] = jnp.zeros((MARGIN,) + r.mixed.shape[1:], F32)


def token_kernel(names, *refs):
    r = SimpleNamespace(**dict(zip(names, refs)))
    r.windows = r.mixed.shape[0] - 2 * MARGIN
    heads = (r.info.shape[1] - 2 * OFFSET) // r.windows
    first = lax.axis_index("head") * r.windows
    scan_windows(r.sides, r.info, heads * r.windows)
    tail = r.windows * SLOT
    r.source[tail:, :] = jnp.zeros((r.source.shape[0] - tail, r.source.shape[1]), F32)
    token_pass(first, r, 0, r.windows)
    shrink(r.source, r.d_tokens, True)


def vmem():
    return pl.BlockSpec(memory_space=pltpu.VMEM)


def smem():
    return pl.BlockSpec(memory_space=pltpu.SMEM)


def work_buffers(windows, heads, width, hidden):
    padded = windows * SLOT
    extra = (windows + SPAN) * SLOT
    return {
        "info": pltpu.SMEM((3, heads * windows + 2 * OFFSET), jnp.int32),
        "dout": pltpu.VMEM((padded, width), F32),
        "field": pltpu.VMEM((padded, width), F32),
        "scaled": pltpu.VMEM((padded, width), F32),
        "inverse": pltpu.VMEM((padded, 1), F32),
        "normed": pltpu.VMEM((padded, width), BF16),
        "qkv": pltpu.VMEM((windows, TALL, 3 * width), BF16),
        "probs": pltpu.VMEM((windows, TALL, 2 * width), F32),
        "context": pltpu.VMEM((padded, width), BF16),
        "result": pltpu.VMEM((extra, width), F32),
        "scaled_two": pltpu.VMEM((padded, width), F32),
        "inverse_two": pltpu.VMEM((padded, 1), F32),
        "normed_two": pltpu.VMEM((padded, width), BF16),
        "active": pltpu.VMEM((2, padded, 256), BF16),
        "d_pre": pltpu.VMEM((2, padded, 256), BF16),
        "d_parts": pltpu.VMEM((padded, 3 * width), BF16),
        "g_proj": pltpu.VMEM((width, width), F32),
        "g_qkv": pltpu.VMEM((3 * width, width), F32),
        "sums": pltpu.VMEM((16, 8, width), F32),
        "bias": pltpu.VMEM((hidden // 256, 8, 256), F32),
    }


def call(kernel, name, inputs, outputs, scratch, specs=None, **params):
    names = list(inputs) + list(outputs) + list(scratch)
    results = pl.pallas_call(
        functools.partial(kernel, names),
        out_shape=tuple(outputs.values()),
        in_specs=specs or [smem()] + [vmem()] * (len(inputs) - 1),
        out_specs=(vmem(),) * len(outputs),
        scratch_shapes=list(scratch.values()),
        compiler_params=pltpu.CompilerParams(vmem_limit_bytes=VMEM_LIMIT, **params),
        name=name,
    )(*inputs.values())
    return dict(zip(outputs, results))


def on_any_device(tokens, image_sides, qkv_weight, proj_weight, proj_bias, fc_in, fc_in_bias, fc_out, fc_out_bias,
                  norm_gains, norm_shifts, peg_weight, peg_bias, out_grad):
    own_rows, width = tokens.shape
    windows = own_rows // CELLS
    heads = lax.axis_size("head")
    hidden = fc_in_bias.shape[0]
    piece = width // heads // 2
    own = 256 // heads // 2
    shape = jax.ShapeDtypeStruct
    place = lax.axis_index("head") * own_rows
    around = jnp.pad(lax.all_gather(tokens, "head", axis=0, tiled=True), ((HALO, HALO), (0, 0)))
    halo = jnp.stack(
        [lax.dynamic_slice_in_dim(around, place + shift, HALO, 0) for shift in (0, own_rows + HALO)]
    )
    turned = jnp.concatenate([jnp.swapaxes(qkv_weight, 1, 2), proj_weight[None]], axis=0)
    at_w = lax.all_gather(turned, "head", axis=1, tiled=True)
    fc_w = jnp.stack(
        [lax.all_gather(fc, ("img", "head"), axis=0, tiled=True) for fc in (fc_in, fc_out)]
    )
    edges = (windows + 2 * MARGIN, WS, 8, width)
    out = call(
        local_kernel,
        "block",
        {
            "sides": image_sides,
            "tokens": tokens,
            "halo_low": halo[0],
            "halo_high": halo[1],
            "og": out_grad,
            "at_w": at_w.reshape(4, heads, 2, piece, width).transpose(2, 1, 0, 3, 4),
            "fc_w": fc_w.reshape(2, hidden // 256, 2, heads, own, width).transpose(2, 1, 3, 0, 4, 5),
            "proj_bias": proj_bias[None],
            "fc_in_bias": fc_in_bias.reshape(-1, 1, 256),
            "fc_out_bias": fc_out_bias[None],
            "gain": norm_gains,
            "shift": norm_shifts,
            "peg": peg_weight,
            "peg_bias": peg_bias[None],
        },
        {
            "output": shape((own_rows, width), BF16),
            "mixed": shape(edges, F32),
            "g_fc": shape((2, hidden // 256, heads, 2, own, width), BF16),
            "g_at": shape((2, 4, heads, piece, width), BF16),
            "small": shape((SMALL, width), F32),
        },
        dict(work_buffers(windows, heads, width, hidden), ext=pltpu.VMEM(edges, F32)),
    )
    mixed = out["mixed"]
    last, start = windows, MARGIN
    forth = lax.ppermute(mixed[last : last + MARGIN].astype(BF16), "head", [(i, i + 1) for i in range(heads - 1)])
    back = lax.ppermute(mixed[start : start + MARGIN].astype(BF16), "head", [(i + 1, i) for i in range(heads - 1)])
    own = mixed[MARGIN : MARGIN + windows]
    mixed = jnp.concatenate([forth.astype(F32), own, back.astype(F32)], axis=0)
    buffers = work_buffers(windows, heads, width, hidden)
    d_tokens = call(
        token_kernel,
        "tokens",
        {"sides": image_sides, "mixed": mixed, "peg": peg_weight},
        {"d_tokens": shape((own_rows, width), F32)},
        {"info": buffers["info"], "source": buffers["result"]},
    )["d_tokens"]
    everywhere = ("img", "head")
    d_fc_in, d_fc_out = (
        lax.psum_scatter(g.reshape(hidden, width).astype(F32), everywhere, scatter_dimension=0, tiled=True)
        for g in out["g_fc"].transpose(3, 1, 0, 2, 4, 5)
    )
    g_at = out["g_at"].transpose(1, 2, 0, 3, 4).reshape(4, width, width).astype(F32)
    g_at = lax.psum(lax.psum_scatter(g_at, "head", scatter_dimension=1, tiled=True), "img")
    small = lax.psum(out["small"], everywhere)
    return (out["output"], d_tokens, jnp.swapaxes(g_at[:3], 1, 2), g_at[3], small[0], d_fc_in, small[1:5].reshape(-1),
            d_fc_out, small[5], small[6:8], small[8:10], small[10:19], small[19])


def on_device(tokens, image_sides, qkv_weight, proj_weight, proj_bias, fc_in, fc_in_bias, fc_out, fc_out_bias,
              norm_gains, norm_shifts, peg_weight, peg_bias, out_grad):
    own_rows, width = tokens.shape
    windows = own_rows // CELLS
    heads = lax.axis_size("head")
    hidden = fc_in_bias.shape[0]
    quads = lax.axis_size("img") // 2
    own = fc_in.shape[0]
    if quads != 4 or heads != 4 or own % 16 != 0:
        return on_any_device(tokens, image_sides, qkv_weight, proj_weight, proj_bias, fc_in, fc_in_bias, fc_out,
                             fc_out_bias, norm_gains, norm_shifts, peg_weight, peg_bias, out_grad)
    piece = width // heads // 2
    shape = jax.ShapeDtypeStruct
    inputs = {
        "sides": image_sides,
        "tokens": tokens,
        "og": out_grad,
        "qkv_w": jnp.swapaxes(qkv_weight, 1, 2).reshape(3, 2, piece, width),
        "proj_w": proj_weight.reshape(2, piece, width),
        "fc_in": fc_in,
        "fc_out": fc_out,
        "proj_bias": proj_bias[None],
        "fc_in_bias": fc_in_bias.reshape(-1, 1, 256),
        "fc_out_bias": fc_out_bias[None],
        "gain": norm_gains,
        "shift": norm_shifts,
        "peg": peg_weight,
        "peg_bias": peg_bias[None],
    }
    large = {
        "output": shape((own_rows, width), BF16),
        "d_tokens": shape((own_rows, width), F32),
        "d_qkv": shape((3, width // heads, width), F32),
        "d_proj": shape(proj_weight.shape, F32),
        "d_fc_in": shape(fc_in.shape, F32),
        "d_fc_out": shape(fc_out.shape, F32),
    }
    scratch = work_buffers(windows, heads, width, hidden)
    scratch["sides"] = pltpu.SMEM(image_sides.shape, jnp.int32)
    for kind in ("tok", "mix"):
        for place in ("last", "first", "above", "below"):
            scratch[kind + "_" + place] = pltpu.VMEM((EDGE, width), BF16)
    for name in FETCHED:
        if name not in ("sides", "qkv_w", "proj_w", "fc_in", "fc_out"):
            scratch[name] = pltpu.VMEM(inputs[name].shape, inputs[name].dtype)
    scratch.update({
        "ext": pltpu.VMEM((windows + 2 * MARGIN, WS, 8, width), F32),
        "mixed": pltpu.VMEM((windows + 2 * MARGIN, WS, 8, width), F32),
        "at_w": pltpu.VMEM((2, heads, 4, piece, width), BF16),
        "at_own": pltpu.VMEM((4, 2, piece, width), BF16),
        "fc_w": pltpu.VMEM((2, quads, heads, 2, own, width), BF16),
        "g_fc": pltpu.VMEM((2, quads, heads, 2, own, width), BF16),
        "gf_one": pltpu.VMEM((quads, heads, 2, own, width), BF16),
        "gf_two": pltpu.VMEM((quads, heads, 2, own, width), BF16),
        "gf_three": pltpu.VMEM((quads - 1, heads, 2, own, width), BF16),
        "gf_four": pltpu.VMEM((heads, 2, own, width), BF16),
        "gf_five": pltpu.VMEM((heads - 1, 2, own, width), BF16),
        "g_at": pltpu.VMEM((2, 4, heads, piece, width), BF16),
        "ga_one": pltpu.VMEM((4, heads, piece, width), BF16),
        "ga_two": pltpu.VMEM((4, heads, piece, width), BF16),
        "ga_three": pltpu.VMEM((quads - 1, heads, piece, width), BF16),
        "ga_four": pltpu.VMEM((heads, piece, width), BF16),
        "ga_five": pltpu.VMEM((heads - 1, piece, width), BF16),
        "ga_all": pltpu.VMEM((4, 2, piece, width), BF16),
        "small_plane": pltpu.VMEM((quads, 2, SMALL, width), F32),
        "small_sum": pltpu.VMEM((SMALL, width), F32),
        "small_z": pltpu.VMEM((heads, SMALL, width), F32),
        "small": pltpu.VMEM((SMALL, width), F32),
        "local": pltpu.SemaphoreType.DMA((len(FETCHED),)),
        "send": pltpu.SemaphoreType.DMA((COPIES,)),
        "recv": pltpu.SemaphoreType.DMA((COPIES,)),
    })
    made = call(
        fused_kernel,
        "block",
        {"far_" + name: inputs[name] for name in FETCHED},
        dict(large, small_out=shape((SMALL, width), F32)),
        scratch,
        [pl.BlockSpec(memory_space=pltpu.HBM)] * len(FETCHED),
        collective_id=0,
        has_side_effects=True,
    )
    small = {
        "d_proj_bias": shape((1, width), F32),
        "d_fc_in_bias": shape((1, hidden), F32),
        "d_fc_out_bias": shape((1, width), F32),
        "d_gains": shape(norm_gains.shape, F32),
        "d_shifts": shape(norm_shifts.shape, F32),
        "d_peg": shape(peg_weight.shape, F32),
        "d_peg_bias": shape((1, width), F32),
    }
    count = len(large)

    def hand_out(*refs):
        sources, targets = refs[: count + 1], refs[count + 1 :]
        for source, target in zip(sources[:count], targets[:count]):
            target[...] = source[...]
        row = 0
        for target in targets[count:]:
            for part in range(target.shape[1] // width):
                rows = target.shape[0]
                target[:, width * part : width * (part + 1)] = sources[count][row : row + rows, :]
                row += rows

    results = pl.pallas_call(
        hand_out,
        out_shape=tuple(large.values()) + tuple(small.values()),
        in_specs=[vmem()] * (count + 1),
        out_specs=(vmem(),) * (count + len(small)),
        compiler_params=pltpu.CompilerParams(vmem_limit_bytes=VMEM_LIMIT),
        name="hand_out",
    )(*made.values())
    out = dict(zip(list(large) + list(small), results))
    out["d_qkv"] = jnp.swapaxes(out["d_qkv"], 1, 2)
    for name in ("d_proj_bias", "d_fc_in_bias", "d_fc_out_bias", "d_peg_bias"):
        out[name] = out[name].reshape(-1)
    order = ("output", "d_tokens", "d_qkv", "d_proj", "d_proj_bias", "d_fc_in", "d_fc_in_bias", "d_fc_out", "d_fc_out_bias",
             "d_gains", "d_shifts", "d_peg", "d_peg_bias")
    return tuple(out[name] for name in order)


def solution(mesh):
    rows = P(("img", "head"), None)
    placed = (rows, P("img", None), P(None, None, "head"), P("head", None), P(), rows, P(), rows, P(), P(), P(), P(), P(), rows)
    return jax.shard_map(
        on_device,
        mesh=mesh,
        in_specs=placed,
        out_specs=(rows, rows, P(None, None, "head"), P("head", None), P(), rows, P(), rows, P(), P(), P(), P(), P()),
        check_vma=False,
    )
```

```python
import functools
from types import SimpleNamespace

import jax
import jax.numpy as jnp
from jax import lax
from jax.experimental import pallas as pl
from jax.experimental.pallas import tpu as pltpu
from jax.sharding import PartitionSpec as P

F32 = jnp.float32
BF16 = jnp.bfloat16
MESH = pl.DeviceIdType.MESH

HDIM = 32
WS = 7
CELLS = WS * WS
SLOT = WS * 8
TALL = 64
MARGIN = 5
HALO = 256
EDGE = 96
OFFSET = 8
BLOCK = 8
FEED = 16
ATTEND = 16
SPAN = 4
SMALL = 24
VMEM_LIMIT = 56 * 1024 * 1024


def nn(left, right):
    return lax.dot_general(left, right, (((1,), (0,)), ((), ())), preferred_element_type=F32)


def nt(left, right):
    return lax.dot_general(left, right, (((1,), (1,)), ((), ())), preferred_element_type=F32)


def tn(left, right):
    return lax.dot_general(left, right, (((0,), (0,)), ((), ())), preferred_element_type=F32)


def iota(shape, axis):
    return lax.broadcasted_iota(jnp.int32, shape, axis)


def identity(size):
    return jnp.where(iota((size, size), 0) == iota((size, size), 1), 1.0, 0.0).astype(BF16)


def scan_windows(sides_ref, info_ref, windows):
    slots = sides_ref.shape[-1]

    def clear(index, carry):
        for kind in range(3):
            info_ref[kind, index] = 0
            info_ref[kind, OFFSET + windows + index] = 0
        return carry

    lax.fori_loop(0, OFFSET, clear, 0)

    def body(window, carry):
        slot, row, col = carry
        side = jnp.where(slot < slots, sides_ref[0, jnp.minimum(slot, slots - 1)], 0)
        info_ref[0, OFFSET + window] = side
        info_ref[1, OFFSET + window] = row
        info_ref[2, OFFSET + window] = col
        end_col = col + 1 >= side
        end_row = row + 1 >= side
        next_slot = jnp.where(end_col & end_row, slot + 1, slot)
        next_row = jnp.where(end_col, jnp.where(end_row, 0, row + 1), row)
        next_col = jnp.where(end_col, 0, col + 1)
        return (next_slot, next_row, next_col)

    zero = jnp.int32(0)
    lax.fori_loop(0, windows, body, (zero, zero, zero))


def window_of(info_ref, window):
    side = info_ref[0, OFFSET + window]
    row = info_ref[1, OFFSET + window]
    col = info_ref[2, OFFSET + window]
    limit = jnp.where(side == 2, 14, jnp.where(side == 3, 18, jnp.where(side == 4, 24, 0)))
    high = jnp.minimum(limit - WS * row, WS)
    wide = jnp.minimum(limit - WS * col, WS)
    return side, row, col, high, wide


def expand(rows_ref, starts, limits):
    place = iota((SLOT, TALL), 0)
    patch_row, patch_col = place >> 3, place & 7
    wanted = WS * patch_row + patch_col - iota((SLOT, TALL), 1)
    hits, bases = [], []
    for start, (high, wide) in zip(starts, limits):
        base = (start // 16) * 16
        base = base if isinstance(base, int) else pl.multiple_of(base, 16)
        hit = (wanted == base - start) & (patch_col < wide) & (patch_row < high)
        hits.append(jnp.where(hit, 1.0, 0.0).astype(BF16))
        bases.append(base)
    return [nn(hit, rows_ref[pl.ds(base, TALL), :]) for hit, base in zip(hits, bases)]


def contract_mask(step, rows):
    first = rows * step
    window = first // CELLS
    shift = first - CELLS * window
    source = iota((rows, SPAN * SLOT), 1)
    hit = (iota((rows, SPAN * SLOT), 0) + shift == WS * (source >> 3) + (source & 7)) & (
        (source & 7) < WS
    )
    return window, jnp.where(hit, 1.0, 0.0).astype(BF16)


def near(ext_ref, place, side, row, col):
    lane_col = iota((1, 8, ext_ref.shape[-1]), 1)
    first = jnp.where(col > 0, 0, 8)
    last = jnp.where(col < side - 1, WS - 1, 8)

    def triple(window, rows):
        own = ext_ref[window, rows]
        left = pltpu.roll(ext_ref[window - 1, rows], 2, 1)
        right = pltpu.roll(ext_ref[window + 1, rows], 6, 1)
        return (
            jnp.where(lane_col == first, left, pltpu.roll(own, 1, 1)),
            own,
            jnp.where(lane_col == last, right, pltpu.roll(own, 7, 1)),
        )

    above_on = jnp.where(row > 0, 1.0, 0.0)
    below_on = jnp.where(row < side - 1, 1.0, 0.0)
    above = triple(place - side, slice(WS - 1, WS))
    middle = triple(place, slice(0, WS))
    below = triple(place + side, slice(0, 1))
    return [
        jnp.concatenate([up * above_on, mid, down * below_on], axis=0)
        for up, mid, down in zip(above, middle, below)
    ]


def edge_of(ext_ref, full, rest, patch_row):
    width = ext_ref.shape[-1]
    tiles = [ext_ref[full].reshape(SLOT, width)] + [ext_ref[window, patch_row] for window in rest]
    rows = SLOT + 8 * len(rest)
    return jnp.concatenate(tiles + [jnp.zeros((EDGE - rows, width), F32)], axis=0).astype(BF16)


def edge_to(ext_ref, full, rest, patch_row, edge):
    edge = edge.astype(F32)
    ext_ref[full] = edge[0:SLOT].reshape(WS, 8, -1)
    for index, window in enumerate(rest):
        ext_ref[window, patch_row] = edge[SLOT + 8 * index : SLOT + 8 * (index + 1)]


def valid_cells(high, wide, width):
    shape = (WS, 8, width)
    return (iota(shape, 0) < high) & (iota(shape, 1) < wide)


def fold(values):
    rows, width = values.shape
    return jnp.sum(values.reshape(rows // 8, 8, width), axis=0)


def normalize(values):
    centre = values - jnp.mean(values, axis=-1, keepdims=True)
    inverse = lax.rsqrt(jnp.mean(centre * centre, axis=-1, keepdims=True) + 1e-06)
    return centre * inverse, inverse


def normalize_back(gradient, scaled, inverse, gain):
    d_scaled = gradient * gain
    mean_one = jnp.mean(d_scaled, axis=-1, keepdims=True)
    mean_two = jnp.mean(d_scaled * scaled, axis=-1, keepdims=True)
    return inverse * (d_scaled - mean_one - scaled * mean_two)


def stack_heads(values):
    head = iota(values.shape, 1) // HDIM
    zero = jnp.zeros_like(values)
    return jnp.concatenate([jnp.where(head == g, values, zero) for g in range(128 // HDIM)], axis=0)


def pick_heads(stacked):
    head = iota((TALL, 128), 1) // HDIM
    taken = stacked[0:TALL]
    for g in range(1, 128 // HDIM):
        taken = jnp.where(head == g, stacked[TALL * g : TALL * (g + 1)], taken)
    return taken


def to_tall(rows):
    return jnp.concatenate([rows, jnp.zeros((TALL - SLOT, rows.shape[1]), F32)], axis=0).astype(
        BF16
    )


def gelu_parts(values):
    cdf = 0.5 + 0.5 * lax.erf(values * (0.5**0.5))
    density = jnp.exp(-0.5 * values * values) * 0.3989422804014327
    return values * cdf, cdf + values * density


def rows_at(index, size):
    return pl.ds(pl.multiple_of(index * size, size), size)


def take_tokens(first, r):
    def source(step, carry):
        windows = [BLOCK * step + i for i in range(BLOCK)]
        limits = [window_of(r.info, first + window)[3:] for window in windows]
        starts = [CELLS * window for window in windows]
        for window, rows in zip(windows, expand(r.tokens, starts, limits)):
            r.ext[MARGIN + window] = rows.reshape(WS, 8, -1)
        return carry

    lax.fori_loop(0, r.windows // BLOCK, source, 0)


def take_margin(first, r, rows_ref, skip, place):
    windows = list(range(MARGIN))
    limits = [window_of(r.info, first + place - MARGIN + window)[3:] for window in windows]
    starts = [skip + CELLS * window for window in windows]
    for window, rows in zip(windows, expand(rows_ref, starts, limits)):
        r.ext[place + window] = rows.reshape(WS, 8, -1)


def take_cotangent(first, r):
    def cotangent(step, carry):
        windows = [BLOCK * step + i for i in range(BLOCK)]
        limits = [window_of(r.info, first + window)[3:] for window in windows]
        starts = [CELLS * window for window in windows]
        total = carry
        for window, rows in zip(windows, expand(r.og, starts, limits)):
            r.dout[rows_at(window, SLOT), :] = rows
            total = total + fold(rows)
        return total

    r.sums[1] = lax.fori_loop(0, r.windows // BLOCK, cotangent, jnp.zeros(r.sums.shape[1:], F32))


def field_pass(first, r, start, stop):
    count = 4

    def body(step, carry):
        totals = []
        for sub in range(count):
            window = count * step + sub
            side, row, col, high, wide = window_of(r.info, first + window)
            bands = near(r.ext, window + MARGIN, side, row, col)
            total = bands[1][1 : 1 + WS] + r.peg_bias[...]
            for a in range(3):
                for b in range(3):
                    tap = 3 * a + b
                    total = total + bands[b][a : a + WS] * r.peg[tap : tap + 1, :]
            total = jnp.where(valid_cells(high, wide, total.shape[-1]), total, 0.0)
            totals.append(total.reshape(SLOT, -1))
        field = jnp.concatenate(totals, axis=0)
        scaled, inverse = normalize(field)
        place = rows_at(step, count * SLOT)
        r.field[place, :] = field
        r.scaled[place, :] = scaled
        r.inverse[place, :] = inverse
        r.normed[place, :] = (scaled * r.gain[0:1, :] + r.shift[0:1, :]).astype(BF16)
        return carry

    lax.fori_loop(start // count, stop // count, body, 0)


def parts_of(qkv, half):
    width = qkv.shape[1] // 3
    return [qkv[:, width * t + 128 * half : width * t + 128 * (half + 1)] for t in range(3)]


def attend(qkvs, limits, probs_ref, windows):
    key = iota((TALL, 256), 0)
    key_row, key_col = key >> 3, key & 7
    usable = [(key_row < high) & (key_col < wide) for high, wide in limits]
    halves = range(qkvs[0].shape[1] // 3 // 128)
    pairs = [(i, half) for i in range(len(windows)) for half in halves]
    parts = [parts_of(qkvs[i], half) for i, half in pairs]
    scores = [nt(keys, stack_heads(query)) for query, keys, _ in parts]
    scores = [jnp.where(usable[i], score, -1e30) for (i, _), score in zip(pairs, scores)]
    tops = [jnp.max(score, axis=0, keepdims=True) for score in scores]
    exponents = [jnp.exp((score - top) * HDIM**-0.5) for score, top in zip(scores, tops)]
    shares = [1.0 / jnp.sum(exponent, axis=0, keepdims=True) for exponent in exponents]
    probs = [exponent * share for exponent, share in zip(exponents, shares)]
    for (i, half), prob in zip(pairs, probs):
        probs_ref[windows[i], :, 256 * half : 256 * (half + 1)] = prob
    context = [tn(prob.astype(BF16), value) for prob, (_, _, value) in zip(probs, parts)]
    context = [pick_heads(one) for one in context]
    return [
        jnp.concatenate([one for (j, _), one in zip(pairs, context) if j == i], axis=1)
        for i in range(len(windows))
    ]


def attend_back(qkvs, d_contexts, probs_ref, windows):
    halves = range(qkvs[0].shape[1] // 3 // 128)
    pairs = [(i, half) for i in range(len(windows)) for half in halves]
    parts = [parts_of(qkvs[i], half) for i, half in pairs]
    stacks = [stack_heads(d_contexts[i][:, 128 * half : 128 * (half + 1)]) for i, half in pairs]
    probs = [probs_ref[windows[i], :, 256 * half : 256 * (half + 1)] for i, half in pairs]
    d_probs = [nt(value, stack) for (_, _, value), stack in zip(parts, stacks)]
    d_value = [nn(prob.astype(BF16), stack) for prob, stack in zip(probs, stacks)]
    inner = [jnp.sum(d * prob, axis=0, keepdims=True) for d, prob in zip(d_probs, probs)]
    d_score = [(prob * (d - one)).astype(BF16) for prob, d, one in zip(probs, d_probs, inner)]
    d_key = [nn(d, stack_heads(query)) * HDIM**-0.5 for d, (query, _, _) in zip(d_score, parts)]
    d_query = [tn(d, keys) for d, (_, keys, _) in zip(d_score, parts)]
    d_query = [pick_heads(one) * HDIM**-0.5 for one in d_query]
    return [
        jnp.concatenate(
            [one for kind in (d_query, d_key, d_value) for (j, _), one in zip(pairs, kind) if j == i],
            axis=1,
        )
        for i in range(len(windows))
    ]


def qkv_weights(r):
    halves, heads = r.at_w.shape[:2]
    return jnp.concatenate(
        [r.at_w[half, z, kind] for kind in range(3) for z in range(heads) for half in range(halves)], axis=0
    )


def proj_weights(r):
    halves, heads = r.at_w.shape[:2]
    return jnp.concatenate([r.at_w[half, z, 3] for z in range(heads) for half in range(halves)], axis=0)


def feed_weights(r, slot, kind):
    cores, _, heads = r.fc_w.shape[:3]
    return jnp.concatenate(
        [r.fc_w[core, slot, z, kind] for core in range(cores) for z in range(heads)], axis=0
    )


def attention_block(first, r, step):
    rows = ATTEND * SLOT
    place = rows_at(step, rows)
    windows = [ATTEND * step + sub for sub in range(ATTEND)]
    limits = [window_of(r.info, first + window)[3:] for window in windows]
    projected = nt(r.normed[place, :], qkv_weights(r))
    qkvs = [to_tall(projected[SLOT * sub : SLOT * (sub + 1)]) for sub in range(ATTEND)]
    for window, qkv in zip(windows, qkvs):
        r.qkv[window] = qkv
    context = attend(qkvs, limits, r.probs, windows)
    context = jnp.concatenate([one[0:SLOT] for one in context], axis=0).astype(BF16)
    r.context[place, :] = context
    hidden = r.field[place, :] + nn(context, proj_weights(r)) + r.proj_bias[...]
    scaled, inverse = normalize(hidden)
    r.scaled_two[place, :] = scaled
    r.inverse_two[place, :] = inverse
    r.normed_two[place, :] = (scaled * r.gain[1:2, :] + r.shift[1:2, :]).astype(BF16)
    r.result[place, :] = hidden + r.fc_out_bias[...]


def feed_chunk(r, slot, chunk, keep):
    rows = FEED * SLOT
    blocks = r.windows // FEED
    w_in, w_out = feed_weights(r, slot, 0), feed_weights(r, slot, 1)
    bias = r.fc_in_bias[chunk]
    places = [slice(rows * block, rows * (block + 1)) for block in range(blocks)]

    def ahead(block):
        place = places[block]
        return nt(r.normed_two[place, :], w_in), nt(r.dout[place, :].astype(BF16), w_out)

    waiting = ahead(0)
    d_bias = jnp.zeros((8, w_in.shape[0]), F32)
    for block in range(blocks):
        pre, d_active = waiting
        place = places[block]
        if block + 1 < blocks:
            waiting = ahead(block + 1)
        active, slope = gelu_parts(pre + bias)
        active = active.astype(BF16)
        d_pre = d_active * slope
        d_bias = d_bias + fold(d_pre)
        d_pre = d_pre.astype(BF16)
        r.active[slot, place, :] = active
        r.d_pre[keep, place, :] = d_pre
        d_normed = nn(d_pre, w_in)
        r.d_two[place, :] = d_normed if slot == 0 else r.d_two[place, :] + d_normed
    r.bias[chunk] = d_bias


def feed_gradients(r, slot, keep):
    cores, _, heads, _, own, _ = r.g_fc.shape
    d_in = tn(r.d_pre[keep], r.normed_two[...]).astype(BF16)
    d_out = tn(r.active[slot], r.dout[...].astype(BF16)).astype(BF16)
    for core in range(cores):
        for z in range(heads):
            place = own * (heads * core + z)
            r.g_fc[core, slot, z, 0] = d_in[place : place + own]
            r.g_fc[core, slot, z, 1] = d_out[place : place + own]


def attention_back(first, r, step):
    rows = ATTEND * SLOT
    place = rows_at(step, rows)
    windows = [ATTEND * step + sub for sub in range(ATTEND)]
    d_output = r.dout[place, :]
    scaled = r.scaled_two[place, :]
    d_normed = r.d_two[place, :]
    d_hidden = d_output + normalize_back(d_normed, scaled, r.inverse_two[place, :], r.gain[1:2, :])
    r.hidden[place, :] = d_hidden
    d_branch = d_hidden.astype(BF16)
    d_context = nt(d_branch, proj_weights(r))
    d_context = [to_tall(d_context[SLOT * sub : SLOT * (sub + 1)]) for sub in range(ATTEND)]
    r.g_proj[...] += tn(r.context[place, :], d_branch)
    r.sums[0] += fold(d_branch.astype(F32))
    r.sums[3] += fold(d_normed * scaled)
    r.sums[5] += fold(d_normed)
    d_qkv = attend_back([r.qkv[window] for window in windows], d_context, r.probs, windows)
    d_qkv = jnp.concatenate([one[0:SLOT] for one in d_qkv], axis=0).astype(BF16)
    r.d_parts[place, :] = d_qkv
    r.g_qkv[...] += tn(d_qkv, r.normed[place, :])


def field_back(first, r, step):
    rows = BLOCK * SLOT
    place = rows_at(step, rows)
    width = r.field.shape[1]
    d_normed = nn(r.d_parts[place, :], qkv_weights(r))
    scaled = r.scaled[place, :]
    r.sums[2] += fold(d_normed * scaled)
    r.sums[4] += fold(d_normed)
    d_norm = normalize_back(d_normed, scaled, r.inverse[place, :], r.gain[0:1, :])
    d_field = r.hidden[place, :] + d_norm
    taps = [jnp.zeros((8, width), F32) for _ in range(10)]
    for sub in range(BLOCK):
        window = BLOCK * step + sub
        side, row, col, high, wide = window_of(r.info, first + window)
        own = d_field[SLOT * sub : SLOT * (sub + 1)].reshape(WS, 8, -1)
        own = jnp.where(valid_cells(high, wide, width), own, 0.0)
        r.mixed[window + MARGIN] = own
        bands = near(r.ext, window + MARGIN, side, row, col)
        for a in range(3):
            for b in range(3):
                taps[3 * a + b] = taps[3 * a + b] + jnp.sum(own * bands[b][a : a + WS], axis=0)
        taps[9] = taps[9] + jnp.sum(own, axis=0)
    for tap in range(10):
        r.sums[6 + tap] += taps[tap]


def token_pass(first, r, start, stop):
    count = 4

    def body(step, carry):
        for sub in range(count):
            window = start + count * step + sub
            side, row, col, high, wide = window_of(r.info, first + window)
            grads = near(r.mixed, window + MARGIN, side, row, col)
            total = grads[1][1 : 1 + WS]
            for a in range(3):
                for b in range(3):
                    tap = 3 * a + b
                    total = total + grads[2 - b][2 - a : 2 - a + WS] * r.peg[tap : tap + 1, :]
            total = jnp.where(valid_cells(high, wide, total.shape[-1]), total, 0.0)
            r.source[rows_at(window, SLOT), :] = total.reshape(SLOT, -1)
        return carry

    lax.fori_loop(0, (stop - start) // count, body, 0)


def shrink(padded_ref, dense_ref, exact):
    rows, count = 112, 7

    def body(step, carry):
        steps = [count * step + i for i in range(count)]
        masks = [contract_mask(one, rows) for one in steps]
        values = [
            padded_ref[pl.ds(pl.multiple_of(SLOT * window, 8), SPAN * SLOT), :] for window, _ in masks
        ]
        highs = [value.astype(BF16) for value in values]
        dense = [nn(hit, high) for (_, hit), high in zip(masks, highs)]
        if exact:
            lows = [(value - high.astype(F32)).astype(BF16) for value, high in zip(values, highs)]
            dense = [one + nn(hit, low) for one, (_, hit), low in zip(dense, masks, lows)]
        for one, result in zip(steps, dense):
            dense_ref[rows_at(one, rows), :] = result.astype(dense_ref.dtype)
        return carry

    lax.fori_loop(0, dense_ref.shape[0] // rows // count, body, 0)


def share_buffers(r):
    r.d_two = r.field
    r.hidden = r.field
    r.source = r.result


def clear(r):
    for ref in (r.g_proj, r.g_qkv, r.sums):
        ref[...] = jnp.zeros_like(ref)
    tail = r.windows * SLOT
    r.result[tail:, :] = jnp.zeros((r.result.shape[0] - tail, r.result.shape[1]), F32)


def finish_result(first, r):
    weights = [feed_weights(r, slot, 1) for slot in range(r.fc_w.shape[1])]

    def body(step, carry):
        place = rows_at(step, BLOCK * SLOT)
        total = r.result[place, :]
        for slot, w_out in enumerate(weights):
            total = total + nn(r.active[slot, place, :], w_out)
        for sub in range(BLOCK):
            window = BLOCK * step + sub
            _, _, _, high, wide = window_of(r.info, first + window)
            cells = total[SLOT * sub : SLOT * (sub + 1)].reshape(WS, 8, -1)
            cells = jnp.where(valid_cells(high, wide, cells.shape[-1]), cells, 0.0)
            r.result[rows_at(window, SLOT), :] = cells.reshape(SLOT, -1)
        return carry

    lax.fori_loop(0, r.windows // BLOCK, body, 0)


def turn_attention_gradients(r):
    halves, _, heads, piece, width = r.g_at.shape
    for kind in range(4):
        rows = r.g_qkv[width * kind : width * (kind + 1), :] if kind < 3 else r.g_proj[...]
        rows = rows.astype(BF16)
        for half in range(halves):
            for z in range(heads):
                place = piece * (halves * z + half)
                r.g_at[half, kind, z] = rows[place : place + piece]


def collect_small(r):
    total = jnp.sum(r.sums[...], axis=1)
    r.small[...] = jnp.zeros_like(r.small)
    r.small[0:1, :] = total[0:1]
    r.small[1:5, :] = jnp.sum(r.bias[...], axis=1)
    r.small[5:6, :] = total[1:2]
    r.small[6:10, :] = total[2:6]
    r.small[10:20, :] = total[6:16]


def loop(start, stop, body):
    def step(index, carry):
        body(index)
        return carry

    lax.fori_loop(start, stop, step, 0)


COPIES = 65
FEED_ORDER = (0, 3, 1, 2)
FETCHED = ("sides", "qkv_w", "proj_w", "og", "tokens", "fc_in", "fc_out", "proj_bias", "fc_in_bias", "fc_out_bias", "gain", "shift",
           "peg", "peg_bias")


def fused_kernel(names, *refs):
    r = SimpleNamespace(**dict(zip(names, refs)))
    r.windows = r.mixed.shape[0] - 2 * MARGIN
    share_buffers(r)
    blocks = r.windows // BLOCK
    own_rows = r.tokens.shape[0]
    heads = r.at_w.shape[1]
    quads = r.fc_w.shape[1]
    piece = r.at_w.shape[3]
    z, img = lax.axis_index("head"), lax.axis_index("img")
    yx, core = img // 2, img % 2
    other = 1 - core
    first = z * r.windows

    def flip(value, mask):
        low, high = value % 2, value // 2
        low = 1 - low if mask & 1 else low
        high = 1 - high if mask & 2 else high
        return 2 * high + low

    z_peer = {m: (img, flip(z, m)) for m in range(1, heads)}
    yx_peer = {m: (2 * flip(yx, m) + core, z) for m in range(1, quads)}
    sibling = (2 * yx + other, z)
    cross = {m: (2 * flip(yx, m) + other, z) for m in range(1, quads)}
    plane = [yx_peer[m] for m in yx_peer] + [sibling] + [cross[m] for m in cross]
    numbers = iter(range(COPIES))

    def copy(source, target, device):
        index = next(numbers)
        return pltpu.make_async_remote_copy(
            src_ref=source,
            dst_ref=target,
            send_sem=r.send.at[index],
            recv_sem=r.recv.at[index],
            device_id=device,
            device_id_type=MESH,
        )

    forth = copy(r.tok_last, r.tok_above, (img, z + 1))
    back = copy(r.tok_first, r.tok_below, (img, z - 1))
    at_z = [copy(r.at_w.at[core, z, yx], r.at_w.at[core, z, yx], z_peer[m]) for m in z_peer]
    at_yx = [
        [copy(r.at_w.at[core, flip(z, m), yx], r.at_w.at[core, flip(z, m), yx], yx_peer[n]) for n in yx_peer]
        for m in z_peer
    ]
    at_core = [copy(r.at_w.at[core, flip(z, m)], r.at_w.at[core, flip(z, m)], sibling) for m in z_peer]
    fc_own = r.fc_w.at[core, 0]
    fc_z = [copy(fc_own.at[z], fc_own.at[z], z_peer[m]) for m in z_peer]
    fc_yx = [copy(fc_own, r.fc_w.at[core, m], yx_peer[m]) for m in yx_peer]
    fc_core = [copy(r.fc_w.at[core, m], r.fc_w.at[core, m], sibling) for m in range(quads)]
    gf_core = [copy(r.g_fc.at[other, m], r.gf_one.at[m], sibling) for m in range(quads)]
    gf_yx = [copy(r.gf_two.at[m], r.gf_three.at[m - 1], yx_peer[m]) for m in yx_peer]
    gf_z = [copy(r.gf_four.at[flip(z, m)], r.gf_five.at[m - 1], z_peer[m]) for m in z_peer]
    ga_core = copy(r.g_at.at[other], r.ga_one, sibling)
    ga_yx = [copy(r.ga_two.at[flip(yx, m)], r.ga_three.at[m - 1], yx_peer[m]) for m in yx_peer]
    ga_z = [copy(r.ga_four.at[flip(z, m)], r.ga_five.at[m - 1], z_peer[m]) for m in z_peer]
    ga_plane = [copy(r.ga_all.at[yx, core], r.ga_all.at[yx, core], peer) for peer in plane]
    sm_plane = [copy(r.small, r.small_plane.at[yx, core], peer) for peer in plane]
    sm_z = [copy(r.small_sum, r.small_z.at[z], z_peer[m]) for m in z_peer]
    mix_forth = copy(r.mix_last, r.mix_above, (img, z + 1))
    mix_back = copy(r.mix_first, r.mix_below, (img, z - 1))
    has_next, has_last = z < heads - 1, z > 0

    def start(copies):
        for one in copies:
            one.start()

    def arrive(copies):
        for one in copies:
            one.wait_recv()

    def total_of(own, others):
        total = own.astype(F32)
        for index in range(others.shape[0]):
            total = total + others[index].astype(F32)
        return total

    barrier = pltpu.get_barrier_semaphore()
    greeted = [z_peer[m] for m in z_peer] + plane
    for peer in greeted:
        pl.semaphore_signal(barrier, inc=1, device_id=peer, device_id_type=MESH)
    fetched = {}
    targets = {"qkv_w": r.at_own.at[0:3], "proj_w": r.at_own.at[3], "fc_in": r.fc_w.at[core, 0, z, 0], "fc_out": r.fc_w.at[core, 0, z, 1]}
    for index, name in enumerate(FETCHED):
        source = getattr(r, "far_" + name)
        target = targets[name] if name in targets else getattr(r, name)
        fetched[name] = pltpu.make_async_copy(source, target, r.local.at[index])
        fetched[name].start()
    fetched["sides"].wait()
    scan_windows(r.sides, r.info, heads * r.windows)
    fetched["qkv_w"].wait()
    fetched["proj_w"].wait()
    for kind in range(4):
        for half in range(2):
            r.at_w[half, z, kind] = r.at_own[kind, half]
    pl.semaphore_wait(barrier, len(greeted))
    start(at_z)
    fetched["fc_in"].wait()
    fetched["fc_out"].wait()
    fetched["tokens"].wait()
    take_tokens(first, r)
    start(fc_z)
    margin = (MARGIN,) + r.ext.shape[1:]
    end = MARGIN + r.windows
    above, below = (MARGIN - 1, range(MARGIN - 1), WS - 1), (end, range(end + 1, end + MARGIN), 0)
    last, foremost = (end - 1, range(end - MARGIN, end - 1), WS - 1), (MARGIN, range(MARGIN + 1, 2 * MARGIN), 0)
    r.tok_last[...] = edge_of(r.ext, *last)
    r.tok_first[...] = edge_of(r.ext, *foremost)

    @pl.when(has_next)
    def _():
        forth.start()

    @pl.when(has_last)
    def _():
        back.start()

    fetched["og"].wait()
    clear(r)
    take_cotangent(first, r)
    for one, many in zip(at_z, at_yx):
        one.wait_recv()
        start(many)
    for name in FETCHED[7:]:
        fetched[name].wait()
    field_pass(first, r, BLOCK, r.windows - BLOCK)
    arrive(fc_z)
    start([fc_yx[m - 1] for m in FEED_ORDER[1:]])
    fc_core[0].start()

    def margins(ext_ref, forth, back, from_above, from_below):
        @pl.when(has_last)
        def _():
            forth.wait_recv()
            edge_to(ext_ref, *above, from_above[...])

        @pl.when(z == 0)
        def _():
            ext_ref[0:MARGIN] = jnp.zeros(margin, F32)

        @pl.when(has_next)
        def _():
            back.wait_recv()
            edge_to(ext_ref, *below, from_below[...])

        @pl.when(z == heads - 1)
        def _():
            ext_ref[end:] = jnp.zeros(margin, F32)

    margins(r.ext, forth, back, r.tok_above, r.tok_below)
    field_pass(first, r, 0, BLOCK)
    field_pass(first, r, r.windows - BLOCK, r.windows)
    for many, one in zip(at_yx, at_core):
        arrive(many)
        one.start()
    arrive(at_core)
    steps = r.windows // ATTEND
    loop(0, steps, lambda step: attention_block(first, r, step))
    for m in FEED_ORDER[1:]:
        fc_yx[m - 1].wait_recv()
        fc_core[m].start()

    def add_cores(m):
        gf_core[m].wait_recv()
        r.gf_two[m] = (r.g_fc[core, m].astype(F32) + r.gf_one[m].astype(F32)).astype(BF16)
        if m > 0:
            gf_yx[m - 1].start()

    sent_slot = None
    for m in FEED_ORDER:
        fc_core[m].wait_recv()
        feed_chunk(r, m, flip(yx, m), min(m, 1))
        if m > 0:
            feed_gradients(r, m, 1)
            gf_core[m].start()
            if sent_slot is not None:
                add_cores(sent_slot)
            sent_slot = m

    def attention(start, stop):
        loop(start, stop, lambda step: attention_back(first, r, step))

    attention(0, 1)
    add_cores(sent_slot)
    attention(1, steps)
    turn_attention_gradients(r)
    ga_core.start()

    def field(start, stop):
        loop(start, stop, lambda step: field_back(first, r, (step + blocks - 1) % blocks))

    feed_gradients(r, 0, 0)
    gf_core[0].start()
    ga_core.wait_recv()
    r.ga_two[...] = (r.g_at[core].astype(F32) + r.ga_one[...].astype(F32)).astype(BF16)
    start(ga_yx)
    field(0, 2)
    r.mix_last[...] = edge_of(r.mixed, *last)
    r.mix_first[...] = edge_of(r.mixed, *foremost)

    @pl.when(has_next)
    def _():
        mix_forth.start()

    @pl.when(has_last)
    def _():
        mix_back.start()

    add_cores(0)
    arrive(gf_yx)
    r.gf_four[...] = total_of(r.gf_two[0], r.gf_three).astype(BF16)
    start(gf_z)
    field(2, blocks)
    collect_small(r)
    arrive(ga_yx)
    r.ga_four[...] = total_of(r.ga_two[yx], r.ga_three).astype(BF16)
    start(ga_z)
    start(sm_plane)
    finish_result(first, r)
    shrink(r.result, r.output, False)
    written = [
        pltpu.make_async_copy(r.output, r.far_output, r.written.at[0]),
        pltpu.make_async_copy(r.d_tokens, r.far_d_tokens, r.written.at[1]),
    ]
    written[0].start()
    token_pass(first, r, BLOCK, r.windows - BLOCK)
    arrive(ga_z)
    r.ga_all[yx, core] = total_of(r.ga_four[z], r.ga_five).astype(BF16)
    start(ga_plane)
    arrive(sm_plane)
    r.small_plane[yx, core] = r.small[...]
    total = jnp.zeros(r.small.shape, F32)
    for a in range(quads):
        for b in range(2):
            total = total + r.small_plane[a, b]
    r.small_sum[...] = total
    start(sm_z)
    margins(r.mixed, mix_forth, mix_back, r.mix_above, r.mix_below)
    token_pass(first, r, 0, BLOCK)
    token_pass(first, r, r.windows - BLOCK, r.windows)
    shrink(r.source, r.d_tokens, True)
    written[1].start()
    arrive(gf_z)
    total = total_of(r.gf_four[z], r.gf_five)
    r.d_fc_in[...] = total[0]
    r.d_fc_out[...] = total[1]
    arrive(sm_z)
    r.small_z[z] = r.small_sum[...]
    total = jnp.zeros(r.small.shape, F32)
    for a in range(heads):
        total = total + r.small_z[a]
    r.small_out[...] = total
    arrive(ga_plane)
    for kind in range(4):
        for half in range(2):
            rows = r.ga_all[kind, half].astype(F32)
            place = slice(piece * half, piece * (half + 1))
            if kind < 3:
                r.d_qkv[kind, place, :] = rows
            else:
                r.d_proj[place, :] = rows

    for one in written:
        one.wait()
    sent = at_z + sum(at_yx, []) + at_core + fc_z + fc_yx + fc_core + gf_core + gf_yx + gf_z + [ga_core] + ga_yx + ga_z
    for one in sent + ga_plane + sm_plane + sm_z:
        one.wait_send()

    @pl.when(has_next)
    def _():
        forth.wait_send()
        mix_forth.wait_send()

    @pl.when(has_last)
    def _():
        back.wait_send()
        mix_back.wait_send()


def local_kernel(names, *refs):
    r = SimpleNamespace(**dict(zip(names, refs)))
    r.windows = r.mixed.shape[0] - 2 * MARGIN
    share_buffers(r)
    blocks = r.windows // BLOCK
    first = lax.axis_index("head") * r.windows
    scan_windows(r.sides, r.info, r.at_w.shape[1] * r.windows)
    clear(r)
    take_cotangent(first, r)
    take_tokens(first, r)
    take_margin(first, r, r.halo_low, HALO - MARGIN * CELLS, 0)
    take_margin(first, r, r.halo_high, 0, MARGIN + r.windows)
    field_pass(first, r, 0, r.windows)
    loop(0, r.windows // ATTEND, lambda step: attention_block(first, r, step))
    for chunk in range(r.fc_w.shape[1]):
        feed_chunk(r, chunk, chunk, 0)
        feed_gradients(r, chunk, 0)
    loop(0, r.windows // ATTEND, lambda step: attention_back(first, r, step))
    loop(0, blocks, lambda step: field_back(first, r, step))
    turn_attention_gradients(r)
    collect_small(r)
    finish_result(first, r)
    shrink(r.result, r.output, False)
    for edge in (slice(0, MARGIN), slice(MARGIN + r.windows, 2 * MARGIN + r.windows)):
        r.mixed[edge] = jnp.zeros((MARGIN,) + r.mixed.shape[1:], F32)


def token_kernel(names, *refs):
    r = SimpleNamespace(**dict(zip(names, refs)))
    r.windows = r.mixed.shape[0] - 2 * MARGIN
    heads = (r.info.shape[1] - 2 * OFFSET) // r.windows
    first = lax.axis_index("head") * r.windows
    scan_windows(r.sides, r.info, heads * r.windows)
    tail = r.windows * SLOT
    r.source[tail:, :] = jnp.zeros((r.source.shape[0] - tail, r.source.shape[1]), F32)
    token_pass(first, r, 0, r.windows)
    shrink(r.source, r.d_tokens, True)


def vmem():
    return pl.BlockSpec(memory_space=pltpu.VMEM)


def smem():
    return pl.BlockSpec(memory_space=pltpu.SMEM)


def work_buffers(windows, heads, width, hidden):
    padded = windows * SLOT
    extra = (windows + SPAN) * SLOT
    return {
        "info": pltpu.SMEM((3, heads * windows + 2 * OFFSET), jnp.int32),
        "dout": pltpu.VMEM((padded, width), F32),
        "field": pltpu.VMEM((padded, width), F32),
        "scaled": pltpu.VMEM((padded, width), F32),
        "inverse": pltpu.VMEM((padded, 1), F32),
        "normed": pltpu.VMEM((padded, width), BF16),
        "qkv": pltpu.VMEM((windows, TALL, 3 * width), BF16),
        "probs": pltpu.VMEM((windows, TALL, 2 * width), F32),
        "context": pltpu.VMEM((padded, width), BF16),
        "result": pltpu.VMEM((extra, width), F32),
        "scaled_two": pltpu.VMEM((padded, width), F32),
        "inverse_two": pltpu.VMEM((padded, 1), F32),
        "normed_two": pltpu.VMEM((padded, width), BF16),
        "active": pltpu.VMEM((hidden // 256, padded, 256), BF16),
        "d_pre": pltpu.VMEM((2, padded, 256), BF16),
        "d_parts": pltpu.VMEM((padded, 3 * width), BF16),
        "g_proj": pltpu.VMEM((width, width), F32),
        "g_qkv": pltpu.VMEM((3 * width, width), F32),
        "sums": pltpu.VMEM((16, 8, width), F32),
        "bias": pltpu.VMEM((hidden // 256, 8, 256), F32),
    }


def call(kernel, name, inputs, outputs, scratch, specs=None, out_specs=None, **params):
    names = list(inputs) + list(outputs) + list(scratch)
    results = pl.pallas_call(
        functools.partial(kernel, names),
        out_shape=tuple(outputs.values()),
        in_specs=specs or [smem()] + [vmem()] * (len(inputs) - 1),
        out_specs=out_specs or (vmem(),) * len(outputs),
        scratch_shapes=list(scratch.values()),
        compiler_params=pltpu.CompilerParams(vmem_limit_bytes=VMEM_LIMIT, **params),
        name=name,
    )(*inputs.values())
    return dict(zip(outputs, results))


def on_any_device(tokens, image_sides, qkv_weight, proj_weight, proj_bias, fc_in, fc_in_bias, fc_out, fc_out_bias,
                  norm_gains, norm_shifts, peg_weight, peg_bias, out_grad):
    own_rows, width = tokens.shape
    windows = own_rows // CELLS
    heads = lax.axis_size("head")
    hidden = fc_in_bias.shape[0]
    piece = width // heads // 2
    own = 256 // heads // 2
    shape = jax.ShapeDtypeStruct
    place = lax.axis_index("head") * own_rows
    around = jnp.pad(lax.all_gather(tokens, "head", axis=0, tiled=True), ((HALO, HALO), (0, 0)))
    halo = jnp.stack(
        [lax.dynamic_slice_in_dim(around, place + shift, HALO, 0) for shift in (0, own_rows + HALO)]
    )
    turned = jnp.concatenate([jnp.swapaxes(qkv_weight, 1, 2), proj_weight[None]], axis=0)
    at_w = lax.all_gather(turned, "head", axis=1, tiled=True)
    fc_w = jnp.stack(
        [lax.all_gather(fc, ("img", "head"), axis=0, tiled=True) for fc in (fc_in, fc_out)]
    )
    edges = (windows + 2 * MARGIN, WS, 8, width)
    out = call(
        local_kernel,
        "block",
        {
            "sides": image_sides,
            "tokens": tokens,
            "halo_low": halo[0],
            "halo_high": halo[1],
            "og": out_grad,
            "at_w": at_w.reshape(4, heads, 2, piece, width).transpose(2, 1, 0, 3, 4),
            "fc_w": fc_w.reshape(2, hidden // 256, 2, heads, own, width).transpose(2, 1, 3, 0, 4, 5),
            "proj_bias": proj_bias[None],
            "fc_in_bias": fc_in_bias.reshape(-1, 1, 256),
            "fc_out_bias": fc_out_bias[None],
            "gain": norm_gains,
            "shift": norm_shifts,
            "peg": peg_weight,
            "peg_bias": peg_bias[None],
        },
        {
            "output": shape((own_rows, width), BF16),
            "mixed": shape(edges, F32),
            "g_fc": shape((2, hidden // 256, heads, 2, own, width), BF16),
            "g_at": shape((2, 4, heads, piece, width), BF16),
            "small": shape((SMALL, width), F32),
        },
        dict(work_buffers(windows, heads, width, hidden), ext=pltpu.VMEM(edges, F32)),
    )
    mixed = out["mixed"]
    last, start = windows, MARGIN
    forth = lax.ppermute(mixed[last : last + MARGIN].astype(BF16), "head", [(i, i + 1) for i in range(heads - 1)])
    back = lax.ppermute(mixed[start : start + MARGIN].astype(BF16), "head", [(i + 1, i) for i in range(heads - 1)])
    own = mixed[MARGIN : MARGIN + windows]
    mixed = jnp.concatenate([forth.astype(F32), own, back.astype(F32)], axis=0)
    buffers = work_buffers(windows, heads, width, hidden)
    d_tokens = call(
        token_kernel,
        "tokens",
        {"sides": image_sides, "mixed": mixed, "peg": peg_weight},
        {"d_tokens": shape((own_rows, width), F32)},
        {"info": buffers["info"], "source": buffers["result"]},
    )["d_tokens"]
    everywhere = ("img", "head")
    d_fc_in, d_fc_out = (
        lax.psum_scatter(g.reshape(hidden, width).astype(F32), everywhere, scatter_dimension=0, tiled=True)
        for g in out["g_fc"].transpose(3, 1, 0, 2, 4, 5)
    )
    g_at = out["g_at"].transpose(1, 2, 0, 3, 4).reshape(4, width, width).astype(F32)
    g_at = lax.psum(lax.psum_scatter(g_at, "head", scatter_dimension=1, tiled=True), "img")
    small = lax.psum(out["small"], everywhere)
    return (out["output"], d_tokens, jnp.swapaxes(g_at[:3], 1, 2), g_at[3], small[0], d_fc_in, small[1:5].reshape(-1),
            d_fc_out, small[5], small[6:8], small[8:10], small[10:19], small[19])


def on_device(tokens, image_sides, qkv_weight, proj_weight, proj_bias, fc_in, fc_in_bias, fc_out, fc_out_bias,
              norm_gains, norm_shifts, peg_weight, peg_bias, out_grad):
    own_rows, width = tokens.shape
    windows = own_rows // CELLS
    heads = lax.axis_size("head")
    hidden = fc_in_bias.shape[0]
    quads = lax.axis_size("img") // 2
    own = fc_in.shape[0]
    if quads != 4 or heads != 4 or own % 16 != 0:
        return on_any_device(tokens, image_sides, qkv_weight, proj_weight, proj_bias, fc_in, fc_in_bias, fc_out,
                             fc_out_bias, norm_gains, norm_shifts, peg_weight, peg_bias, out_grad)
    piece = width // heads // 2
    shape = jax.ShapeDtypeStruct
    inputs = {
        "sides": image_sides,
        "tokens": tokens,
        "og": out_grad,
        "qkv_w": jnp.swapaxes(qkv_weight, 1, 2).reshape(3, 2, piece, width),
        "proj_w": proj_weight.reshape(2, piece, width),
        "fc_in": fc_in,
        "fc_out": fc_out,
        "proj_bias": proj_bias[None],
        "fc_in_bias": fc_in_bias.reshape(-1, 1, 256),
        "fc_out_bias": fc_out_bias[None],
        "gain": norm_gains,
        "shift": norm_shifts,
        "peg": peg_weight,
        "peg_bias": peg_bias[None],
    }
    large = {
        "output": shape((own_rows, width), BF16),
        "d_tokens": shape((own_rows, width), F32),
        "d_qkv": shape((3, width // heads, width), F32),
        "d_proj": shape(proj_weight.shape, F32),
        "d_fc_in": shape(fc_in.shape, F32),
        "d_fc_out": shape(fc_out.shape, F32),
    }
    scratch = work_buffers(windows, heads, width, hidden)
    scratch["sides"] = pltpu.SMEM(image_sides.shape, jnp.int32)
    for kind in ("tok", "mix"):
        for place in ("last", "first", "above", "below"):
            scratch[kind + "_" + place] = pltpu.VMEM((EDGE, width), BF16)
    for name in FETCHED:
        if name not in ("sides", "qkv_w", "proj_w", "fc_in", "fc_out"):
            scratch[name] = pltpu.VMEM(inputs[name].shape, inputs[name].dtype)
    scratch.update({
        "ext": pltpu.VMEM((windows + 2 * MARGIN, WS, 8, width), F32),
        "mixed": pltpu.VMEM((windows + 2 * MARGIN, WS, 8, width), F32),
        "at_w": pltpu.VMEM((2, heads, 4, piece, width), BF16),
        "at_own": pltpu.VMEM((4, 2, piece, width), BF16),
        "fc_w": pltpu.VMEM((2, quads, heads, 2, own, width), BF16),
        "g_fc": pltpu.VMEM((2, quads, heads, 2, own, width), BF16),
        "gf_one": pltpu.VMEM((quads, heads, 2, own, width), BF16),
        "gf_two": pltpu.VMEM((quads, heads, 2, own, width), BF16),
        "gf_three": pltpu.VMEM((quads - 1, heads, 2, own, width), BF16),
        "gf_four": pltpu.VMEM((heads, 2, own, width), BF16),
        "gf_five": pltpu.VMEM((heads - 1, 2, own, width), BF16),
        "g_at": pltpu.VMEM((2, 4, heads, piece, width), BF16),
        "ga_one": pltpu.VMEM((4, heads, piece, width), BF16),
        "ga_two": pltpu.VMEM((4, heads, piece, width), BF16),
        "ga_three": pltpu.VMEM((quads - 1, heads, piece, width), BF16),
        "ga_four": pltpu.VMEM((heads, piece, width), BF16),
        "ga_five": pltpu.VMEM((heads - 1, piece, width), BF16),
        "ga_all": pltpu.VMEM((4, 2, piece, width), BF16),
        "small_plane": pltpu.VMEM((quads, 2, SMALL, width), F32),
        "small_sum": pltpu.VMEM((SMALL, width), F32),
        "small_z": pltpu.VMEM((heads, SMALL, width), F32),
        "small": pltpu.VMEM((SMALL, width), F32),
        "output": pltpu.VMEM((own_rows, width), BF16),
        "d_tokens": pltpu.VMEM((own_rows, width), F32),
        "written": pltpu.SemaphoreType.DMA((2,)),
        "local": pltpu.SemaphoreType.DMA((len(FETCHED),)),
        "send": pltpu.SemaphoreType.DMA((COPIES,)),
        "recv": pltpu.SemaphoreType.DMA((COPIES,)),
    })
    far = pl.BlockSpec(memory_space=pltpu.HBM)
    made = {"far_" + name if name in ("output", "d_tokens") else name: array for name, array in large.items()}
    made["small_out"] = shape((SMALL, width), F32)
    made = call(
        fused_kernel,
        "block",
        {"far_" + name: inputs[name] for name in FETCHED},
        made,
        scratch,
        [far] * len(FETCHED),
        tuple(far if name.startswith("far_") else vmem() for name in made),
        collective_id=0,
        has_side_effects=True,
    )
    small = {
        "d_proj_bias": shape((1, width), F32),
        "d_fc_in_bias": shape((1, hidden), F32),
        "d_fc_out_bias": shape((1, width), F32),
        "d_gains": shape(norm_gains.shape, F32),
        "d_shifts": shape(norm_shifts.shape, F32),
        "d_peg": shape(peg_weight.shape, F32),
        "d_peg_bias": shape((1, width), F32),
    }
    count = len(large)

    def hand_out(*refs):
        sources, targets = refs[: count + 1], refs[count + 1 :]
        for source, target in zip(sources[:count], targets[:count]):
            target[...] = source[...]
        row = 0
        for target in targets[count:]:
            for part in range(target.shape[1] // width):
                rows = target.shape[0]
                target[:, width * part : width * (part + 1)] = sources[count][row : row + rows, :]
                row += rows

    parts = 2

    def spec(array, cut):
        shape = array.shape
        block = (shape[0] // parts,) + tuple(shape[1:]) if cut else shape
        return pl.BlockSpec(block, lambda i: (i if cut else 0,) + (0,) * (len(shape) - 1))

    cuts = {"output", "d_tokens"}
    results = pl.pallas_call(
        hand_out,
        grid=(parts,),
        out_shape=tuple(large.values()) + tuple(small.values()),
        in_specs=[spec(array, name.startswith("far_")) for name, array in made.items()],
        out_specs=tuple(spec(array, name in cuts) for name, array in {**large, **small}.items()),
        compiler_params=pltpu.CompilerParams(vmem_limit_bytes=VMEM_LIMIT),
        name="hand_out",
    )(*made.values())
    out = dict(zip(list(large) + list(small), results))
    out["d_qkv"] = jnp.swapaxes(out["d_qkv"], 1, 2)
    for name in ("d_proj_bias", "d_fc_in_bias", "d_fc_out_bias", "d_peg_bias"):
        out[name] = out[name].reshape(-1)
    order = ("output", "d_tokens", "d_qkv", "d_proj", "d_proj_bias", "d_fc_in", "d_fc_in_bias", "d_fc_out", "d_fc_out_bias",
             "d_gains", "d_shifts", "d_peg", "d_peg_bias")
    return tuple(out[name] for name in order)


def solution(mesh):
    rows = P(("img", "head"), None)
    placed = (rows, P("img", None), P(None, None, "head"), P("head", None), P(), rows, P(), rows, P(), P(), P(), P(), P(), rows)
    return jax.shard_map(
        on_device,
        mesh=mesh,
        in_specs=placed,
        out_specs=(rows, rows, P(None, None, "head"), P("head", None), P(), rows, P(), rows, P(), P(), P(), P(), P()),
        check_vma=False,
    )
```

```python
import functools
from types import SimpleNamespace

import jax
import jax.numpy as jnp
from jax import lax
from jax.experimental import pallas as pl
from jax.experimental.pallas import tpu as pltpu
from jax.sharding import PartitionSpec as P

F32 = jnp.float32
BF16 = jnp.bfloat16
MESH = pl.DeviceIdType.MESH

HDIM = 32
WS = 7
CELLS = WS * WS
SLOT = WS * 8
TALL = 64
MARGIN = 5
HALO = 256
EDGE = 96
OFFSET = 8
BLOCK = 8
FEED = 32
ATTEND = 32
SPAN = 4
SMALL = 24
VMEM_LIMIT = 56 * 1024 * 1024


def nn(left, right):
    return lax.dot_general(left, right, (((1,), (0,)), ((), ())), preferred_element_type=F32)


def nt(left, right):
    return lax.dot_general(left, right, (((1,), (1,)), ((), ())), preferred_element_type=F32)


def tn(left, right):
    return lax.dot_general(left, right, (((0,), (0,)), ((), ())), preferred_element_type=F32)


def iota(shape, axis):
    return lax.broadcasted_iota(jnp.int32, shape, axis)


def identity(size):
    return jnp.where(iota((size, size), 0) == iota((size, size), 1), 1.0, 0.0).astype(BF16)


def scan_windows(sides_ref, info_ref, windows):
    slots = sides_ref.shape[-1]

    def clear(index, carry):
        for kind in range(3):
            info_ref[kind, index] = 0
            info_ref[kind, OFFSET + windows + index] = 0
        return carry

    lax.fori_loop(0, OFFSET, clear, 0)

    def body(window, carry):
        slot, row, col = carry
        side = jnp.where(slot < slots, sides_ref[0, jnp.minimum(slot, slots - 1)], 0)
        info_ref[0, OFFSET + window] = side
        info_ref[1, OFFSET + window] = row
        info_ref[2, OFFSET + window] = col
        end_col = col + 1 >= side
        end_row = row + 1 >= side
        next_slot = jnp.where(end_col & end_row, slot + 1, slot)
        next_row = jnp.where(end_col, jnp.where(end_row, 0, row + 1), row)
        next_col = jnp.where(end_col, 0, col + 1)
        return (next_slot, next_row, next_col)

    zero = jnp.int32(0)
    lax.fori_loop(0, windows, body, (zero, zero, zero))


def window_of(info_ref, window):
    side = info_ref[0, OFFSET + window]
    row = info_ref[1, OFFSET + window]
    col = info_ref[2, OFFSET + window]
    limit = jnp.where(side == 2, 14, jnp.where(side == 3, 18, jnp.where(side == 4, 24, 0)))
    high = jnp.minimum(limit - WS * row, WS)
    wide = jnp.minimum(limit - WS * col, WS)
    return side, row, col, high, wide


def expand(rows_ref, starts, limits):
    place = iota((SLOT, TALL), 0)
    patch_row, patch_col = place >> 3, place & 7
    wanted = WS * patch_row + patch_col - iota((SLOT, TALL), 1)
    hits, bases = [], []
    for start, (high, wide) in zip(starts, limits):
        base = (start // 16) * 16
        base = base if isinstance(base, int) else pl.multiple_of(base, 16)
        hit = (wanted == base - start) & (patch_col < wide) & (patch_row < high)
        hits.append(jnp.where(hit, 1.0, 0.0).astype(BF16))
        bases.append(base)
    return [nn(hit, rows_ref[pl.ds(base, TALL), :]) for hit, base in zip(hits, bases)]


def contract_mask(step, rows):
    first = rows * step
    window = first // CELLS
    shift = first - CELLS * window
    source = iota((rows, SPAN * SLOT), 1)
    hit = (iota((rows, SPAN * SLOT), 0) + shift == WS * (source >> 3) + (source & 7)) & (
        (source & 7) < WS
    )
    return window, jnp.where(hit, 1.0, 0.0).astype(BF16)


def near(ext_ref, place, side, row, col):
    lane_col = iota((1, 8, ext_ref.shape[-1]), 1)
    first = jnp.where(col > 0, 0, 8)
    last = jnp.where(col < side - 1, WS - 1, 8)

    def triple(window, rows):
        own = ext_ref[window, rows]
        left = pltpu.roll(ext_ref[window - 1, rows], 2, 1)
        right = pltpu.roll(ext_ref[window + 1, rows], 6, 1)
        return (
            jnp.where(lane_col == first, left, pltpu.roll(own, 1, 1)),
            own,
            jnp.where(lane_col == last, right, pltpu.roll(own, 7, 1)),
        )

    above_on = jnp.where(row > 0, 1.0, 0.0)
    below_on = jnp.where(row < side - 1, 1.0, 0.0)
    above = triple(place - side, slice(WS - 1, WS))
    middle = triple(place, slice(0, WS))
    below = triple(place + side, slice(0, 1))
    return [
        jnp.concatenate([up * above_on, mid, down * below_on], axis=0)
        for up, mid, down in zip(above, middle, below)
    ]


def edge_of(ext_ref, full, rest, patch_row):
    width = ext_ref.shape[-1]
    tiles = [ext_ref[full].reshape(SLOT, width)] + [ext_ref[window, patch_row] for window in rest]
    rows = SLOT + 8 * len(rest)
    return jnp.concatenate(tiles + [jnp.zeros((EDGE - rows, width), F32)], axis=0).astype(BF16)


def edge_to(ext_ref, full, rest, patch_row, edge):
    edge = edge.astype(F32)
    ext_ref[full] = edge[0:SLOT].reshape(WS, 8, -1)
    for index, window in enumerate(rest):
        ext_ref[window, patch_row] = edge[SLOT + 8 * index : SLOT + 8 * (index + 1)]


def valid_cells(high, wide, width):
    shape = (WS, 8, width)
    return (iota(shape, 0) < high) & (iota(shape, 1) < wide)


def fold(values):
    rows, width = values.shape
    return jnp.sum(values.reshape(rows // 8, 8, width), axis=0)


def normalize(values):
    centre = values - jnp.mean(values, axis=-1, keepdims=True)
    inverse = lax.rsqrt(jnp.mean(centre * centre, axis=-1, keepdims=True) + 1e-06)
    return centre * inverse, inverse


def normalize_back(gradient, scaled, inverse, gain):
    d_scaled = gradient * gain
    mean_one = jnp.mean(d_scaled, axis=-1, keepdims=True)
    mean_two = jnp.mean(d_scaled * scaled, axis=-1, keepdims=True)
    return inverse * (d_scaled - mean_one - scaled * mean_two)


def stack_heads(values):
    head = iota(values.shape, 1) // HDIM
    zero = jnp.zeros_like(values)
    return jnp.concatenate([jnp.where(head == g, values, zero) for g in range(128 // HDIM)], axis=0)


def pick_heads(stacked):
    head = iota((TALL, 128), 1) // HDIM
    taken = stacked[0:TALL]
    for g in range(1, 128 // HDIM):
        taken = jnp.where(head == g, stacked[TALL * g : TALL * (g + 1)], taken)
    return taken


def to_tall(rows):
    return jnp.concatenate([rows, jnp.zeros((TALL - SLOT, rows.shape[1]), F32)], axis=0).astype(
        BF16
    )


def gelu_parts(values):
    cdf = 0.5 + 0.5 * lax.erf(values * (0.5**0.5))
    density = jnp.exp(-0.5 * values * values) * 0.3989422804014327
    return values * cdf, cdf + values * density


def rows_at(index, size):
    return pl.ds(pl.multiple_of(index * size, size), size)


def take_tokens(first, r):
    def source(step, carry):
        windows = [BLOCK * step + i for i in range(BLOCK)]
        limits = [window_of(r.info, first + window)[3:] for window in windows]
        starts = [CELLS * window for window in windows]
        for window, rows in zip(windows, expand(r.tokens, starts, limits)):
            r.ext[MARGIN + window] = rows.reshape(WS, 8, -1)
        return carry

    lax.fori_loop(0, r.windows // BLOCK, source, 0)


def take_margin(first, r, rows_ref, skip, place):
    windows = list(range(MARGIN))
    limits = [window_of(r.info, first + place - MARGIN + window)[3:] for window in windows]
    starts = [skip + CELLS * window for window in windows]
    for window, rows in zip(windows, expand(rows_ref, starts, limits)):
        r.ext[place + window] = rows.reshape(WS, 8, -1)


def take_cotangent(first, r):
    def cotangent(step, carry):
        windows = [BLOCK * step + i for i in range(BLOCK)]
        limits = [window_of(r.info, first + window)[3:] for window in windows]
        starts = [CELLS * window for window in windows]
        total = carry
        for window, rows in zip(windows, expand(r.og, starts, limits)):
            r.dout[rows_at(window, SLOT), :] = rows
            total = total + fold(rows)
        return total

    r.sums[1] = lax.fori_loop(0, r.windows // BLOCK, cotangent, jnp.zeros(r.sums.shape[1:], F32))


def field_pass(first, r, start, stop):
    count = 4

    def body(step, carry):
        totals = []
        for sub in range(count):
            window = count * step + sub
            side, row, col, high, wide = window_of(r.info, first + window)
            bands = near(r.ext, window + MARGIN, side, row, col)
            total = bands[1][1 : 1 + WS] + r.peg_bias[...]
            for a in range(3):
                for b in range(3):
                    tap = 3 * a + b
                    total = total + bands[b][a : a + WS] * r.peg[tap : tap + 1, :]
            total = jnp.where(valid_cells(high, wide, total.shape[-1]), total, 0.0)
            totals.append(total.reshape(SLOT, -1))
        field = jnp.concatenate(totals, axis=0)
        scaled, inverse = normalize(field)
        place = rows_at(step, count * SLOT)
        r.field[place, :] = field
        r.scaled[place, :] = scaled
        r.inverse[place, :] = inverse
        r.normed[place, :] = (scaled * r.gain[0:1, :] + r.shift[0:1, :]).astype(BF16)
        return carry

    lax.fori_loop(start // count, stop // count, body, 0)


def parts_of(qkv, half):
    width = qkv.shape[1] // 3
    return [qkv[:, width * t + 128 * half : width * t + 128 * (half + 1)] for t in range(3)]


def attend(qkvs, limits, probs_ref, windows):
    key = iota((TALL, 256), 0)
    key_row, key_col = key >> 3, key & 7
    usable = [(key_row < high) & (key_col < wide) for high, wide in limits]
    halves = range(qkvs[0].shape[1] // 3 // 128)
    pairs = [(i, half) for i in range(len(windows)) for half in halves]
    parts = [parts_of(qkvs[i], half) for i, half in pairs]
    scores = [nt(keys, stack_heads(query)) for query, keys, _ in parts]
    scores = [jnp.where(usable[i], score, -1e30) for (i, _), score in zip(pairs, scores)]
    tops = [jnp.max(score, axis=0, keepdims=True) for score in scores]
    exponents = [jnp.exp((score - top) * HDIM**-0.5) for score, top in zip(scores, tops)]
    shares = [1.0 / jnp.sum(exponent, axis=0, keepdims=True) for exponent in exponents]
    probs = [exponent * share for exponent, share in zip(exponents, shares)]
    for (i, half), prob in zip(pairs, probs):
        probs_ref[windows[i], :, 256 * half : 256 * (half + 1)] = prob
    context = [tn(prob.astype(BF16), value) for prob, (_, _, value) in zip(probs, parts)]
    context = [pick_heads(one) for one in context]
    return [
        jnp.concatenate([one for (j, _), one in zip(pairs, context) if j == i], axis=1)
        for i in range(len(windows))
    ]


def attend_back(qkvs, d_contexts, probs_ref, windows):
    halves = range(qkvs[0].shape[1] // 3 // 128)
    pairs = [(i, half) for i in range(len(windows)) for half in halves]
    parts = [parts_of(qkvs[i], half) for i, half in pairs]
    stacks = [stack_heads(d_contexts[i][:, 128 * half : 128 * (half + 1)]) for i, half in pairs]
    probs = [probs_ref[windows[i], :, 256 * half : 256 * (half + 1)] for i, half in pairs]
    d_probs = [nt(value, stack) for (_, _, value), stack in zip(parts, stacks)]
    d_value = [nn(prob.astype(BF16), stack) for prob, stack in zip(probs, stacks)]
    inner = [jnp.sum(d * prob, axis=0, keepdims=True) for d, prob in zip(d_probs, probs)]
    d_score = [(prob * (d - one)).astype(BF16) for prob, d, one in zip(probs, d_probs, inner)]
    d_key = [nn(d, stack_heads(query)) * HDIM**-0.5 for d, (query, _, _) in zip(d_score, parts)]
    d_query = [tn(d, keys) for d, (_, keys, _) in zip(d_score, parts)]
    d_query = [pick_heads(one) * HDIM**-0.5 for one in d_query]
    return [
        jnp.concatenate(
            [one for kind in (d_query, d_key, d_value) for (j, _), one in zip(pairs, kind) if j == i],
            axis=1,
        )
        for i in range(len(windows))
    ]


def qkv_weights(r):
    halves, heads = r.at_w.shape[:2]
    return jnp.concatenate(
        [r.at_w[half, z, kind] for kind in range(3) for z in range(heads) for half in range(halves)], axis=0
    )


def proj_weights(r):
    halves, heads = r.at_w.shape[:2]
    return jnp.concatenate([r.at_w[half, z, 3] for z in range(heads) for half in range(halves)], axis=0)


def feed_weights(r, slot, kind):
    cores, _, heads = r.fc_w.shape[:3]
    return jnp.concatenate(
        [r.fc_w[core, slot, z, kind] for core in range(cores) for z in range(heads)], axis=0
    )


def attention_block(first, r, step):
    rows = ATTEND * SLOT
    place = rows_at(step, rows)
    windows = [ATTEND * step + sub for sub in range(ATTEND)]
    limits = [window_of(r.info, first + window)[3:] for window in windows]
    projected = nt(r.normed[place, :], qkv_weights(r))
    qkvs = [to_tall(projected[SLOT * sub : SLOT * (sub + 1)]) for sub in range(ATTEND)]
    for window, qkv in zip(windows, qkvs):
        r.qkv[window] = qkv
    context = attend(qkvs, limits, r.probs, windows)
    context = jnp.concatenate([one[0:SLOT] for one in context], axis=0).astype(BF16)
    r.context[place, :] = context
    hidden = r.field[place, :] + nn(context, proj_weights(r)) + r.proj_bias[...]
    scaled, inverse = normalize(hidden)
    r.scaled_two[place, :] = scaled
    r.inverse_two[place, :] = inverse
    r.normed_two[place, :] = (scaled * r.gain[1:2, :] + r.shift[1:2, :]).astype(BF16)
    r.result[place, :] = hidden + r.fc_out_bias[...]


def feed_chunk(r, slot, chunk, keep):
    rows = FEED * SLOT
    blocks = r.windows // FEED
    w_in, w_out = feed_weights(r, slot, 0), feed_weights(r, slot, 1)
    bias = r.fc_in_bias[chunk]
    places = [slice(rows * block, rows * (block + 1)) for block in range(blocks)]

    def ahead(block):
        place = places[block]
        return nt(r.normed_two[place, :], w_in), nt(r.dout[place, :].astype(BF16), w_out)

    waiting = ahead(0)
    d_bias = jnp.zeros((8, w_in.shape[0]), F32)
    for block in range(blocks):
        pre, d_active = waiting
        place = places[block]
        if block + 1 < blocks:
            waiting = ahead(block + 1)
        active, slope = gelu_parts(pre + bias)
        active = active.astype(BF16)
        d_pre = d_active * slope
        d_bias = d_bias + fold(d_pre)
        d_pre = d_pre.astype(BF16)
        r.active[slot, place, :] = active
        r.d_pre[keep, place, :] = d_pre
        d_normed = nn(d_pre, w_in)
        r.d_two[place, :] = d_normed if slot == 0 else r.d_two[place, :] + d_normed
    r.bias[chunk] = d_bias


def feed_gradients(r, slot, keep):
    cores, _, heads, _, own, _ = r.g_fc.shape
    d_in = tn(r.d_pre[keep], r.normed_two[...]).astype(BF16)
    d_out = tn(r.active[slot], r.dout[...].astype(BF16)).astype(BF16)
    for core in range(cores):
        for z in range(heads):
            place = own * (heads * core + z)
            r.g_fc[core, slot, z, 0] = d_in[place : place + own]
            r.g_fc[core, slot, z, 1] = d_out[place : place + own]


def attention_back(first, r, step, between=None):
    rows = ATTEND * SLOT
    place = rows_at(step, rows)
    windows = [ATTEND * step + sub for sub in range(ATTEND)]
    d_output = r.dout[place, :]
    scaled = r.scaled_two[place, :]
    d_normed = r.d_two[place, :]
    d_hidden = d_output + normalize_back(d_normed, scaled, r.inverse_two[place, :], r.gain[1:2, :])
    r.hidden[place, :] = d_hidden
    d_branch = d_hidden.astype(BF16)
    d_context = nt(d_branch, proj_weights(r))
    if between is not None:
        between()
    d_context = [to_tall(d_context[SLOT * sub : SLOT * (sub + 1)]) for sub in range(ATTEND)]
    r.g_proj[...] += tn(r.context[place, :], d_branch)
    r.sums[0] += fold(d_branch.astype(F32))
    r.sums[3] += fold(d_normed * scaled)
    r.sums[5] += fold(d_normed)
    d_qkv = attend_back([r.qkv[window] for window in windows], d_context, r.probs, windows)
    d_qkv = jnp.concatenate([one[0:SLOT] for one in d_qkv], axis=0).astype(BF16)
    r.d_parts[place, :] = d_qkv
    r.g_qkv[...] += tn(d_qkv, r.normed[place, :])


def field_back(first, r, step):
    rows = BLOCK * SLOT
    place = rows_at(step, rows)
    width = r.field.shape[1]
    d_normed = nn(r.d_parts[place, :], qkv_weights(r))
    scaled = r.scaled[place, :]
    r.sums[2] += fold(d_normed * scaled)
    r.sums[4] += fold(d_normed)
    d_norm = normalize_back(d_normed, scaled, r.inverse[place, :], r.gain[0:1, :])
    d_field = r.hidden[place, :] + d_norm
    taps = [jnp.zeros((8, width), F32) for _ in range(10)]
    for sub in range(BLOCK):
        window = BLOCK * step + sub
        side, row, col, high, wide = window_of(r.info, first + window)
        own = d_field[SLOT * sub : SLOT * (sub + 1)].reshape(WS, 8, -1)
        own = jnp.where(valid_cells(high, wide, width), own, 0.0)
        r.mixed[window + MARGIN] = own
        bands = near(r.ext, window + MARGIN, side, row, col)
        for a in range(3):
            for b in range(3):
                taps[3 * a + b] = taps[3 * a + b] + jnp.sum(own * bands[b][a : a + WS], axis=0)
        taps[9] = taps[9] + jnp.sum(own, axis=0)
    for tap in range(10):
        r.sums[6 + tap] += taps[tap]


def token_pass(first, r, start, stop):
    count = 4

    def body(step, carry):
        for sub in range(count):
            window = start + count * step + sub
            side, row, col, high, wide = window_of(r.info, first + window)
            grads = near(r.mixed, window + MARGIN, side, row, col)
            total = grads[1][1 : 1 + WS]
            for a in range(3):
                for b in range(3):
                    tap = 3 * a + b
                    total = total + grads[2 - b][2 - a : 2 - a + WS] * r.peg[tap : tap + 1, :]
            total = jnp.where(valid_cells(high, wide, total.shape[-1]), total, 0.0)
            r.source[rows_at(window, SLOT), :] = total.reshape(SLOT, -1)
        return carry

    lax.fori_loop(0, (stop - start) // count, body, 0)


def shrink(padded_ref, dense_ref, exact):
    rows, count = 112, 7

    def body(step, carry):
        steps = [count * step + i for i in range(count)]
        masks = [contract_mask(one, rows) for one in steps]
        values = [
            padded_ref[pl.ds(pl.multiple_of(SLOT * window, 8), SPAN * SLOT), :] for window, _ in masks
        ]
        highs = [value.astype(BF16) for value in values]
        dense = [nn(hit, high) for (_, hit), high in zip(masks, highs)]
        if exact:
            lows = [(value - high.astype(F32)).astype(BF16) for value, high in zip(values, highs)]
            dense = [one + nn(hit, low) for one, (_, hit), low in zip(dense, masks, lows)]
        for one, result in zip(steps, dense):
            dense_ref[rows_at(one, rows), :] = result.astype(dense_ref.dtype)
        return carry

    lax.fori_loop(0, dense_ref.shape[0] // rows // count, body, 0)


def share_buffers(r):
    r.d_two = r.field
    r.hidden = r.field
    r.source = r.result


def clear(r):
    for ref in (r.g_proj, r.g_qkv, r.sums):
        ref[...] = jnp.zeros_like(ref)
    tail = r.windows * SLOT
    r.result[tail:, :] = jnp.zeros((r.result.shape[0] - tail, r.result.shape[1]), F32)


def finish_result(first, r):
    weights = [feed_weights(r, slot, 1) for slot in range(r.fc_w.shape[1])]

    def body(step, carry):
        place = rows_at(step, BLOCK * SLOT)
        total = r.result[place, :]
        for slot, w_out in enumerate(weights):
            total = total + nn(r.active[slot, place, :], w_out)
        for sub in range(BLOCK):
            window = BLOCK * step + sub
            _, _, _, high, wide = window_of(r.info, first + window)
            cells = total[SLOT * sub : SLOT * (sub + 1)].reshape(WS, 8, -1)
            cells = jnp.where(valid_cells(high, wide, cells.shape[-1]), cells, 0.0)
            r.result[rows_at(window, SLOT), :] = cells.reshape(SLOT, -1)
        return carry

    lax.fori_loop(0, r.windows // BLOCK, body, 0)


def turn_attention_gradients(r):
    halves, _, heads, piece, width = r.g_at.shape
    for kind in range(4):
        rows = r.g_qkv[width * kind : width * (kind + 1), :] if kind < 3 else r.g_proj[...]
        rows = rows.astype(BF16)
        for half in range(halves):
            for z in range(heads):
                place = piece * (halves * z + half)
                r.g_at[half, kind, z] = rows[place : place + piece]


def collect_small(r):
    total = jnp.sum(r.sums[...], axis=1)
    r.small[...] = jnp.zeros_like(r.small)
    r.small[0:1, :] = total[0:1]
    r.small[1:5, :] = jnp.sum(r.bias[...], axis=1)
    r.small[5:6, :] = total[1:2]
    r.small[6:10, :] = total[2:6]
    r.small[10:20, :] = total[6:16]


def loop(start, stop, body):
    def step(index, carry):
        body(index)
        return carry

    lax.fori_loop(start, stop, step, 0)


COPIES = 65
FEED_ORDER = (0, 1, 2, 3)
FETCHED = ("sides", "qkv_w", "proj_w", "og", "tokens", "fc_in", "fc_out", "proj_bias", "fc_in_bias", "fc_out_bias", "gain", "shift",
           "peg", "peg_bias")


def fused_kernel(names, *refs):
    r = SimpleNamespace(**dict(zip(names, refs)))
    r.windows = r.mixed.shape[0] - 2 * MARGIN
    share_buffers(r)
    blocks = r.windows // BLOCK
    own_rows = r.tokens.shape[0]
    heads = r.at_w.shape[1]
    quads = r.fc_w.shape[1]
    piece = r.at_w.shape[3]
    z, img = lax.axis_index("head"), lax.axis_index("img")
    yx, core = img // 2, img % 2
    other = 1 - core
    first = z * r.windows

    def flip(value, mask):
        low, high = value % 2, value // 2
        low = 1 - low if mask & 1 else low
        high = 1 - high if mask & 2 else high
        return 2 * high + low

    z_peer = {m: (img, flip(z, m)) for m in range(1, heads)}
    yx_peer = {m: (2 * flip(yx, m) + core, z) for m in range(1, quads)}
    sibling = (2 * yx + other, z)
    cross = {m: (2 * flip(yx, m) + other, z) for m in range(1, quads)}
    plane = [yx_peer[m] for m in yx_peer] + [sibling] + [cross[m] for m in cross]
    numbers = iter(range(COPIES))

    def copy(source, target, device):
        index = next(numbers)
        return pltpu.make_async_remote_copy(
            src_ref=source,
            dst_ref=target,
            send_sem=r.send.at[index],
            recv_sem=r.recv.at[index],
            device_id=device,
            device_id_type=MESH,
        )

    forth = copy(r.tok_last, r.tok_above, (img, z + 1))
    back = copy(r.tok_first, r.tok_below, (img, z - 1))
    at_z = [copy(r.at_w.at[core, z, yx], r.at_w.at[core, z, yx], z_peer[m]) for m in z_peer]
    at_yx = [
        [copy(r.at_w.at[core, flip(z, m), yx], r.at_w.at[core, flip(z, m), yx], yx_peer[n]) for n in yx_peer]
        for m in z_peer
    ]
    at_core = [copy(r.at_w.at[core, flip(z, m)], r.at_w.at[core, flip(z, m)], sibling) for m in z_peer]
    fc_own = r.fc_w.at[core, 0]
    fc_z = [copy(fc_own.at[z], fc_own.at[z], z_peer[m]) for m in z_peer]
    fc_yx = [copy(fc_own, r.fc_w.at[core, m], yx_peer[m]) for m in yx_peer]
    fc_core = [copy(r.fc_w.at[core, m], r.fc_w.at[core, m], sibling) for m in range(quads)]
    gf_core = [copy(r.g_fc.at[other, m], r.gf_one.at[m], sibling) for m in range(quads)]
    gf_yx = [copy(r.gf_two.at[m], r.gf_three.at[m - 1], yx_peer[m]) for m in yx_peer]
    gf_z = [copy(r.gf_four.at[flip(z, m)], r.gf_five.at[m - 1], z_peer[m]) for m in z_peer]
    ga_core = copy(r.g_at.at[other], r.ga_one, sibling)
    ga_yx = [copy(r.ga_two.at[flip(yx, m)], r.ga_three.at[m - 1], yx_peer[m]) for m in yx_peer]
    ga_z = [copy(r.ga_four.at[flip(z, m)], r.ga_five.at[m - 1], z_peer[m]) for m in z_peer]
    ga_plane = [copy(r.ga_all.at[yx, core], r.ga_all.at[yx, core], peer) for peer in plane]
    sm_plane = [copy(r.small, r.small_plane.at[yx, core], peer) for peer in plane]
    sm_z = [copy(r.small_sum, r.small_z.at[z], z_peer[m]) for m in z_peer]
    mix_forth = copy(r.mix_last, r.mix_above, (img, z + 1))
    mix_back = copy(r.mix_first, r.mix_below, (img, z - 1))
    has_next, has_last = z < heads - 1, z > 0

    def start(copies):
        for one in copies:
            one.start()

    def arrive(copies):
        for one in copies:
            one.wait_recv()

    def total_of(own, others):
        total = own.astype(F32)
        for index in range(others.shape[0]):
            total = total + others[index].astype(F32)
        return total

    barrier = pltpu.get_barrier_semaphore()
    greeted = [z_peer[m] for m in z_peer] + plane
    for peer in greeted:
        pl.semaphore_signal(barrier, inc=1, device_id=peer, device_id_type=MESH)
    fetched = {}
    targets = {"qkv_w": r.at_own.at[0:3], "proj_w": r.at_own.at[3], "fc_in": r.fc_w.at[core, 0, z, 0], "fc_out": r.fc_w.at[core, 0, z, 1]}
    for index, name in enumerate(FETCHED):
        source = getattr(r, "far_" + name)
        target = targets[name] if name in targets else getattr(r, name)
        fetched[name] = pltpu.make_async_copy(source, target, r.local.at[index])
        fetched[name].start()
    fetched["qkv_w"].wait()
    fetched["proj_w"].wait()
    for kind in range(4):
        for half in range(2):
            r.at_w[half, z, kind] = r.at_own[kind, half]
    pl.semaphore_wait(barrier, len(greeted))
    start(at_z)
    fetched["fc_in"].wait()
    fetched["fc_out"].wait()
    start(fc_z)
    fetched["sides"].wait()
    scan_windows(r.sides, r.info, heads * r.windows)
    fetched["tokens"].wait()
    take_tokens(first, r)
    margin = (MARGIN,) + r.ext.shape[1:]
    end = MARGIN + r.windows
    above, below = (MARGIN - 1, range(MARGIN - 1), WS - 1), (end, range(end + 1, end + MARGIN), 0)
    last, foremost = (end - 1, range(end - MARGIN, end - 1), WS - 1), (MARGIN, range(MARGIN + 1, 2 * MARGIN), 0)
    r.tok_last[...] = edge_of(r.ext, *last)
    r.tok_first[...] = edge_of(r.ext, *foremost)

    @pl.when(has_next)
    def _():
        forth.start()

    @pl.when(has_last)
    def _():
        back.start()

    fetched["og"].wait()
    clear(r)
    take_cotangent(first, r)
    for one, many in zip(at_z, at_yx):
        one.wait_recv()
        start(many)
    for name in FETCHED[7:]:
        fetched[name].wait()
    field_pass(first, r, BLOCK, r.windows - BLOCK)
    arrive(fc_z)
    start([fc_yx[m - 1] for m in FEED_ORDER[1:]])
    fc_core[0].start()

    def margins(ext_ref, forth, back, from_above, from_below):
        @pl.when(has_last)
        def _():
            forth.wait_recv()
            edge_to(ext_ref, *above, from_above[...])

        @pl.when(z == 0)
        def _():
            ext_ref[0:MARGIN] = jnp.zeros(margin, F32)

        @pl.when(has_next)
        def _():
            back.wait_recv()
            edge_to(ext_ref, *below, from_below[...])

        @pl.when(z == heads - 1)
        def _():
            ext_ref[end:] = jnp.zeros(margin, F32)

    margins(r.ext, forth, back, r.tok_above, r.tok_below)
    field_pass(first, r, 0, BLOCK)
    field_pass(first, r, r.windows - BLOCK, r.windows)
    for many, one in zip(at_yx, at_core):
        arrive(many)
        one.start()
    arrive(at_core)
    steps = r.windows // ATTEND
    for step in range(steps):
        attention_block(first, r, step)
    for m in FEED_ORDER[1:]:
        fc_yx[m - 1].wait_recv()
        fc_core[m].start()

    def add_cores(m):
        gf_core[m].wait_recv()
        r.gf_two[m] = (r.g_fc[core, m].astype(F32) + r.gf_one[m].astype(F32)).astype(BF16)
        if m > 0:
            gf_yx[m - 1].start()

    sent_slot = None
    for m in FEED_ORDER:
        fc_core[m].wait_recv()
        feed_chunk(r, m, flip(yx, m), min(m, 1))
        if m > 0:
            feed_gradients(r, m, 1)
            gf_core[m].start()
            if sent_slot is not None:
                add_cores(sent_slot)
            sent_slot = m

    attention_back(first, r, 0, lambda: add_cores(sent_slot))
    for step in range(1, steps):
        attention_back(first, r, step)
    turn_attention_gradients(r)
    ga_core.start()

    def field(start, stop):
        loop(start, stop, lambda step: field_back(first, r, (step + blocks - 1) % blocks))

    feed_gradients(r, 0, 0)
    gf_core[0].start()
    ga_core.wait_recv()
    r.ga_two[...] = (r.g_at[core].astype(F32) + r.ga_one[...].astype(F32)).astype(BF16)
    start(ga_yx)
    field(0, 2)
    r.mix_last[...] = edge_of(r.mixed, *last)
    r.mix_first[...] = edge_of(r.mixed, *foremost)

    @pl.when(has_next)
    def _():
        mix_forth.start()

    @pl.when(has_last)
    def _():
        mix_back.start()

    add_cores(0)
    arrive(gf_yx)
    r.gf_four[...] = total_of(r.gf_two[0], r.gf_three).astype(BF16)
    start(gf_z)
    field(2, blocks)
    collect_small(r)
    start(sm_plane)
    arrive(ga_yx)
    r.ga_four[...] = total_of(r.ga_two[yx], r.ga_three).astype(BF16)
    start(ga_z)
    finish_result(first, r)
    shrink(r.result, r.output, False)
    written = [
        pltpu.make_async_copy(r.output, r.far_output, r.written.at[0]),
        pltpu.make_async_copy(r.d_tokens, r.far_d_tokens, r.written.at[1]),
    ]
    written[0].start()
    token_pass(first, r, BLOCK, r.windows - BLOCK)
    arrive(ga_z)
    r.ga_all[yx, core] = total_of(r.ga_four[z], r.ga_five).astype(BF16)
    start(ga_plane)
    arrive(sm_plane)
    r.small_plane[yx, core] = r.small[...]
    total = jnp.zeros(r.small.shape, F32)
    for a in range(quads):
        for b in range(2):
            total = total + r.small_plane[a, b]
    r.small_sum[...] = total
    start(sm_z)
    margins(r.mixed, mix_forth, mix_back, r.mix_above, r.mix_below)
    token_pass(first, r, 0, BLOCK)
    token_pass(first, r, r.windows - BLOCK, r.windows)
    shrink(r.source, r.d_tokens, True)
    written[1].start()
    arrive(gf_z)
    total = total_of(r.gf_four[z], r.gf_five)
    r.d_fc_in[...] = total[0]
    r.d_fc_out[...] = total[1]
    arrive(sm_z)
    r.small_z[z] = r.small_sum[...]
    total = jnp.zeros(r.small.shape, F32)
    for a in range(heads):
        total = total + r.small_z[a]
    r.small_out[...] = total
    arrive(ga_plane)
    for kind in range(4):
        for half in range(2):
            rows = r.ga_all[kind, half].astype(F32)
            place = slice(piece * half, piece * (half + 1))
            if kind < 3:
                r.d_qkv[kind, place, :] = rows
            else:
                r.d_proj[place, :] = rows

    for one in written:
        one.wait()
    sent = at_z + sum(at_yx, []) + at_core + fc_z + fc_yx + fc_core + gf_core + gf_yx + gf_z + [ga_core] + ga_yx + ga_z
    for one in sent + ga_plane + sm_plane + sm_z:
        one.wait_send()

    @pl.when(has_next)
    def _():
        forth.wait_send()
        mix_forth.wait_send()

    @pl.when(has_last)
    def _():
        back.wait_send()
        mix_back.wait_send()


def local_kernel(names, *refs):
    r = SimpleNamespace(**dict(zip(names, refs)))
    r.windows = r.mixed.shape[0] - 2 * MARGIN
    share_buffers(r)
    blocks = r.windows // BLOCK
    first = lax.axis_index("head") * r.windows
    scan_windows(r.sides, r.info, r.at_w.shape[1] * r.windows)
    clear(r)
    take_cotangent(first, r)
    take_tokens(first, r)
    take_margin(first, r, r.halo_low, HALO - MARGIN * CELLS, 0)
    take_margin(first, r, r.halo_high, 0, MARGIN + r.windows)
    field_pass(first, r, 0, r.windows)
    for step in range(r.windows // ATTEND):
        attention_block(first, r, step)
    for chunk in range(r.fc_w.shape[1]):
        feed_chunk(r, chunk, chunk, 0)
        feed_gradients(r, chunk, 0)
    for step in range(r.windows // ATTEND):
        attention_back(first, r, step)
    loop(0, blocks, lambda step: field_back(first, r, step))
    turn_attention_gradients(r)
    collect_small(r)
    finish_result(first, r)
    shrink(r.result, r.output, False)
    for edge in (slice(0, MARGIN), slice(MARGIN + r.windows, 2 * MARGIN + r.windows)):
        r.mixed[edge] = jnp.zeros((MARGIN,) + r.mixed.shape[1:], F32)


def token_kernel(names, *refs):
    r = SimpleNamespace(**dict(zip(names, refs)))
    r.windows = r.mixed.shape[0] - 2 * MARGIN
    heads = (r.info.shape[1] - 2 * OFFSET) // r.windows
    first = lax.axis_index("head") * r.windows
    scan_windows(r.sides, r.info, heads * r.windows)
    tail = r.windows * SLOT
    r.source[tail:, :] = jnp.zeros((r.source.shape[0] - tail, r.source.shape[1]), F32)
    token_pass(first, r, 0, r.windows)
    shrink(r.source, r.d_tokens, True)


def vmem():
    return pl.BlockSpec(memory_space=pltpu.VMEM)


def smem():
    return pl.BlockSpec(memory_space=pltpu.SMEM)


def work_buffers(windows, heads, width, hidden):
    padded = windows * SLOT
    extra = (windows + SPAN) * SLOT
    return {
        "info": pltpu.SMEM((3, heads * windows + 2 * OFFSET), jnp.int32),
        "dout": pltpu.VMEM((padded, width), F32),
        "field": pltpu.VMEM((padded, width), F32),
        "scaled": pltpu.VMEM((padded, width), F32),
        "inverse": pltpu.VMEM((padded, 1), F32),
        "normed": pltpu.VMEM((padded, width), BF16),
        "qkv": pltpu.VMEM((windows, TALL, 3 * width), BF16),
        "probs": pltpu.VMEM((windows, TALL, 2 * width), F32),
        "context": pltpu.VMEM((padded, width), BF16),
        "result": pltpu.VMEM((extra, width), F32),
        "scaled_two": pltpu.VMEM((padded, width), F32),
        "inverse_two": pltpu.VMEM((padded, 1), F32),
        "normed_two": pltpu.VMEM((padded, width), BF16),
        "active": pltpu.VMEM((hidden // 256, padded, 256), BF16),
        "d_pre": pltpu.VMEM((2, padded, 256), BF16),
        "d_parts": pltpu.VMEM((padded, 3 * width), BF16),
        "g_proj": pltpu.VMEM((width, width), F32),
        "g_qkv": pltpu.VMEM((3 * width, width), F32),
        "sums": pltpu.VMEM((16, 8, width), F32),
        "bias": pltpu.VMEM((hidden // 256, 8, 256), F32),
    }


def call(kernel, name, inputs, outputs, scratch, specs=None, out_specs=None, **params):
    names = list(inputs) + list(outputs) + list(scratch)
    results = pl.pallas_call(
        functools.partial(kernel, names),
        out_shape=tuple(outputs.values()),
        in_specs=specs or [smem()] + [vmem()] * (len(inputs) - 1),
        out_specs=out_specs or (vmem(),) * len(outputs),
        scratch_shapes=list(scratch.values()),
        compiler_params=pltpu.CompilerParams(vmem_limit_bytes=VMEM_LIMIT, **params),
        name=name,
    )(*inputs.values())
    return dict(zip(outputs, results))


def on_any_device(tokens, image_sides, qkv_weight, proj_weight, proj_bias, fc_in, fc_in_bias, fc_out, fc_out_bias,
                  norm_gains, norm_shifts, peg_weight, peg_bias, out_grad):
    own_rows, width = tokens.shape
    windows = own_rows // CELLS
    heads = lax.axis_size("head")
    hidden = fc_in_bias.shape[0]
    piece = width // heads // 2
    own = 256 // heads // 2
    shape = jax.ShapeDtypeStruct
    place = lax.axis_index("head") * own_rows
    around = jnp.pad(lax.all_gather(tokens, "head", axis=0, tiled=True), ((HALO, HALO), (0, 0)))
    halo = jnp.stack(
        [lax.dynamic_slice_in_dim(around, place + shift, HALO, 0) for shift in (0, own_rows + HALO)]
    )
    turned = jnp.concatenate([jnp.swapaxes(qkv_weight, 1, 2), proj_weight[None]], axis=0)
    at_w = lax.all_gather(turned, "head", axis=1, tiled=True)
    fc_w = jnp.stack(
        [lax.all_gather(fc, ("img", "head"), axis=0, tiled=True) for fc in (fc_in, fc_out)]
    )
    edges = (windows + 2 * MARGIN, WS, 8, width)
    out = call(
        local_kernel,
        "block",
        {
            "sides": image_sides,
            "tokens": tokens,
            "halo_low": halo[0],
            "halo_high": halo[1],
            "og": out_grad,
            "at_w": at_w.reshape(4, heads, 2, piece, width).transpose(2, 1, 0, 3, 4),
            "fc_w": fc_w.reshape(2, hidden // 256, 2, heads, own, width).transpose(2, 1, 3, 0, 4, 5),
            "proj_bias": proj_bias[None],
            "fc_in_bias": fc_in_bias.reshape(-1, 1, 256),
            "fc_out_bias": fc_out_bias[None],
            "gain": norm_gains,
            "shift": norm_shifts,
            "peg": peg_weight,
            "peg_bias": peg_bias[None],
        },
        {
            "output": shape((own_rows, width), BF16),
            "mixed": shape(edges, F32),
            "g_fc": shape((2, hidden // 256, heads, 2, own, width), BF16),
            "g_at": shape((2, 4, heads, piece, width), BF16),
            "small": shape((SMALL, width), F32),
        },
        dict(work_buffers(windows, heads, width, hidden), ext=pltpu.VMEM(edges, F32)),
    )
    mixed = out["mixed"]
    last, start = windows, MARGIN
    forth = lax.ppermute(mixed[last : last + MARGIN].astype(BF16), "head", [(i, i + 1) for i in range(heads - 1)])
    back = lax.ppermute(mixed[start : start + MARGIN].astype(BF16), "head", [(i + 1, i) for i in range(heads - 1)])
    own = mixed[MARGIN : MARGIN + windows]
    mixed = jnp.concatenate([forth.astype(F32), own, back.astype(F32)], axis=0)
    buffers = work_buffers(windows, heads, width, hidden)
    d_tokens = call(
        token_kernel,
        "tokens",
        {"sides": image_sides, "mixed": mixed, "peg": peg_weight},
        {"d_tokens": shape((own_rows, width), F32)},
        {"info": buffers["info"], "source": buffers["result"]},
    )["d_tokens"]
    everywhere = ("img", "head")
    d_fc_in, d_fc_out = (
        lax.psum_scatter(g.reshape(hidden, width).astype(F32), everywhere, scatter_dimension=0, tiled=True)
        for g in out["g_fc"].transpose(3, 1, 0, 2, 4, 5)
    )
    g_at = out["g_at"].transpose(1, 2, 0, 3, 4).reshape(4, width, width).astype(F32)
    g_at = lax.psum(lax.psum_scatter(g_at, "head", scatter_dimension=1, tiled=True), "img")
    small = lax.psum(out["small"], everywhere)
    return (out["output"], d_tokens, jnp.swapaxes(g_at[:3], 1, 2), g_at[3], small[0], d_fc_in, small[1:5].reshape(-1),
            d_fc_out, small[5], small[6:8], small[8:10], small[10:19], small[19])


def on_device(tokens, image_sides, qkv_weight, proj_weight, proj_bias, fc_in, fc_in_bias, fc_out, fc_out_bias,
              norm_gains, norm_shifts, peg_weight, peg_bias, out_grad):
    own_rows, width = tokens.shape
    windows = own_rows // CELLS
    heads = lax.axis_size("head")
    hidden = fc_in_bias.shape[0]
    quads = lax.axis_size("img") // 2
    own = fc_in.shape[0]
    if quads != 4 or heads != 4 or own % 16 != 0:
        return on_any_device(tokens, image_sides, qkv_weight, proj_weight, proj_bias, fc_in, fc_in_bias, fc_out,
                             fc_out_bias, norm_gains, norm_shifts, peg_weight, peg_bias, out_grad)
    piece = width // heads // 2
    shape = jax.ShapeDtypeStruct
    inputs = {
        "sides": image_sides,
        "tokens": tokens,
        "og": out_grad,
        "qkv_w": jnp.swapaxes(qkv_weight, 1, 2).reshape(3, 2, piece, width),
        "proj_w": proj_weight.reshape(2, piece, width),
        "fc_in": fc_in,
        "fc_out": fc_out,
        "proj_bias": proj_bias[None],
        "fc_in_bias": fc_in_bias.reshape(-1, 1, 256),
        "fc_out_bias": fc_out_bias[None],
        "gain": norm_gains,
        "shift": norm_shifts,
        "peg": peg_weight,
        "peg_bias": peg_bias[None],
    }
    large = {
        "output": shape((own_rows, width), BF16),
        "d_tokens": shape((own_rows, width), F32),
        "d_qkv": shape((3, width // heads, width), F32),
        "d_proj": shape(proj_weight.shape, F32),
        "d_fc_in": shape(fc_in.shape, F32),
        "d_fc_out": shape(fc_out.shape, F32),
    }
    scratch = work_buffers(windows, heads, width, hidden)
    scratch["sides"] = pltpu.SMEM(image_sides.shape, jnp.int32)
    for kind in ("tok", "mix"):
        for place in ("last", "first", "above", "below"):
            scratch[kind + "_" + place] = pltpu.VMEM((EDGE, width), BF16)
    for name in FETCHED:
        if name not in ("sides", "qkv_w", "proj_w", "fc_in", "fc_out"):
            scratch[name] = pltpu.VMEM(inputs[name].shape, inputs[name].dtype)
    scratch.update({
        "ext": pltpu.VMEM((windows + 2 * MARGIN, WS, 8, width), F32),
        "mixed": pltpu.VMEM((windows + 2 * MARGIN, WS, 8, width), F32),
        "at_w": pltpu.VMEM((2, heads, 4, piece, width), BF16),
        "at_own": pltpu.VMEM((4, 2, piece, width), BF16),
        "fc_w": pltpu.VMEM((2, quads, heads, 2, own, width), BF16),
        "g_fc": pltpu.VMEM((2, quads, heads, 2, own, width), BF16),
        "gf_one": pltpu.VMEM((quads, heads, 2, own, width), BF16),
        "gf_two": pltpu.VMEM((quads, heads, 2, own, width), BF16),
        "gf_three": pltpu.VMEM((quads - 1, heads, 2, own, width), BF16),
        "gf_four": pltpu.VMEM((heads, 2, own, width), BF16),
        "gf_five": pltpu.VMEM((heads - 1, 2, own, width), BF16),
        "g_at": pltpu.VMEM((2, 4, heads, piece, width), BF16),
        "ga_one": pltpu.VMEM((4, heads, piece, width), BF16),
        "ga_two": pltpu.VMEM((4, heads, piece, width), BF16),
        "ga_three": pltpu.VMEM((quads - 1, heads, piece, width), BF16),
        "ga_four": pltpu.VMEM((heads, piece, width), BF16),
        "ga_five": pltpu.VMEM((heads - 1, piece, width), BF16),
        "ga_all": pltpu.VMEM((4, 2, piece, width), BF16),
        "small_plane": pltpu.VMEM((quads, 2, SMALL, width), F32),
        "small_sum": pltpu.VMEM((SMALL, width), F32),
        "small_z": pltpu.VMEM((heads, SMALL, width), F32),
        "small": pltpu.VMEM((SMALL, width), F32),
        "output": pltpu.VMEM((own_rows, width), BF16),
        "d_tokens": pltpu.VMEM((own_rows, width), F32),
        "written": pltpu.SemaphoreType.DMA((2,)),
        "local": pltpu.SemaphoreType.DMA((len(FETCHED),)),
        "send": pltpu.SemaphoreType.DMA((COPIES,)),
        "recv": pltpu.SemaphoreType.DMA((COPIES,)),
    })
    far = pl.BlockSpec(memory_space=pltpu.HBM)
    made = {"far_" + name if name in ("output", "d_tokens") else name: array for name, array in large.items()}
    made["small_out"] = shape((SMALL, width), F32)
    made = call(
        fused_kernel,
        "block",
        {"far_" + name: inputs[name] for name in FETCHED},
        made,
        scratch,
        [far] * len(FETCHED),
        tuple(far if name.startswith("far_") else vmem() for name in made),
        collective_id=0,
        has_side_effects=True,
    )
    small = {
        "d_proj_bias": shape((1, width), F32),
        "d_fc_in_bias": shape((1, hidden), F32),
        "d_fc_out_bias": shape((1, width), F32),
        "d_gains": shape(norm_gains.shape, F32),
        "d_shifts": shape(norm_shifts.shape, F32),
        "d_peg": shape(peg_weight.shape, F32),
        "d_peg_bias": shape((1, width), F32),
    }
    count = len(large)

    def hand_out(*refs):
        sources, targets = refs[: count + 1], refs[count + 1 :]
        for source, target in zip(sources[:count], targets[:count]):
            target[...] = source[...]
        row = 0
        for target in targets[count:]:
            for part in range(target.shape[1] // width):
                rows = target.shape[0]
                target[:, width * part : width * (part + 1)] = sources[count][row : row + rows, :]
                row += rows

    parts = 2

    def spec(array, cut):
        shape = array.shape
        block = (shape[0] // parts,) + tuple(shape[1:]) if cut else shape
        return pl.BlockSpec(block, lambda i: (i if cut else 0,) + (0,) * (len(shape) - 1))

    cuts = {"output", "d_tokens"}
    results = pl.pallas_call(
        hand_out,
        grid=(parts,),
        out_shape=tuple(large.values()) + tuple(small.values()),
        in_specs=[spec(array, name.startswith("far_")) for name, array in made.items()],
        out_specs=tuple(spec(array, name in cuts) for name, array in {**large, **small}.items()),
        compiler_params=pltpu.CompilerParams(vmem_limit_bytes=VMEM_LIMIT),
        name="hand_out",
    )(*made.values())
    out = dict(zip(list(large) + list(small), results))
    out["d_qkv"] = jnp.swapaxes(out["d_qkv"], 1, 2)
    for name in ("d_proj_bias", "d_fc_in_bias", "d_fc_out_bias", "d_peg_bias"):
        out[name] = out[name].reshape(-1)
    order = ("output", "d_tokens", "d_qkv", "d_proj", "d_proj_bias", "d_fc_in", "d_fc_in_bias", "d_fc_out", "d_fc_out_bias",
             "d_gains", "d_shifts", "d_peg", "d_peg_bias")
    return tuple(out[name] for name in order)


def solution(mesh):
    rows = P(("img", "head"), None)
    placed = (rows, P("img", None), P(None, None, "head"), P("head", None), P(), rows, P(), rows, P(), P(), P(), P(), P(), rows)
    return jax.shard_map(
        on_device,
        mesh=mesh,
        in_specs=placed,
        out_specs=(rows, rows, P(None, None, "head"), P("head", None), P(), rows, P(), rows, P(), P(), P(), P(), P()),
        check_vma=False,
    )
```
